32 devices in a mesh: seq: 16 (over z, y, x), chan: 2 (over core).
Axes of the slice: x: 2, y: 2, z: 4, core: 2. Of those that a mesh axis runs over, the one named last changes fastest.
Arguments:
- inputs: bfloat16 [3, 64, 4096], P(None, 'chan', 'seq'), may hold values from -6 to 6
- short_weights: float32 [3, 3, 64], P(None, None, 'chan'), may hold values from -3 to 3
- filters: float32 [32, 4096], P(None, 'seq'), may hold values from -1.2 to 1.2
- skip: float32 [64], P('chan'), may hold values from -4 to 4
- grad_out: bfloat16 [64, 4096], P('chan', 'seq'), may hold values from -7.5 to 7.5
Outputs:
- input_grads: float32 [3, 64, 4096], P(None, 'chan', 'seq')
- filter_grad: float32 [32, 4096], P('chan', 'seq')
- skip_grad: float32 [64], P('chan')
- short_grad: float32 [3, 3, 64], P(None, None, 'chan')
The draws below stay inside these ranges and needn't reach their ends.
All inputs are finite; a program needn't handle non-finite values.
Results may differ from the reference program's by a relative error of at most 0.0003.
Values may be sent and summed in bfloat16 or wider, within the bound.
A program may use at most 64 MiB of HBM per device.

```python
import jax
import jax.numpy as jnp
from jax import lax

KS = 3
SEQ = 4096
CHANNELS = 64
FILTERS = 32


def draw_filters(key, part):
    key = jax.random.fold_in(key, 11)
    first, second = jax.random.split(key)
    position = jnp.arange(SEQ, dtype=jnp.float32)[None, :]
    lowest, highest = (40.0, 4.0 * SEQ)
    spread = jax.random.uniform(first, (FILTERS, 1), jnp.float32)
    reach = jnp.exp(jnp.log(lowest) + spread * (jnp.log(highest) - jnp.log(lowest)))
    envelope = jnp.exp(-position / reach) * jnp.sqrt(2.0 / jnp.minimum(reach, 1.0 * SEQ))
    return envelope * jnp.clip(jax.random.normal(second, (FILTERS, SEQ), jnp.float32), -5.0, 5.0)


def draw_grad_out(key, part):
    key = jax.random.fold_in(key, 23)
    position = jnp.arange(SEQ, dtype=jnp.float32)[None, :] / SEQ
    values = jnp.clip(jax.random.normal(key, (CHANNELS, SEQ), jnp.float32), -5.0, 5.0)
    return (values * (0.5 + position)).astype(jnp.bfloat16)


def steps_of(rng, shape, shards, low, largest):
    def one(dim, shards_of):
        draws = jax.random.uniform(jax.random.fold_in(jax.random.fold_in(rng, 6), dim), (shards_of,), jnp.float32, low / len(shards), largest / len(shards))
        return jnp.repeat(jnp.exp(draws), shape[dim] // shards_of).reshape((-1,) + (1,) * (len(shape) - dim - 1))

    gain = one(*shards[0])
    for cut in shards[1:]:
        gain = gain * one(*cut)
    return gain


def bell_draw(own_key, extent, scale, limit, cuts=(), held_as=jnp.bfloat16):
    gain = steps_of(own_key, extent, cuts, -0.22, 0.18) if cuts else 1.0
    values = jax.random.normal(own_key, extent, jnp.float32) * scale * gain
    return jnp.minimum(jnp.maximum(values, -limit), limit).astype(held_as)


def setup_inputs(seed: int = 0) -> dict:
    seeds = jax.random.split(jax.random.key(seed), 6)
    inputs = bell_draw(seeds[0], (3, CHANNELS, SEQ), 1.0, 6.0, ((1, 2), (2, 16)))
    short_weights = bell_draw(seeds[1], (3, KS, CHANNELS), 0.6, 3.0, ((2, 2),), jnp.float32)
    filters = draw_filters(jax.random.fold_in(seeds[5], 71), 0)
    skip = bell_draw(seeds[3], (CHANNELS,), 0.8, 4.0, ((0, 2),), jnp.float32)
    grad_out = draw_grad_out(jax.random.fold_in(seeds[5], 71), 0)
    return {"inputs": inputs, "short_weights": short_weights, "filters": filters, "skip": skip, "grad_out": grad_out}


def causal_short(signal, taps):
    result = taps[0][:, None] * signal
    for offset in range(1, KS):
        moved = jnp.pad(signal, ((0, 0), (offset, 0)))[:, :-offset]
        result = result + taps[offset][:, None] * moved
    return result


def adjoint_short(gradient, taps):
    result = taps[0][:, None] * gradient
    for offset in range(1, KS):
        moved = jnp.pad(gradient, ((0, 0), (0, offset)))[:, offset:]
        result = result + taps[offset][:, None] * moved
    return result


def short_terms(gradient, signal):
    rows = [jnp.sum(gradient * signal, axis=1)]
    for offset in range(1, KS):
        rows.append(jnp.sum(gradient[:, offset:] * signal[:, :-offset], axis=1))
    return jnp.stack(rows)


def reference(inputs, short_weights, filters, skip, grad_out):
    blocks = CHANNELS // FILTERS
    padded = 2 * SEQ
    spec_filter = jnp.fft.rfft(filters, n=padded, axis=1)
    branch_blocks = jnp.swapaxes(inputs.reshape(3, blocks, FILTERS, SEQ), 0, 1)
    tap_blocks = jnp.transpose(short_weights.reshape(3, KS, blocks, FILTERS), (2, 0, 1, 3))
    skip_blocks = skip.reshape(blocks, FILTERS)
    grad_blocks = grad_out.reshape(blocks, FILTERS, SEQ)

    def one_block(items):
        branches, taps, direct, cotangent = items
        signals = branches.astype(jnp.float32)
        grad = cotangent.astype(jnp.float32)
        query = causal_short(signals[0], taps[0])
        key_part = causal_short(signals[1], taps[1])
        value = causal_short(signals[2], taps[2])
        product = key_part * value
        spec_product = jnp.fft.rfft(product, n=padded, axis=1)
        conv_out = jnp.fft.irfft(spec_filter * spec_product, n=padded, axis=1)[:, :SEQ]
        conv_out = conv_out + direct[:, None] * product
        dw = grad * query
        spec_dw = jnp.fft.rfft(dw, n=padded, axis=1)
        dz = jnp.fft.irfft(spec_dw * jnp.conj(spec_filter), n=padded, axis=1)[:, :SEQ]
        dz = dz + direct[:, None] * dw
        filter_part = jnp.fft.irfft(spec_dw * jnp.conj(spec_product), n=padded, axis=1)[:, :SEQ]
        skip_part = jnp.sum(dw * product, axis=1)
        grads = [grad * conv_out, dz * value, dz * key_part]
        in_grads = jnp.stack([adjoint_short(grads[b], taps[b]) for b in range(3)])
        short_part = jnp.stack([short_terms(grads[b], signals[b]) for b in range(3)])
        return in_grads, filter_part, skip_part, short_part

    in_grads, filter_parts, skip_parts, short_parts = lax.map(one_block, (branch_blocks, tap_blocks, skip_blocks, grad_blocks))
    scale = SEQ ** -0.5
    input_grads = jnp.swapaxes(in_grads, 0, 1).reshape(3, CHANNELS, SEQ)
    filter_grad = jnp.sum(filter_parts, axis=0) * ((SEQ * blocks) ** -0.5)
    skip_grad = skip_parts.reshape(CHANNELS) * scale
    short_grad = jnp.transpose(short_parts, (1, 2, 0, 3)).reshape(3, KS, CHANNELS) * scale
    return input_grads, filter_grad, skip_grad, short_grad
```

```python
import functools
import math

import jax
import jax.numpy as jnp
import numpy as np
from jax import lax
from jax.experimental import pallas as pl
from jax.experimental.pallas import tpu as pltpu
from jax.sharding import PartitionSpec as P

highest = lax.Precision.HIGHEST


def shifted(block, axis, distance):
    devices = range(lax.axis_size(axis))
    route = [(i - distance, i) for i in devices if i - distance in devices]
    return lax.ppermute(block, axis, route)


def angle_table(rows, cols, period, sign):
    grid = (
        jnp.arange(rows, dtype=jnp.int32)[:, None]
        * jnp.arange(cols, dtype=jnp.int32)[None, :]
        % period
    )
    angle = sign * 2.0 * math.pi / period * grid.astype(jnp.float32)
    return (jnp.cos(angle), jnp.sin(angle))


def rotate(real_part, imag_part, cosine, sine):
    return (real_part * cosine - imag_part * sine, real_part * sine + imag_part * cosine)


def transform_last(real_part, imag_part, sign):
    length = real_part.shape[-1]
    if length <= 128 or length % 64 != 0:
        cosine, sine = angle_table(length, length, length, sign)
        new_real = jnp.dot(real_part, cosine, precision=highest) - jnp.dot(
            imag_part, sine, precision=highest
        )
        new_imag = jnp.dot(real_part, sine, precision=highest) + jnp.dot(
            imag_part, cosine, precision=highest
        )
        return (new_real, new_imag)
    outer = 64
    inner = length // outer
    leading = real_part.shape[:-1]
    real_part = jnp.swapaxes(real_part.reshape(leading + (inner, outer)), -1, -2)
    imag_part = jnp.swapaxes(imag_part.reshape(leading + (inner, outer)), -1, -2)
    real_part, imag_part = transform_last(real_part, imag_part, sign)
    cosine, sine = angle_table(outer, inner, length, sign)
    real_part, imag_part = rotate(real_part, imag_part, cosine, sine)
    cosine, sine = angle_table(outer, outer, outer, sign)
    new_real = jnp.einsum("...jk,jl->...lk", real_part, cosine, precision=highest) - jnp.einsum(
        "...jk,jl->...lk", imag_part, sine, precision=highest
    )
    new_imag = jnp.einsum("...jk,jl->...lk", real_part, sine, precision=highest) + jnp.einsum(
        "...jk,jl->...lk", imag_part, cosine, precision=highest
    )
    return (new_real.reshape(leading + (length,)), new_imag.reshape(leading + (length,)))


def forward_spectrum(stacked):
    parts = lax.axis_size("seq")
    rank = lax.axis_index("seq")
    span = stacked.shape[2]
    width = span // parts
    period = 2 * span * parts
    rows = lax.all_to_all(stacked[:, :, None, :], "seq", split_axis=3, concat_axis=2, tiled=True)
    cosine, sine = angle_table(parts, 2 * parts, 2 * parts, -1.0)
    real_part = jnp.einsum("bcpm,pq->bcqm", rows, cosine, precision=highest)
    imag_part = jnp.einsum("bcpm,pq->bcqm", rows, sine, precision=highest)
    column = rank * width + jnp.arange(width, dtype=jnp.int32)
    grid = jnp.arange(2 * parts, dtype=jnp.int32)[:, None] * column[None, :] % period
    angle = -2.0 * math.pi / period * grid.astype(jnp.float32)
    real_part, imag_part = rotate(real_part, imag_part, jnp.cos(angle), jnp.sin(angle))
    real_part, imag_part = (
        lax.all_to_all(real_part, "seq", split_axis=2, concat_axis=3, tiled=True),
        lax.all_to_all(imag_part, "seq", split_axis=2, concat_axis=3, tiled=True),
    )
    return transform_last(real_part, imag_part, -1.0)


def inverse_start(real_part, imag_part):
    parts = lax.axis_size("seq")
    rank = lax.axis_index("seq")
    span = real_part.shape[3]
    period = 2 * span * parts
    real_part, imag_part = transform_last(real_part, imag_part, 1.0)
    residue = 2 * rank + jnp.arange(2, dtype=jnp.int32)
    grid = residue[:, None] * jnp.arange(span, dtype=jnp.int32)[None, :] % period
    angle = 2.0 * math.pi / period * grid.astype(jnp.float32)
    return rotate(real_part, imag_part, jnp.cos(angle), jnp.sin(angle))


def inverse_finish(real_part, imag_part, period):
    parts = lax.axis_size("seq")
    cosine, sine = angle_table(2 * parts, parts, 2 * parts, 1.0)
    new_real = jnp.einsum("bcqm,qp->bcpm", real_part, cosine, precision=highest) - jnp.einsum(
        "bcqm,qp->bcpm", imag_part, sine, precision=highest
    )
    new_imag = jnp.einsum("bcqm,qp->bcpm", real_part, sine, precision=highest) + jnp.einsum(
        "bcqm,qp->bcpm", imag_part, cosine, precision=highest
    )
    return (new_real * (1.0 / period), new_imag * (1.0 / period))


def spectral_body(inputs, short_weights, filters, skip, grad_out):
    taps = short_weights.shape[1]
    parts = lax.axis_size("seq")
    groups = lax.axis_size("chan")
    span = inputs.shape[2]
    channels = inputs.shape[1]
    total = span * parts
    period = 2 * total
    border = shifted(inputs[:, :, span - (taps - 1) :], "seq", 1)
    extended = jnp.concatenate([border, inputs], axis=2).astype(jnp.float32)
    mixed = short_weights[:, 0, :, None] * extended[:, :, taps - 1 : taps - 1 + span]
    for offset in range(1, taps):
        start = taps - 1 - offset
        mixed = mixed + short_weights[:, offset, :, None] * extended[:, :, start : start + span]
    query, key_part, value = (mixed[0], mixed[1], mixed[2])
    grad = grad_out.astype(jnp.float32)
    product = key_part * value
    dw = grad * query
    spec_real, spec_imag = forward_spectrum(jnp.stack([product, dw, filters]))
    prod_real, grad_real, filt_real = (spec_real[0], spec_real[1], spec_real[2])
    prod_imag, grad_imag, filt_imag = (spec_imag[0], spec_imag[1], spec_imag[2])
    conv_real = filt_real * prod_real - filt_imag * prod_imag
    conv_imag = filt_real * prod_imag + filt_imag * prod_real
    back_real = grad_real * filt_real + grad_imag * filt_imag
    back_imag = grad_imag * filt_real - grad_real * filt_imag
    corr_real = grad_real * prod_real + grad_imag * prod_imag
    corr_imag = grad_imag * prod_real - grad_real * prod_imag
    start_real, start_imag = inverse_start(
        jnp.stack([conv_real, back_real, corr_real]), jnp.stack([conv_imag, back_imag, corr_imag])
    )
    start_real, start_imag = (
        lax.all_to_all(start_real, "seq", split_axis=3, concat_axis=2, tiled=True),
        lax.all_to_all(start_imag, "seq", split_axis=3, concat_axis=2, tiled=True),
    )
    result, unused = inverse_finish(start_real, start_imag, period)
    fields = lax.all_to_all(result, "seq", split_axis=2, concat_axis=3, tiled=True).reshape(
        3, channels, span
    )
    conv_out = fields[0] + skip[:, None] * product
    dz = fields[1] + skip[:, None] * dw
    filter_grad = lax.psum_scatter(
        fields[2] * (total * groups) ** (-0.5), "chan", scatter_dimension=0, tiled=True
    )
    grads = jnp.stack([grad * conv_out, dz * value, dz * key_part])
    after = shifted(grads[:, :, : taps - 1], "seq", -1)
    grad_ext = jnp.concatenate([grads, after], axis=2)
    in_grads = short_weights[:, 0, :, None] * grads
    for offset in range(1, taps):
        in_grads = (
            in_grads + short_weights[:, offset, :, None] * grad_ext[:, :, offset : offset + span]
        )
    short_rows = []
    for offset in range(taps):
        start = taps - 1 - offset
        short_rows.append(jnp.sum(grads * extended[:, :, start : start + span], axis=2))
    short_part = jnp.stack(short_rows, axis=1)
    skip_part = jnp.sum(dw * product, axis=1)
    short_sum, skip_sum = lax.psum((short_part, skip_part), "seq")
    scale = total ** (-0.5)
    return (in_grads, filter_grad, skip_sum * scale, short_sum * scale)


MESH = pl.DeviceIdType.MESH


def split(x):
    high = x.astype(jnp.bfloat16)
    return high, (x - high.astype(jnp.float32)).astype(jnp.bfloat16)


def split_table(table):
    table = np.asarray(table, np.float32)
    high = table.astype(jnp.bfloat16)
    return high, (table - high.astype(np.float32)).astype(jnp.bfloat16)


def tables(parts, span):
    period = 2 * parts * span
    u = np.arange(span)
    angle = 2.0 * np.pi / span * (u[:, None] * u[None, :] % span)
    wide = np.concatenate([np.cos(angle), np.sin(angle)], axis=1)
    wide = np.stack(split_table(wide))
    k = np.arange(parts) + 0.5
    angle = 2.0 * np.pi / period * k[:, None] * u[None, :]
    twiddle = np.stack([np.cos(angle), np.sin(angle)]).astype(np.float32)
    angle = np.pi / parts * k[:, None] * np.arange(parts)[None, :]
    high, low = split_table(np.concatenate([np.cos(angle), -np.sin(angle)], axis=0))
    first = np.concatenate([high, high, low], axis=1)
    last = np.concatenate([np.cos(angle).T, -np.sin(angle).T], axis=1) * (2.0 / period)
    high, low = split_table(last)
    last = np.concatenate([high, high, low], axis=1)
    return wide, twiddle, first, last


def dot(a, b):
    return jnp.dot(a, b, preferred_element_type=jnp.float32)


def kernel(
    parts, groups, x_ref, g_ref, f_ref, sw_ref, sk_ref, wide_ref, tw_ref, first_ref, last_ref,
    ig_ref, fg_ref, skg_ref, sg_ref,
    stage, send, recv, wide, gsend, grecv, fsend, frecv, fstage, sems, wide_sem,
):
    taps = sw_ref.shape[1]
    channels, span = f_ref.shape
    half = span // 2
    per = channels // parts
    rows = per * parts
    total = parts * span
    me = lax.axis_index("seq")
    group = lax.axis_index("chan")
    share = parts // groups
    target = me // share

    load_wide = pltpu.make_async_copy(wide_ref, wide, wide_sem)
    load_wide.start()

    barrier = pltpu.get_barrier_semaphore()
    for i in range(parts):
        for j in range(groups):
            if i or j:
                pl.semaphore_signal(
                    barrier,
                    inc=1,
                    device_id={"seq": (me + i) % parts, "chan": (group + j) % groups},
                    device_id_type=MESH,
                )

    fhigh, flow = split(f_ref[...])
    pieces = [x_ref[0], x_ref[1], x_ref[2], g_ref[...], fhigh, flow]
    pieces = [p.astype(jnp.float32) for p in pieces]
    pieces += [jnp.zeros_like(pieces[0])] * 2
    for a, piece in enumerate(pieces):
        stage[pl.ds(2 * a, channels, stride=16), :] = piece[:, :half]
        stage[pl.ds(2 * a + 1, channels, stride=16), :] = piece[:, half:]
    send[...] = stage[...].astype(jnp.bfloat16).reshape(send.shape)
    recv[pl.ds(me, 1)] = send[pl.ds(me, 1)]

    pl.semaphore_wait(barrier, parts * groups - 1)
    for i in range(1, parts):
        peer = (me + i) % parts
        pltpu.make_async_remote_copy(
            src_ref=send.at[peer], dst_ref=recv.at[me], send_sem=sems.at[0], recv_sem=sems.at[1],
            device_id={"seq": peer}, device_id_type=MESH,
        ).start()

    def wait_blocks(ref, count, sem):
        part = ref.at[pl.ds(0, count)]
        pltpu.make_async_copy(part, part, sem).wait()

    wait_blocks(recv, parts - 1, sems.at[1])
    stage[...] = recv[...].astype(jnp.float32).reshape(stage.shape)

    def received(a):
        blocks = []
        for ch in range(per):
            blocks.append(
                jnp.concatenate(
                    [stage[pl.ds(16 * ch + 2 * a + h, parts, stride=16 * per), :] for h in (0, 1)],
                    axis=1,
                )
            )
        return jnp.concatenate(blocks, axis=0)

    row = lax.broadcasted_iota(jnp.int32, (rows, span), 0)
    lane = lax.broadcasted_iota(jnp.int32, (rows, span), 1)

    def delayed(x, j):
        if j == 0:
            return x
        y = pltpu.roll(x, j, 1)
        z = jnp.where(row % parts == 0, 0.0, pltpu.roll(y, 1, 0))
        return jnp.where(lane < j, z, y)

    def advanced(x, j):
        if j == 0:
            return x
        y = pltpu.roll(x, span - j, 1)
        z = jnp.where(row % parts == parts - 1, 0.0, pltpu.roll(y, rows - 1, 0))
        return jnp.where(lane >= span - j, z, y)

    def per_channel(values):
        result = jnp.full((rows, span), values[0], jnp.float32)
        for ch in range(1, per):
            result = jnp.where(row >= ch * parts, values[ch], result)
        return result

    weight = [
        [per_channel([sw_ref[b, j, per * me + ch] for ch in range(per)]) for j in range(taps)]
        for b in range(3)
    ]
    direct = per_channel([sk_ref[per * me + ch] for ch in range(per)])

    signals = [received(a) for a in range(6)]
    grad = signals[3]
    filt = signals[4] + signals[5]
    moved = [[delayed(signals[b], j) for j in range(taps)] for b in range(3)]
    mixed = []
    for b in range(3):
        value = weight[b][0] * moved[b][0]
        for j in range(1, taps):
            value = value + weight[b][j] * moved[b][j]
        mixed.append(value)
    query, key_part, value = mixed
    product = key_part * value
    dw = grad * query

    cosine, sine = tw_ref[0], tw_ref[1]
    reals, imags = [], []
    for signal in (product, dw, filt):
        for ch in range(per):
            high, low = split(signal[ch * parts : (ch + 1) * parts])
            spec = dot(first_ref[...], jnp.concatenate([high, low, high], axis=0))
            re, im = spec[:parts], spec[parts:]
            reals.append(re * cosine + im * sine)
            imags.append(im * cosine - re * sine)
    load_wide.wait()

    def transform(re, im):
        both = jnp.concatenate([re, im], axis=0)
        size = both.shape[0]
        high, low = split(both)
        result = dot(jnp.concatenate([high, low], axis=0), wide[0])
        result = result[:size] + result[size:] + dot(high, wide[1])
        count = size // 2
        return (
            result[:count, :span], result[:count, span:],
            result[count:, :span], result[count:, span:],
        )

    rc, rs, ic, is_ = transform(jnp.concatenate(reals, axis=0), jnp.concatenate(imags, axis=0))
    re, im = rc + is_, ic - rs
    pr, dr, fr = (re[i * rows : (i + 1) * rows] for i in range(3))
    pi, di, fi = (im[i * rows : (i + 1) * rows] for i in range(3))
    out_r = jnp.concatenate([dr * pr + di * pi, fr * pr - fi * pi, dr * fr + di * fi], axis=0)
    out_i = jnp.concatenate([di * pr - dr * pi, fr * pi + fi * pr, di * fr - dr * fi], axis=0)
    rc, rs, ic, is_ = transform(out_r, out_i)
    re, im = rc - is_, ic + rs

    def finish(i):
        blocks = []
        for ch in range(per):
            start = (i * per + ch) * parts
            cr, ci = re[start : start + parts], im[start : start + parts]
            both = jnp.concatenate([cr * cosine - ci * sine, ci * cosine + cr * sine], axis=0)
            high, low = split(both)
            blocks.append(dot(last_ref[...], jnp.concatenate([high, low, high], axis=0)))
        return jnp.concatenate(blocks, axis=0)

    corr = finish(0) * (total * groups) ** (-0.5)
    for ch in range(per):
        block = corr[ch * parts : (ch + 1) * parts]
        fstage[pl.ds(2 * ch, parts, stride=2 * per), :] = block[:, :half]
        fstage[pl.ds(2 * ch + 1, parts, stride=2 * per), :] = block[:, half:]
    for s in range(parts):
        fsend[s] = fstage[2 * per * s : 2 * per * (s + 1), :]
    slot = group * share + me % share
    for i in range(parts):
        peer = (me + i) % parts
        remote = pltpu.make_async_remote_copy(
            src_ref=fsend.at[peer], dst_ref=frecv.at[slot], send_sem=sems.at[2],
            recv_sem=sems.at[3], device_id={"seq": peer, "chan": target}, device_id_type=MESH,
        )
        if i:
            remote.start()
        else:

            @pl.when(target != group)
            def _():
                remote.start()

            @pl.when(target == group)
            def _():
                pltpu.make_async_copy(fsend.at[me], frecv.at[slot], sems.at[3]).start()

    conv_out = finish(1) + direct * product
    dz = finish(2) + direct * dw
    grads = [grad * conv_out, dz * value, dz * key_part]
    for b in range(3):
        result = weight[b][0] * grads[b]
        for j in range(1, taps):
            result = result + weight[b][j] * advanced(grads[b], j)
        for ch in range(per):
            block = result[ch * parts : (ch + 1) * parts]
            stage[pl.ds(8 * ch + 2 * b, parts, stride=8 * per), :] = block[:, :half]
            stage[pl.ds(8 * ch + 2 * b + 1, parts, stride=8 * per), :] = block[:, half:]

    scale = total ** (-0.5)
    sums = [grads[b] * moved[b][j] for b in range(3) for j in range(taps)] + [dw * product]
    pack = half // channels
    spot = lax.broadcasted_iota(jnp.int32, (1, half), 1)
    lines = [jnp.zeros((1, half), jnp.float32) for _ in range(2 * per)]
    for k, array in enumerate(sums):
        folded = array[:, :half] + array[:, half:]
        for ch in range(per):
            block = jnp.sum(folded[ch * parts : (ch + 1) * parts], axis=0, keepdims=True)
            amount = jnp.sum(block, axis=1, keepdims=True) * scale
            at = (k % pack) * channels + per * me + ch
            lines[k // pack] = jnp.where(spot == at, amount, lines[k // pack])
    for n, line in enumerate(lines):
        stage[pl.ds(8 * (n // 2) + 6 + n % 2, parts, stride=8 * per), :] = jnp.broadcast_to(
            line, (parts, half)
        )
    gsend[...] = stage[: 8 * per * parts, :].reshape(gsend.shape)
    grecv[pl.ds(me, 1)] = gsend[pl.ds(me, 1)]
    for i in range(1, parts):
        peer = (me + i) % parts
        pltpu.make_async_remote_copy(
            src_ref=gsend.at[peer], dst_ref=grecv.at[me], send_sem=sems.at[4],
            recv_sem=sems.at[5], device_id={"seq": peer}, device_id_type=MESH,
        ).start()

    wait_blocks(frecv, parts, sems.at[3])
    both = frecv[:share]
    for j in range(1, groups):
        both = both + frecv[j * share : (j + 1) * share]
    for i in range(share):
        fstage[2 * per * i : 2 * per * (i + 1), :] = both[i]
    for h in (0, 1):
        fg_ref[:, h * half : (h + 1) * half] = fstage[pl.ds(h, share * per, stride=2), :]

    wait_blocks(grecv, parts - 1, sems.at[5])
    stage[: 8 * per * parts, :] = grecv[...].reshape(8 * per * parts, half)
    for b in range(3):
        for h in (0, 1):
            ig_ref[b, :, h * half : (h + 1) * half] = stage[
                pl.ds(2 * b + h, channels, stride=8), :
            ]
    lines = []
    for n in range(2 * per):
        line = stage[pl.ds(8 * (n // 2) + 6 + n % 2, parts, stride=8 * per), :]
        lines.append(jnp.sum(line, axis=0, keepdims=True))
    for k in range(3 * taps + 1):
        start = (k % pack) * channels
        piece = lines[k // pack][:, start : start + channels]
        if k < 3 * taps:
            sg_ref[k // taps, pl.ds(k % taps, 1), :] = piece
        else:
            skg_ref[...] = piece

    wait_blocks(send, parts - 1, sems.at[0])
    wait_blocks(gsend, parts - 1, sems.at[4])
    wait_blocks(fsend, parts - 1, sems.at[2])

    @pl.when(target != group)
    def _():
        wait_blocks(fsend, 1, sems.at[2])


def owner_body(inputs, short_weights, filters, skip, grad_out):
    parts = lax.axis_size("seq")
    groups = lax.axis_size("chan")
    taps = short_weights.shape[1]
    channels, span = grad_out.shape
    per = channels // parts
    half = span // 2
    wide, twiddle, first, last = (jnp.asarray(t) for t in tables(parts, span))
    vmem = pl.BlockSpec(memory_space=pltpu.VMEM)
    smem = pl.BlockSpec(memory_space=pltpu.SMEM)
    anywhere = pl.BlockSpec(memory_space=pl.ANY)
    f32 = jnp.float32
    results = pl.pallas_call(
        functools.partial(kernel, parts, groups),
        out_shape=(
            jax.ShapeDtypeStruct((3, channels, span), f32),
            jax.ShapeDtypeStruct((channels // groups, span), f32),
            jax.ShapeDtypeStruct((1, channels), f32),
            jax.ShapeDtypeStruct((3, taps, channels), f32),
        ),
        in_specs=[vmem, vmem, vmem, smem, smem, anywhere, vmem, vmem, vmem],
        out_specs=(vmem, vmem, vmem, vmem),
        scratch_shapes=[
            pltpu.VMEM((16 * channels, half), f32),
            pltpu.VMEM((parts, 16 * per, half), jnp.bfloat16),
            pltpu.VMEM((parts, 16 * per, half), jnp.bfloat16),
            pltpu.VMEM(wide.shape, jnp.bfloat16),
            pltpu.VMEM((parts, 8 * per, half), f32),
            pltpu.VMEM((parts, 8 * per, half), f32),
            pltpu.VMEM((parts, 2 * per, half), f32),
            pltpu.VMEM((parts, 2 * per, half), f32),
            pltpu.VMEM((2 * channels, half), f32),
            pltpu.SemaphoreType.DMA((6,)),
            pltpu.SemaphoreType.DMA,
        ],
        compiler_params=pltpu.CompilerParams(
            collective_id=0, has_side_effects=True, vmem_limit_bytes=32 * 1024 * 1024
        ),
        name="owner_convolutions",
    )(inputs, grad_out, filters, short_weights, skip, wide, twiddle, first, last)
    in_grads, filter_grad, skip_grad, short_grad = results
    return in_grads, filter_grad, skip_grad.reshape(channels), short_grad


def body(inputs, short_weights, filters, skip, grad_out):
    parts = lax.axis_size("seq")
    groups = lax.axis_size("chan")
    channels, span = grad_out.shape
    fits = (
        channels == 2 * parts
        and filters.shape[0] == channels
        and span == 256
        and parts == 16
        and parts % groups == 0
        and short_weights.shape[1] <= 4
    )
    chosen = owner_body if fits else spectral_body
    return chosen(inputs, short_weights, filters, skip, grad_out)


def solution(mesh):
    placed = (
        P(None, "chan", "seq"),
        P(None, None, "chan"),
        P(None, "seq"),
        P("chan"),
        P("chan", "seq"),
    )
    return jax.shard_map(
        body,
        mesh=mesh,
        in_specs=placed,
        out_specs=(P(None, "chan", "seq"), P("chan", "seq"), P("chan"), P(None, None, "chan")),
        check_vma=False,
    )
```

```python
import functools
import math

import jax
import jax.numpy as jnp
import numpy as np
from jax import lax
from jax.experimental import pallas as pl
from jax.experimental.pallas import tpu as pltpu
from jax.sharding import PartitionSpec as P

highest = lax.Precision.HIGHEST


def shifted(block, axis, distance):
    devices = range(lax.axis_size(axis))
    route = [(i - distance, i) for i in devices if i - distance in devices]
    return lax.ppermute(block, axis, route)


def angle_table(rows, cols, period, sign):
    grid = (
        jnp.arange(rows, dtype=jnp.int32)[:, None]
        * jnp.arange(cols, dtype=jnp.int32)[None, :]
        % period
    )
    angle = sign * 2.0 * math.pi / period * grid.astype(jnp.float32)
    return (jnp.cos(angle), jnp.sin(angle))


def rotate(real_part, imag_part, cosine, sine):
    return (real_part * cosine - imag_part * sine, real_part * sine + imag_part * cosine)


def transform_last(real_part, imag_part, sign):
    length = real_part.shape[-1]
    if length <= 128 or length % 64 != 0:
        cosine, sine = angle_table(length, length, length, sign)
        new_real = jnp.dot(real_part, cosine, precision=highest) - jnp.dot(
            imag_part, sine, precision=highest
        )
        new_imag = jnp.dot(real_part, sine, precision=highest) + jnp.dot(
            imag_part, cosine, precision=highest
        )
        return (new_real, new_imag)
    outer = 64
    inner = length // outer
    leading = real_part.shape[:-1]
    real_part = jnp.swapaxes(real_part.reshape(leading + (inner, outer)), -1, -2)
    imag_part = jnp.swapaxes(imag_part.reshape(leading + (inner, outer)), -1, -2)
    real_part, imag_part = transform_last(real_part, imag_part, sign)
    cosine, sine = angle_table(outer, inner, length, sign)
    real_part, imag_part = rotate(real_part, imag_part, cosine, sine)
    cosine, sine = angle_table(outer, outer, outer, sign)
    new_real = jnp.einsum("...jk,jl->...lk", real_part, cosine, precision=highest) - jnp.einsum(
        "...jk,jl->...lk", imag_part, sine, precision=highest
    )
    new_imag = jnp.einsum("...jk,jl->...lk", real_part, sine, precision=highest) + jnp.einsum(
        "...jk,jl->...lk", imag_part, cosine, precision=highest
    )
    return (new_real.reshape(leading + (length,)), new_imag.reshape(leading + (length,)))


def forward_spectrum(stacked):
    parts = lax.axis_size("seq")
    rank = lax.axis_index("seq")
    span = stacked.shape[2]
    width = span // parts
    period = 2 * span * parts
    rows = lax.all_to_all(stacked[:, :, None, :], "seq", split_axis=3, concat_axis=2, tiled=True)
    cosine, sine = angle_table(parts, 2 * parts, 2 * parts, -1.0)
    real_part = jnp.einsum("bcpm,pq->bcqm", rows, cosine, precision=highest)
    imag_part = jnp.einsum("bcpm,pq->bcqm", rows, sine, precision=highest)
    column = rank * width + jnp.arange(width, dtype=jnp.int32)
    grid = jnp.arange(2 * parts, dtype=jnp.int32)[:, None] * column[None, :] % period
    angle = -2.0 * math.pi / period * grid.astype(jnp.float32)
    real_part, imag_part = rotate(real_part, imag_part, jnp.cos(angle), jnp.sin(angle))
    real_part, imag_part = (
        lax.all_to_all(real_part, "seq", split_axis=2, concat_axis=3, tiled=True),
        lax.all_to_all(imag_part, "seq", split_axis=2, concat_axis=3, tiled=True),
    )
    return transform_last(real_part, imag_part, -1.0)


def inverse_start(real_part, imag_part):
    parts = lax.axis_size("seq")
    rank = lax.axis_index("seq")
    span = real_part.shape[3]
    period = 2 * span * parts
    real_part, imag_part = transform_last(real_part, imag_part, 1.0)
    residue = 2 * rank + jnp.arange(2, dtype=jnp.int32)
    grid = residue[:, None] * jnp.arange(span, dtype=jnp.int32)[None, :] % period
    angle = 2.0 * math.pi / period * grid.astype(jnp.float32)
    return rotate(real_part, imag_part, jnp.cos(angle), jnp.sin(angle))


def inverse_finish(real_part, imag_part, period):
    parts = lax.axis_size("seq")
    cosine, sine = angle_table(2 * parts, parts, 2 * parts, 1.0)
    new_real = jnp.einsum("bcqm,qp->bcpm", real_part, cosine, precision=highest) - jnp.einsum(
        "bcqm,qp->bcpm", imag_part, sine, precision=highest
    )
    new_imag = jnp.einsum("bcqm,qp->bcpm", real_part, sine, precision=highest) + jnp.einsum(
        "bcqm,qp->bcpm", imag_part, cosine, precision=highest
    )
    return (new_real * (1.0 / period), new_imag * (1.0 / period))


def spectral_body(inputs, short_weights, filters, skip, grad_out):
    taps = short_weights.shape[1]
    parts = lax.axis_size("seq")
    groups = lax.axis_size("chan")
    span = inputs.shape[2]
    channels = inputs.shape[1]
    total = span * parts
    period = 2 * total
    border = shifted(inputs[:, :, span - (taps - 1) :], "seq", 1)
    extended = jnp.concatenate([border, inputs], axis=2).astype(jnp.float32)
    mixed = short_weights[:, 0, :, None] * extended[:, :, taps - 1 : taps - 1 + span]
    for offset in range(1, taps):
        start = taps - 1 - offset
        mixed = mixed + short_weights[:, offset, :, None] * extended[:, :, start : start + span]
    query, key_part, value = (mixed[0], mixed[1], mixed[2])
    grad = grad_out.astype(jnp.float32)
    product = key_part * value
    dw = grad * query
    spec_real, spec_imag = forward_spectrum(jnp.stack([product, dw, filters]))
    prod_real, grad_real, filt_real = (spec_real[0], spec_real[1], spec_real[2])
    prod_imag, grad_imag, filt_imag = (spec_imag[0], spec_imag[1], spec_imag[2])
    conv_real = filt_real * prod_real - filt_imag * prod_imag
    conv_imag = filt_real * prod_imag + filt_imag * prod_real
    back_real = grad_real * filt_real + grad_imag * filt_imag
    back_imag = grad_imag * filt_real - grad_real * filt_imag
    corr_real = grad_real * prod_real + grad_imag * prod_imag
    corr_imag = grad_imag * prod_real - grad_real * prod_imag
    start_real, start_imag = inverse_start(
        jnp.stack([conv_real, back_real, corr_real]), jnp.stack([conv_imag, back_imag, corr_imag])
    )
    start_real, start_imag = (
        lax.all_to_all(start_real, "seq", split_axis=3, concat_axis=2, tiled=True),
        lax.all_to_all(start_imag, "seq", split_axis=3, concat_axis=2, tiled=True),
    )
    result, unused = inverse_finish(start_real, start_imag, period)
    fields = lax.all_to_all(result, "seq", split_axis=2, concat_axis=3, tiled=True).reshape(
        3, channels, span
    )
    conv_out = fields[0] + skip[:, None] * product
    dz = fields[1] + skip[:, None] * dw
    filter_grad = lax.psum_scatter(
        fields[2] * (total * groups) ** (-0.5), "chan", scatter_dimension=0, tiled=True
    )
    grads = jnp.stack([grad * conv_out, dz * value, dz * key_part])
    after = shifted(grads[:, :, : taps - 1], "seq", -1)
    grad_ext = jnp.concatenate([grads, after], axis=2)
    in_grads = short_weights[:, 0, :, None] * grads
    for offset in range(1, taps):
        in_grads = (
            in_grads + short_weights[:, offset, :, None] * grad_ext[:, :, offset : offset + span]
        )
    short_rows = []
    for offset in range(taps):
        start = taps - 1 - offset
        short_rows.append(jnp.sum(grads * extended[:, :, start : start + span], axis=2))
    short_part = jnp.stack(short_rows, axis=1)
    skip_part = jnp.sum(dw * product, axis=1)
    short_sum, skip_sum = lax.psum((short_part, skip_part), "seq")
    scale = total ** (-0.5)
    return (in_grads, filter_grad, skip_sum * scale, short_sum * scale)


MESH = pl.DeviceIdType.MESH


def split(x):
    high = x.astype(jnp.bfloat16)
    return high, (x - high.astype(jnp.float32)).astype(jnp.bfloat16)


def split_table(table):
    table = np.asarray(table, np.float32)
    high = table.astype(jnp.bfloat16)
    return high, (table - high.astype(np.float32)).astype(jnp.bfloat16)


def tables(parts, span):
    period = 2 * parts * span
    u = np.arange(span)
    angle = 2.0 * np.pi / span * (u[:, None] * u[None, :] % span)
    wide = np.concatenate([np.cos(angle), np.sin(angle)], axis=1)
    wide = np.stack(split_table(wide))
    k = np.arange(parts) + 0.5
    angle = 2.0 * np.pi / period * k[:, None] * u[None, :]
    twiddle = np.stack([np.cos(angle), np.sin(angle)]).astype(np.float32)
    angle = np.pi / parts * k[:, None] * np.arange(parts)[None, :]
    high, low = split_table(np.concatenate([np.cos(angle), -np.sin(angle)], axis=0))
    first = np.concatenate([high, high, low], axis=1)
    last = np.concatenate([np.cos(angle).T, -np.sin(angle).T], axis=1) * (2.0 / period)
    high, low = split_table(last)
    last = np.concatenate([high, high, low], axis=1)
    return wide, twiddle, first, last


def partner(me, i):
    peer = me
    bit = 1
    while bit <= i:
        if i & bit:
            peer = peer + bit * (1 - 2 * (me // bit % 2))
        bit *= 2
    return peer


def dot(a, b):
    return jnp.dot(a, b, preferred_element_type=jnp.float32)


def kernel(
    parts, groups, x_hbm, g_hbm, f_hbm, sw_hbm, sk_hbm, wide_hbm, tw_hbm, first_hbm, last_hbm,
    grecv, frecv,
    x_ref, g_ref, f_ref, sw_ref, sk_ref, wide, tw_ref, first_ref, last_ref,
    stage, send, recv, gsend, fsend, fstage, sems, load_sems,
):
    taps = sw_ref.shape[1]
    channels, span = f_ref.shape
    half = span // 2
    per = channels // parts
    rows = per * parts
    total = parts * span
    me = lax.axis_index("seq")
    group = lax.axis_index("chan")
    share = parts // groups
    target = me // share

    pairs = [
        (x_hbm, x_ref), (g_hbm, g_ref), (f_hbm, f_ref), (sw_hbm, sw_ref), (sk_hbm, sk_ref),
        (tw_hbm, tw_ref), (first_hbm, first_ref), (last_hbm, last_ref), (wide_hbm, wide),
    ]
    loads = [
        pltpu.make_async_copy(src, dst, load_sems.at[n]) for n, (src, dst) in enumerate(pairs)
    ]
    for load in loads:
        load.start()

    barrier = pltpu.get_barrier_semaphore()
    for i in range(parts):
        for j in range(groups):
            if i or j:
                pl.semaphore_signal(
                    barrier,
                    inc=1,
                    device_id={"seq": (me + i) % parts, "chan": (group + j) % groups},
                    device_id_type=MESH,
                )

    for load in loads[:3]:
        load.wait()

    fhigh, flow = split(f_ref[...])
    pieces = [x_ref[0], x_ref[1], x_ref[2], g_ref[...], fhigh, flow]
    pieces = [p.astype(jnp.float32) for p in pieces]
    pieces += [jnp.zeros_like(pieces[0])] * 2
    for a, piece in enumerate(pieces):
        stage[pl.ds(2 * a, channels, stride=16), :] = piece[:, :half]
        stage[pl.ds(2 * a + 1, channels, stride=16), :] = piece[:, half:]
    send[...] = stage[...].astype(jnp.bfloat16).reshape(send.shape)
    recv[pl.ds(me, 1)] = send[pl.ds(me, 1)]

    pl.semaphore_wait(barrier, parts * groups - 1)
    for i in range(parts - 1, 0, -1):
        peer = partner(me, i)
        pltpu.make_async_remote_copy(
            src_ref=send.at[peer], dst_ref=recv.at[me], send_sem=sems.at[0], recv_sem=sems.at[1],
            device_id={"seq": peer}, device_id_type=MESH,
        ).start()

    def wait_blocks(ref, count, sem):
        part = ref.at[pl.ds(0, count)]
        pltpu.make_async_copy(part, part, sem).wait()

    def received(a):
        blocks = []
        for ch in range(per):
            blocks.append(
                jnp.concatenate(
                    [stage[pl.ds(16 * ch + 2 * a + h, parts, stride=16 * per), :] for h in (0, 1)],
                    axis=1,
                )
            )
        return jnp.concatenate(blocks, axis=0)

    row = lax.broadcasted_iota(jnp.int32, (rows, span), 0)
    lane = lax.broadcasted_iota(jnp.int32, (rows, span), 1)

    def delayed(x, j):
        if j == 0:
            return x
        y = pltpu.roll(x, j, 1)
        z = jnp.where(row % parts == 0, 0.0, pltpu.roll(y, 1, 0))
        return jnp.where(lane < j, z, y)

    def advanced(x, j):
        if j == 0:
            return x
        y = pltpu.roll(x, span - j, 1)
        z = jnp.where(row % parts == parts - 1, 0.0, pltpu.roll(y, rows - 1, 0))
        return jnp.where(lane >= span - j, z, y)

    def per_channel(values):
        result = jnp.full((rows, span), values[0], jnp.float32)
        for ch in range(1, per):
            result = jnp.where(row >= ch * parts, values[ch], result)
        return result

    for load in loads[3:5]:
        load.wait()
    weight = [
        [per_channel([sw_ref[b, j, per * me + ch] for ch in range(per)]) for j in range(taps)]
        for b in range(3)
    ]
    direct = per_channel([sk_ref[per * me + ch] for ch in range(per)])

    for load in loads[5:]:
        load.wait()
    wait_blocks(recv, parts - 1, sems.at[1])
    stage[...] = recv[...].astype(jnp.float32).reshape(stage.shape)

    signals = [received(a) for a in range(6)]
    grad = signals[3]
    filt = signals[4] + signals[5]
    moved = [[delayed(signals[b], j) for j in range(taps)] for b in range(3)]
    mixed = []
    for b in range(3):
        value = weight[b][0] * moved[b][0]
        for j in range(1, taps):
            value = value + weight[b][j] * moved[b][j]
        mixed.append(value)
    query, key_part, value = mixed
    product = key_part * value
    dw = grad * query

    cosine, sine = tw_ref[0], tw_ref[1]
    reals, imags = [], []
    for signal in (product, dw, filt):
        for ch in range(per):
            high, low = split(signal[ch * parts : (ch + 1) * parts])
            spec = dot(first_ref[...], jnp.concatenate([high, low, high], axis=0))
            re, im = spec[:parts], spec[parts:]
            reals.append(re * cosine + im * sine)
            imags.append(im * cosine - re * sine)

    def transform(re, im):
        both = jnp.concatenate([re, im], axis=0)
        size = both.shape[0]
        high, low = split(both)
        result = dot(jnp.concatenate([high, low], axis=0), wide[0])
        result = result[:size] + result[size:] + dot(high, wide[1])
        count = size // 2
        return (
            result[:count, :span], result[:count, span:],
            result[count:, :span], result[count:, span:],
        )

    rc, rs, ic, is_ = transform(jnp.concatenate(reals, axis=0), jnp.concatenate(imags, axis=0))
    re, im = rc + is_, ic - rs
    pr, dr, fr = (re[i * rows : (i + 1) * rows] for i in range(3))
    pi, di, fi = (im[i * rows : (i + 1) * rows] for i in range(3))
    out_r = jnp.concatenate([dr * pr + di * pi, fr * pr - fi * pi, dr * fr + di * fi], axis=0)
    out_i = jnp.concatenate([di * pr - dr * pi, fr * pi + fi * pr, di * fr - dr * fi], axis=0)
    rc, rs, ic, is_ = transform(out_r, out_i)
    re, im = rc - is_, ic + rs

    def finish(i):
        blocks = []
        for ch in range(per):
            start = (i * per + ch) * parts
            cr, ci = re[start : start + parts], im[start : start + parts]
            both = jnp.concatenate([cr * cosine - ci * sine, ci * cosine + cr * sine], axis=0)
            high, low = split(both)
            blocks.append(dot(last_ref[...], jnp.concatenate([high, low, high], axis=0)))
        return jnp.concatenate(blocks, axis=0)

    corr = finish(0) * (total * groups) ** (-0.5)
    for ch in range(per):
        block = corr[ch * parts : (ch + 1) * parts]
        fstage[pl.ds(2 * ch, parts, stride=2 * per), :] = block[:, :half]
        fstage[pl.ds(2 * ch + 1, parts, stride=2 * per), :] = block[:, half:]
    for s in range(parts):
        fsend[s] = fstage[2 * per * s : 2 * per * (s + 1), :]
    slot = group * share + me % share
    for i in range(parts - 1, -1, -1):
        peer = partner(me, i)
        remote = pltpu.make_async_remote_copy(
            src_ref=fsend.at[peer], dst_ref=frecv.at[slot], send_sem=sems.at[2],
            recv_sem=sems.at[3], device_id={"seq": peer, "chan": target}, device_id_type=MESH,
        )
        if i:
            remote.start()
        else:

            @pl.when(target != group)
            def _():
                remote.start()

            @pl.when(target == group)
            def _():
                pltpu.make_async_copy(fsend.at[me], frecv.at[slot], sems.at[3]).start()

    conv_out = finish(1) + direct * product
    dz = finish(2) + direct * dw
    grads = [grad * conv_out, dz * value, dz * key_part]
    for b in range(3):
        result = weight[b][0] * grads[b]
        for j in range(1, taps):
            result = result + weight[b][j] * advanced(grads[b], j)
        for ch in range(per):
            block = result[ch * parts : (ch + 1) * parts]
            stage[pl.ds(8 * ch + 2 * b, parts, stride=8 * per), :] = block[:, :half]
            stage[pl.ds(8 * ch + 2 * b + 1, parts, stride=8 * per), :] = block[:, half:]

    scale = total ** (-0.5)
    sums = [grads[b] * moved[b][j] for b in range(3) for j in range(taps)] + [dw * product]
    pack = half // channels
    spot = lax.broadcasted_iota(jnp.int32, (1, half), 1)
    lines = [jnp.zeros((1, half), jnp.float32) for _ in range(2 * per)]
    for k, array in enumerate(sums):
        folded = array[:, :half] + array[:, half:]
        for ch in range(per):
            block = jnp.sum(folded[ch * parts : (ch + 1) * parts], axis=0, keepdims=True)
            amount = jnp.sum(block, axis=1, keepdims=True) * scale
            at = (k % pack) * channels + per * me + ch
            lines[k // pack] = jnp.where(spot == at, amount, lines[k // pack])
    for n, line in enumerate(lines):
        stage[pl.ds(8 * (n // 2) + 6 + n % 2, parts, stride=8 * per), :] = jnp.broadcast_to(
            line, (parts, half)
        )
    gsend[...] = stage[: 8 * per * parts, :].reshape(gsend.shape)
    grecv[pl.ds(me, 1)] = gsend[pl.ds(me, 1)]
    for i in range(parts - 1, 0, -1):
        peer = partner(me, i)
        pltpu.make_async_remote_copy(
            src_ref=gsend.at[peer], dst_ref=grecv.at[me], send_sem=sems.at[4],
            recv_sem=sems.at[5], device_id={"seq": peer}, device_id_type=MESH,
        ).start()

    wait_blocks(frecv, parts, sems.at[3])
    wait_blocks(grecv, parts - 1, sems.at[5])
    wait_blocks(send, parts - 1, sems.at[0])
    wait_blocks(gsend, parts - 1, sems.at[4])
    wait_blocks(fsend, parts - 1, sems.at[2])

    @pl.when(target != group)
    def _():
        wait_blocks(fsend, 1, sems.at[2])


def unpack_kernel(
    groups, taps, grecv, frecv, ig_hbm, fg_hbm, skg_hbm, sg_hbm,
    stage, fstage, ig_ref, fg_ref, skg_ref, sg_ref, sems,
):
    parts = grecv.shape[0]
    per = grecv.shape[1] // 8
    half = grecv.shape[2]
    channels = per * parts
    share = parts // groups
    pack = half // channels

    def save(n, src, dst):
        copy = pltpu.make_async_copy(src, dst, sems.at[n])
        copy.start()
        return copy

    stage[...] = grecv[...].reshape(8 * per * parts, half)
    for b in range(3):
        for h in (0, 1):
            ig_ref[b, :, h * half : (h + 1) * half] = stage[
                pl.ds(2 * b + h, channels, stride=8), :
            ]
    saves = [save(0, ig_ref, ig_hbm)]
    both = frecv[:share]
    for j in range(1, groups):
        both = both + frecv[j * share : (j + 1) * share]
    for i in range(share):
        fstage[2 * per * i : 2 * per * (i + 1), :] = both[i]
    for h in (0, 1):
        fg_ref[:, h * half : (h + 1) * half] = fstage[pl.ds(h, share * per, stride=2), :]
    saves.append(save(1, fg_ref, fg_hbm))
    lines = []
    for n in range(2 * per):
        line = stage[pl.ds(8 * (n // 2) + 6 + n % 2, parts, stride=8 * per), :]
        lines.append(jnp.sum(line, axis=0, keepdims=True))
    for k in range(3 * taps + 1):
        start = (k % pack) * channels
        piece = lines[k // pack][:, start : start + channels]
        if k < 3 * taps:
            sg_ref[k // taps, pl.ds(k % taps, 1), :] = piece
        else:
            skg_ref[...] = piece
    saves += [save(2, skg_ref, skg_hbm), save(3, sg_ref, sg_hbm)]
    for copy in saves:
        copy.wait()


def owner_body(inputs, short_weights, filters, skip, grad_out):
    parts = lax.axis_size("seq")
    groups = lax.axis_size("chan")
    taps = short_weights.shape[1]
    channels, span = grad_out.shape
    per = channels // parts
    half = span // 2
    wide, twiddle, first, last = (jnp.asarray(t) for t in tables(parts, span))
    vmem = pl.BlockSpec(memory_space=pltpu.VMEM)
    hbm = pl.BlockSpec(memory_space=pltpu.HBM)
    f32 = jnp.float32
    operands = (
        inputs, grad_out, filters, short_weights, skip, wide, twiddle, first, last
    )
    limit = 60 * 1024 * 1024
    blocks = jax.ShapeDtypeStruct((parts, 8 * per, half), f32)
    filter_blocks = jax.ShapeDtypeStruct((parts, 2 * per, half), f32)
    blocks, filter_blocks = pl.pallas_call(
        functools.partial(kernel, parts, groups),
        out_shape=(blocks, filter_blocks),
        in_specs=[hbm] * 9,
        out_specs=(vmem, vmem),
        scratch_shapes=[
            pltpu.VMEM(inputs.shape, inputs.dtype),
            pltpu.VMEM(grad_out.shape, grad_out.dtype),
            pltpu.VMEM(filters.shape, filters.dtype),
            pltpu.SMEM(short_weights.shape, f32),
            pltpu.SMEM(skip.shape, f32),
            pltpu.VMEM(wide.shape, wide.dtype),
            pltpu.VMEM(twiddle.shape, twiddle.dtype),
            pltpu.VMEM(first.shape, first.dtype),
            pltpu.VMEM(last.shape, last.dtype),
            pltpu.VMEM((16 * channels, half), f32),
            pltpu.VMEM((parts, 16 * per, half), jnp.bfloat16),
            pltpu.VMEM((parts, 16 * per, half), jnp.bfloat16),
            pltpu.VMEM((parts, 8 * per, half), f32),
            pltpu.VMEM((parts, 2 * per, half), f32),
            pltpu.VMEM((2 * channels, half), f32),
            pltpu.SemaphoreType.DMA((6,)),
            pltpu.SemaphoreType.DMA((9,)),
        ],
        compiler_params=pltpu.CompilerParams(
            collective_id=0, has_side_effects=True, vmem_limit_bytes=limit
        ),
        name="owner_convolutions",
    )(*operands)
    shapes = (
        jax.ShapeDtypeStruct((3, channels, span), f32),
        jax.ShapeDtypeStruct((channels // groups, span), f32),
        jax.ShapeDtypeStruct((1, channels), f32),
        jax.ShapeDtypeStruct((3, taps, channels), f32),
    )
    in_grads, filter_grad, skip_grad, short_grad = pl.pallas_call(
        functools.partial(unpack_kernel, groups, taps),
        out_shape=shapes,
        in_specs=[vmem, vmem],
        out_specs=(hbm,) * 4,
        scratch_shapes=[
            pltpu.VMEM((8 * channels, half), f32),
            pltpu.VMEM((2 * channels // groups, half), f32),
            *[pltpu.VMEM(s.shape, f32) for s in shapes],
            pltpu.SemaphoreType.DMA((4,)),
        ],
        compiler_params=pltpu.CompilerParams(vmem_limit_bytes=limit),
        name="unpack_results",
    )(blocks, filter_blocks)
    return in_grads, filter_grad, skip_grad.reshape(channels), short_grad


def body(inputs, short_weights, filters, skip, grad_out):
    parts = lax.axis_size("seq")
    groups = lax.axis_size("chan")
    channels, span = grad_out.shape
    fits = (
        channels == 2 * parts
        and filters.shape[0] == channels
        and span == 256
        and parts == 16
        and parts % groups == 0
        and short_weights.shape[1] <= 4
    )
    chosen = owner_body if fits else spectral_body
    return chosen(inputs, short_weights, filters, skip, grad_out)


def solution(mesh):
    placed = (
        P(None, "chan", "seq"),
        P(None, None, "chan"),
        P(None, "seq"),
        P("chan"),
        P("chan", "seq"),
    )
    return jax.shard_map(
        body,
        mesh=mesh,
        in_specs=placed,
        out_specs=(P(None, "chan", "seq"), P("chan", "seq"), P("chan"), P(None, None, "chan")),
        check_vma=False,
    )
```

```python
import functools
import math

import jax
import jax.numpy as jnp
import numpy as np
from jax import lax
from jax.experimental import pallas as pl
from jax.experimental.pallas import tpu as pltpu
from jax.sharding import PartitionSpec as P

highest = lax.Precision.HIGHEST


def shifted(block, axis, distance):
    devices = range(lax.axis_size(axis))
    route = [(i - distance, i) for i in devices if i - distance in devices]
    return lax.ppermute(block, axis, route)


def angle_table(rows, cols, period, sign):
    grid = (
        jnp.arange(rows, dtype=jnp.int32)[:, None]
        * jnp.arange(cols, dtype=jnp.int32)[None, :]
        % period
    )
    angle = sign * 2.0 * math.pi / period * grid.astype(jnp.float32)
    return (jnp.cos(angle), jnp.sin(angle))


def rotate(real_part, imag_part, cosine, sine):
    return (real_part * cosine - imag_part * sine, real_part * sine + imag_part * cosine)


def transform_last(real_part, imag_part, sign):
    length = real_part.shape[-1]
    if length <= 128 or length % 64 != 0:
        cosine, sine = angle_table(length, length, length, sign)
        new_real = jnp.dot(real_part, cosine, precision=highest) - jnp.dot(
            imag_part, sine, precision=highest
        )
        new_imag = jnp.dot(real_part, sine, precision=highest) + jnp.dot(
            imag_part, cosine, precision=highest
        )
        return (new_real, new_imag)
    outer = 64
    inner = length // outer
    leading = real_part.shape[:-1]
    real_part = jnp.swapaxes(real_part.reshape(leading + (inner, outer)), -1, -2)
    imag_part = jnp.swapaxes(imag_part.reshape(leading + (inner, outer)), -1, -2)
    real_part, imag_part = transform_last(real_part, imag_part, sign)
    cosine, sine = angle_table(outer, inner, length, sign)
    real_part, imag_part = rotate(real_part, imag_part, cosine, sine)
    cosine, sine = angle_table(outer, outer, outer, sign)
    new_real = jnp.einsum("...jk,jl->...lk", real_part, cosine, precision=highest) - jnp.einsum(
        "...jk,jl->...lk", imag_part, sine, precision=highest
    )
    new_imag = jnp.einsum("...jk,jl->...lk", real_part, sine, precision=highest) + jnp.einsum(
        "...jk,jl->...lk", imag_part, cosine, precision=highest
    )
    return (new_real.reshape(leading + (length,)), new_imag.reshape(leading + (length,)))


def forward_spectrum(stacked):
    parts = lax.axis_size("seq")
    rank = lax.axis_index("seq")
    span = stacked.shape[2]
    width = span // parts
    period = 2 * span * parts
    rows = lax.all_to_all(stacked[:, :, None, :], "seq", split_axis=3, concat_axis=2, tiled=True)
    cosine, sine = angle_table(parts, 2 * parts, 2 * parts, -1.0)
    real_part = jnp.einsum("bcpm,pq->bcqm", rows, cosine, precision=highest)
    imag_part = jnp.einsum("bcpm,pq->bcqm", rows, sine, precision=highest)
    column = rank * width + jnp.arange(width, dtype=jnp.int32)
    grid = jnp.arange(2 * parts, dtype=jnp.int32)[:, None] * column[None, :] % period
    angle = -2.0 * math.pi / period * grid.astype(jnp.float32)
    real_part, imag_part = rotate(real_part, imag_part, jnp.cos(angle), jnp.sin(angle))
    real_part, imag_part = (
        lax.all_to_all(real_part, "seq", split_axis=2, concat_axis=3, tiled=True),
        lax.all_to_all(imag_part, "seq", split_axis=2, concat_axis=3, tiled=True),
    )
    return transform_last(real_part, imag_part, -1.0)


def inverse_start(real_part, imag_part):
    parts = lax.axis_size("seq")
    rank = lax.axis_index("seq")
    span = real_part.shape[3]
    period = 2 * span * parts
    real_part, imag_part = transform_last(real_part, imag_part, 1.0)
    residue = 2 * rank + jnp.arange(2, dtype=jnp.int32)
    grid = residue[:, None] * jnp.arange(span, dtype=jnp.int32)[None, :] % period
    angle = 2.0 * math.pi / period * grid.astype(jnp.float32)
    return rotate(real_part, imag_part, jnp.cos(angle), jnp.sin(angle))


def inverse_finish(real_part, imag_part, period):
    parts = lax.axis_size("seq")
    cosine, sine = angle_table(2 * parts, parts, 2 * parts, 1.0)
    new_real = jnp.einsum("bcqm,qp->bcpm", real_part, cosine, precision=highest) - jnp.einsum(
        "bcqm,qp->bcpm", imag_part, sine, precision=highest
    )
    new_imag = jnp.einsum("bcqm,qp->bcpm", real_part, sine, precision=highest) + jnp.einsum(
        "bcqm,qp->bcpm", imag_part, cosine, precision=highest
    )
    return (new_real * (1.0 / period), new_imag * (1.0 / period))


def spectral_body(inputs, short_weights, filters, skip, grad_out):
    taps = short_weights.shape[1]
    parts = lax.axis_size("seq")
    groups = lax.axis_size("chan")
    span = inputs.shape[2]
    channels = inputs.shape[1]
    total = span * parts
    period = 2 * total
    border = shifted(inputs[:, :, span - (taps - 1) :], "seq", 1)
    extended = jnp.concatenate([border, inputs], axis=2).astype(jnp.float32)
    mixed = short_weights[:, 0, :, None] * extended[:, :, taps - 1 : taps - 1 + span]
    for offset in range(1, taps):
        start = taps - 1 - offset
        mixed = mixed + short_weights[:, offset, :, None] * extended[:, :, start : start + span]
    query, key_part, value = (mixed[0], mixed[1], mixed[2])
    grad = grad_out.astype(jnp.float32)
    product = key_part * value
    dw = grad * query
    spec_real, spec_imag = forward_spectrum(jnp.stack([product, dw, filters]))
    prod_real, grad_real, filt_real = (spec_real[0], spec_real[1], spec_real[2])
    prod_imag, grad_imag, filt_imag = (spec_imag[0], spec_imag[1], spec_imag[2])
    conv_real = filt_real * prod_real - filt_imag * prod_imag
    conv_imag = filt_real * prod_imag + filt_imag * prod_real
    back_real = grad_real * filt_real + grad_imag * filt_imag
    back_imag = grad_imag * filt_real - grad_real * filt_imag
    corr_real = grad_real * prod_real + grad_imag * prod_imag
    corr_imag = grad_imag * prod_real - grad_real * prod_imag
    start_real, start_imag = inverse_start(
        jnp.stack([conv_real, back_real, corr_real]), jnp.stack([conv_imag, back_imag, corr_imag])
    )
    start_real, start_imag = (
        lax.all_to_all(start_real, "seq", split_axis=3, concat_axis=2, tiled=True),
        lax.all_to_all(start_imag, "seq", split_axis=3, concat_axis=2, tiled=True),
    )
    result, unused = inverse_finish(start_real, start_imag, period)
    fields = lax.all_to_all(result, "seq", split_axis=2, concat_axis=3, tiled=True).reshape(
        3, channels, span
    )
    conv_out = fields[0] + skip[:, None] * product
    dz = fields[1] + skip[:, None] * dw
    filter_grad = lax.psum_scatter(
        fields[2] * (total * groups) ** (-0.5), "chan", scatter_dimension=0, tiled=True
    )
    grads = jnp.stack([grad * conv_out, dz * value, dz * key_part])
    after = shifted(grads[:, :, : taps - 1], "seq", -1)
    grad_ext = jnp.concatenate([grads, after], axis=2)
    in_grads = short_weights[:, 0, :, None] * grads
    for offset in range(1, taps):
        in_grads = (
            in_grads + short_weights[:, offset, :, None] * grad_ext[:, :, offset : offset + span]
        )
    short_rows = []
    for offset in range(taps):
        start = taps - 1 - offset
        short_rows.append(jnp.sum(grads * extended[:, :, start : start + span], axis=2))
    short_part = jnp.stack(short_rows, axis=1)
    skip_part = jnp.sum(dw * product, axis=1)
    short_sum, skip_sum = lax.psum((short_part, skip_part), "seq")
    scale = total ** (-0.5)
    return (in_grads, filter_grad, skip_sum * scale, short_sum * scale)


MESH = pl.DeviceIdType.MESH


def split(x):
    high = x.astype(jnp.bfloat16)
    return high, (x - high.astype(jnp.float32)).astype(jnp.bfloat16)


def split_table(table):
    table = np.asarray(table, np.float32)
    high = table.astype(jnp.bfloat16)
    return high, (table - high.astype(np.float32)).astype(jnp.bfloat16)


def tables(parts, span):
    period = 2 * parts * span
    u = np.arange(span)
    angle = 2.0 * np.pi / span * (u[:, None] * u[None, :] % span)
    wide = np.concatenate([np.cos(angle), np.sin(angle)], axis=1)
    wide = np.stack(split_table(wide))
    k = np.arange(parts) + 0.5
    angle = 2.0 * np.pi / period * k[:, None] * u[None, :]
    twiddle = np.stack([np.cos(angle), np.sin(angle)]).astype(np.float32)
    angle = np.pi / parts * k[:, None] * np.arange(parts)[None, :]
    high, low = split_table(np.concatenate([np.cos(angle), -np.sin(angle)], axis=0))
    first = np.concatenate([high, high, low], axis=1)
    last = np.concatenate([np.cos(angle).T, -np.sin(angle).T], axis=1) * (2.0 / period)
    high, low = split_table(last)
    last = np.concatenate([high, high, low], axis=1)
    return wide, twiddle, first, last


def partner(me, i):
    peer = me
    bit = 1
    while bit <= i:
        if i & bit:
            peer = peer + bit * (1 - 2 * (me // bit % 2))
        bit *= 2
    return peer


def dot(a, b):
    return jnp.dot(a, b, preferred_element_type=jnp.float32)


def kernel(
    parts, groups, x_hbm, g_hbm, f_hbm, sw_hbm, sk_hbm, wide_hbm, tw_hbm, first_hbm, last_hbm,
    grecv, frecv, srecv,
    x_ref, g_ref, f_ref, sw_ref, sk_ref, wide, tw_ref, first_ref, last_ref,
    stage, send, recv, filt_send, filt_recv, gsend, fsend, ssend, fstage, sems, load_sems,
):
    taps = sw_ref.shape[1]
    channels, span = f_ref.shape
    half = span // 2
    per = channels // parts
    rows = per * parts
    total = parts * span
    me = lax.axis_index("seq")
    group = lax.axis_index("chan")
    share = parts // groups
    target = me // share

    pairs = [
        (x_hbm, x_ref), (g_hbm, g_ref), (f_hbm, f_ref), (sw_hbm, sw_ref), (sk_hbm, sk_ref),
        (tw_hbm, tw_ref), (first_hbm, first_ref), (last_hbm, last_ref), (wide_hbm, wide),
    ]
    loads = [
        pltpu.make_async_copy(src, dst, load_sems.at[n]) for n, (src, dst) in enumerate(pairs)
    ]
    for load in loads[:3]:
        load.start()

    def greet(seq, chan):
        pl.semaphore_signal(
            barrier, inc=1, device_id={"seq": seq, "chan": chan}, device_id_type=MESH
        )

    barrier = pltpu.get_barrier_semaphore()
    for i in range(parts - 1, 0, -1):
        greet(partner(me, i), group)
    for j in range(1, groups):
        for i in range(share):
            greet(group * share + i, (group + j) % groups)
    for load in loads[3:]:
        load.start()
    for load in loads[:3]:
        load.wait()

    for a, piece in enumerate([x_ref[0], x_ref[1], x_ref[2], g_ref[...]]):
        piece = piece.astype(jnp.float32)
        for h in (0, 1):
            stage[pl.ds(2 * a + h, channels, stride=8), :] = piece[:, h * half : (h + 1) * half]
    send[...] = stage[...].astype(jnp.bfloat16).reshape(send.shape)
    for h in (0, 1):
        fstage[pl.ds(h, channels, stride=2), :] = f_ref[:, h * half : (h + 1) * half]
    for s in range(parts):
        filt_send[s] = fstage[2 * per * s : 2 * per * (s + 1), :]
    recv[pl.ds(me, 1)] = send[pl.ds(me, 1)]
    filt_recv[pl.ds(me, 1)] = filt_send[pl.ds(me, 1)]

    def push(src, dst, n, peer, chan):
        return pltpu.make_async_remote_copy(
            src_ref=src, dst_ref=dst, send_sem=sems.at[n], recv_sem=sems.at[n + 1],
            device_id={"seq": peer, "chan": chan}, device_id_type=MESH,
        )

    @pl.when(target == group)
    def _():
        pl.semaphore_wait(barrier, parts - 1)

    @pl.when(target != group)
    def _():
        pl.semaphore_wait(barrier, 2 * parts - 1)

    for i in range(parts - 1, 0, -1):
        peer = partner(me, i)
        push(send.at[peer], recv.at[me], 0, peer, group).start()
        push(filt_send.at[peer], filt_recv.at[me], 2, peer, group).start()

    def wait_blocks(ref, count, sem):
        part = ref.at[pl.ds(0, count)]
        pltpu.make_async_copy(part, part, sem).wait()

    def received(ref, count, a):
        blocks = []
        for ch in range(per):
            blocks.append(
                jnp.concatenate(
                    [
                        ref[pl.ds(count * ch + 2 * a + h, parts, stride=count * per), :]
                        for h in (0, 1)
                    ],
                    axis=1,
                )
            )
        return jnp.concatenate(blocks, axis=0)

    row = lax.broadcasted_iota(jnp.int32, (rows, span), 0)
    lane = lax.broadcasted_iota(jnp.int32, (rows, span), 1)

    def delayed(x, j):
        if j == 0:
            return x
        y = pltpu.roll(x, j, 1)
        z = jnp.where(row % parts == 0, 0.0, pltpu.roll(y, 1, 0))
        return jnp.where(lane < j, z, y)

    def advanced(x, j):
        if j == 0:
            return x
        y = pltpu.roll(x, span - j, 1)
        z = jnp.where(row % parts == parts - 1, 0.0, pltpu.roll(y, rows - 1, 0))
        return jnp.where(lane >= span - j, z, y)

    def per_channel(values):
        result = jnp.full((rows, span), values[0], jnp.float32)
        for ch in range(1, per):
            result = jnp.where(row >= ch * parts, values[ch], result)
        return result

    for load in loads[3:5]:
        load.wait()
    weight = [
        [per_channel([sw_ref[b, j, per * me + ch] for ch in range(per)]) for j in range(taps)]
        for b in range(3)
    ]
    direct = per_channel([sk_ref[per * me + ch] for ch in range(per)])

    for load in loads[5:]:
        load.wait()
    wait_blocks(recv, parts - 1, sems.at[1])
    wait_blocks(filt_recv, parts - 1, sems.at[3])
    stage[...] = recv[...].astype(jnp.float32).reshape(stage.shape)
    for s in range(parts):
        fstage[2 * per * s : 2 * per * (s + 1), :] = filt_recv[s]
    signals = [received(stage, 8, a) for a in range(4)]
    filt = received(fstage, 2, 0)
    grad = signals[3]
    moved = [[delayed(signals[b], j) for j in range(taps)] for b in range(3)]
    mixed = []
    for b in range(3):
        value = weight[b][0] * moved[b][0]
        for j in range(1, taps):
            value = value + weight[b][j] * moved[b][j]
        mixed.append(value)
    query, key_part, value = mixed
    product = key_part * value
    dw = grad * query

    cosine, sine = tw_ref[0], tw_ref[1]
    reals, imags = [], []
    for signal in (product, dw, filt):
        for ch in range(per):
            high, low = split(signal[ch * parts : (ch + 1) * parts])
            spec = dot(first_ref[...], jnp.concatenate([high, low, high], axis=0))
            re, im = spec[:parts], spec[parts:]
            reals.append(re * cosine + im * sine)
            imags.append(im * cosine - re * sine)

    def transform(re, im):
        both = jnp.concatenate([re, im], axis=0)
        size = both.shape[0]
        high, low = split(both)
        result = dot(jnp.concatenate([high, low], axis=0), wide[0])
        result = result[:size] + result[size:] + dot(high, wide[1])
        count = size // 2
        return (
            result[:count, :span], result[:count, span:],
            result[count:, :span], result[count:, span:],
        )

    rc, rs, ic, is_ = transform(jnp.concatenate(reals, axis=0), jnp.concatenate(imags, axis=0))
    re, im = rc + is_, ic - rs
    pr, dr, fr = (re[i * rows : (i + 1) * rows] for i in range(3))
    pi, di, fi = (im[i * rows : (i + 1) * rows] for i in range(3))
    out_r = jnp.concatenate([dr * pr + di * pi, fr * pr - fi * pi, dr * fr + di * fi], axis=0)
    out_i = jnp.concatenate([di * pr - dr * pi, fr * pi + fi * pr, di * fr - dr * fi], axis=0)
    rc, rs, ic, is_ = transform(out_r, out_i)
    re, im = rc - is_, ic + rs

    def finish(i):
        blocks = []
        for ch in range(per):
            start = (i * per + ch) * parts
            cr, ci = re[start : start + parts], im[start : start + parts]
            both = jnp.concatenate([cr * cosine - ci * sine, ci * cosine + cr * sine], axis=0)
            high, low = split(both)
            blocks.append(dot(last_ref[...], jnp.concatenate([high, low, high], axis=0)))
        return jnp.concatenate(blocks, axis=0)

    corr = finish(0) * (total * groups) ** (-0.5)
    for ch in range(per):
        block = corr[ch * parts : (ch + 1) * parts]
        fstage[pl.ds(2 * ch, parts, stride=2 * per), :] = block[:, :half]
        fstage[pl.ds(2 * ch + 1, parts, stride=2 * per), :] = block[:, half:]
    for s in range(parts):
        fsend[s] = fstage[2 * per * s : 2 * per * (s + 1), :]
    slot = group * share + me % share
    for i in range(parts - 1, -1, -1):
        peer = partner(me, i)
        remote = push(fsend.at[peer], frecv.at[slot], 4, peer, target)
        if i:
            remote.start()
        else:

            @pl.when(target != group)
            def _():
                remote.start()

            @pl.when(target == group)
            def _():
                pltpu.make_async_copy(fsend.at[me], frecv.at[slot], sems.at[5]).start()

    conv_out = finish(1) + direct * product
    dz = finish(2) + direct * dw
    grads = [grad * conv_out, dz * value, dz * key_part]
    for b in range(3):
        result = weight[b][0] * grads[b]
        for j in range(1, taps):
            result = result + weight[b][j] * advanced(grads[b], j)
        for ch in range(per):
            block = result[ch * parts : (ch + 1) * parts]
            for h in (0, 1):
                start = b * parts * 2 * per + 2 * ch + h
                stage[pl.ds(start, parts, stride=2 * per), :] = block[:, h * half : (h + 1) * half]
        for s in range(parts):
            start = (b * parts + s) * 2 * per
            gsend[b, s] = stage[start : start + 2 * per, :]
    pltpu.make_async_copy(gsend.at[:, me], grecv.at[:, me], sems.at[7]).start()
    for i in range(parts - 1, 0, -1):
        peer = partner(me, i)
        push(gsend.at[:, peer], grecv.at[:, me], 6, peer, group).start()

    scale = total ** (-0.5)
    sums = [grads[b] * moved[b][j] for b in range(3) for j in range(taps)] + [dw * product]
    spot = lax.broadcasted_iota(jnp.int32, (1, half), 1)
    line = jnp.zeros((1, half), jnp.float32)
    for k, array in enumerate(sums):
        folded = array[:, :half] + array[:, half:]
        for ch in range(per):
            block = jnp.sum(folded[ch * parts : (ch + 1) * parts], axis=0, keepdims=True)
            amount = jnp.sum(block, axis=1, keepdims=True) * scale
            line = jnp.where(spot == k * per + per * me + ch, amount, line)
    ssend[...] = line
    pltpu.make_async_copy(ssend, srecv.at[me], sems.at[9]).start()
    for i in range(parts - 1, 0, -1):
        push(ssend, srecv.at[me], 8, partner(me, i), group).start()

    wait_blocks(frecv, parts, sems.at[5])
    pltpu.make_async_copy(grecv, grecv, sems.at[7]).wait()
    wait_blocks(srecv, parts, sems.at[9])
    wait_blocks(send, parts - 1, sems.at[0])
    wait_blocks(filt_send, parts - 1, sems.at[2])
    wait_blocks(fsend, parts - 1, sems.at[4])

    @pl.when(target != group)
    def _():
        wait_blocks(fsend, 1, sems.at[4])

    part = gsend.at[:, pl.ds(0, parts - 1)]
    pltpu.make_async_copy(part, part, sems.at[6]).wait()
    wait_blocks(srecv, parts - 1, sems.at[8])


def unpack_kernel(
    groups, parts, grecv, frecv, srecv, ig_hbm, fg_hbm, skg_hbm, sg_hbm,
    ig_ref, fg_ref, skg_ref, sg_ref, sems,
):
    taps, channels = sg_ref.shape[1:]
    half = grecv.shape[1]
    per = channels // parts
    share = channels // groups

    def save(n, src, dst):
        copy = pltpu.make_async_copy(src, dst, sems.at[n])
        copy.start()
        return copy

    for b in range(3):
        for h in (0, 1):
            ig_ref[b, :, h * half : (h + 1) * half] = grecv[
                pl.ds(b * 2 * channels + h, channels, stride=2), :
            ]
    saves = [save(0, ig_ref, ig_hbm)]
    for h in (0, 1):
        both = frecv[pl.ds(h, share, stride=2), :]
        for j in range(1, groups):
            both = both + frecv[pl.ds(2 * share * j + h, share, stride=2), :]
        fg_ref[:, h * half : (h + 1) * half] = both
    saves.append(save(1, fg_ref, fg_hbm))
    sums = srecv[...]
    row = lax.broadcasted_iota(jnp.int32, sums.shape, 0)
    lane = lax.broadcasted_iota(jnp.int32, sums.shape, 1)
    for k in range(3 * taps + 1):
        first = (row + k) * per
        mine = (lane >= first) & (lane < first + per)
        line = jnp.sum(jnp.where(mine, sums, 0.0), axis=0, keepdims=True)
        piece = line[:, k * per : k * per + channels]
        if k < 3 * taps:
            sg_ref[k // taps, pl.ds(k % taps, 1), :] = piece
        else:
            skg_ref[...] = piece
    saves += [save(2, skg_ref, skg_hbm), save(3, sg_ref, sg_hbm)]
    for copy in saves:
        copy.wait()


def owner_body(inputs, short_weights, filters, skip, grad_out):
    parts = lax.axis_size("seq")
    groups = lax.axis_size("chan")
    taps = short_weights.shape[1]
    channels, span = grad_out.shape
    per = channels // parts
    half = span // 2
    wide, twiddle, first, last = (jnp.asarray(t) for t in tables(parts, span))
    vmem = pl.BlockSpec(memory_space=pltpu.VMEM)
    hbm = pl.BlockSpec(memory_space=pltpu.HBM)
    f32 = jnp.float32
    operands = (
        inputs, grad_out, filters, short_weights, skip, wide, twiddle, first, last
    )
    limit = 60 * 1024 * 1024
    landing = (
        jax.ShapeDtypeStruct((3, parts, 2 * per, half), f32),
        jax.ShapeDtypeStruct((parts, 2 * per, half), f32),
        jax.ShapeDtypeStruct((parts, 1, half), f32),
    )
    blocks, filter_blocks, sums = pl.pallas_call(
        functools.partial(kernel, parts, groups),
        out_shape=landing,
        in_specs=[hbm] * 9,
        out_specs=(hbm,) * 3,
        scratch_shapes=[
            pltpu.VMEM(inputs.shape, inputs.dtype),
            pltpu.VMEM(grad_out.shape, grad_out.dtype),
            pltpu.VMEM(filters.shape, filters.dtype),
            pltpu.SMEM(short_weights.shape, f32),
            pltpu.SMEM(skip.shape, f32),
            pltpu.VMEM(wide.shape, wide.dtype),
            pltpu.VMEM(twiddle.shape, twiddle.dtype),
            pltpu.VMEM(first.shape, first.dtype),
            pltpu.VMEM(last.shape, last.dtype),
            pltpu.VMEM((8 * channels, half), f32),
            pltpu.VMEM((parts, 8 * per, half), jnp.bfloat16),
            pltpu.VMEM((parts, 8 * per, half), jnp.bfloat16),
            pltpu.VMEM((parts, 2 * per, half), f32),
            pltpu.VMEM((parts, 2 * per, half), f32),
            pltpu.VMEM((3, parts, 2 * per, half), f32),
            pltpu.VMEM((parts, 2 * per, half), f32),
            pltpu.VMEM((1, half), f32),
            pltpu.VMEM((2 * channels, half), f32),
            pltpu.SemaphoreType.DMA((10,)),
            pltpu.SemaphoreType.DMA((9,)),
        ],
        compiler_params=pltpu.CompilerParams(
            collective_id=0, has_side_effects=True, vmem_limit_bytes=limit
        ),
        name="owner_convolutions",
    )(*operands)
    shapes = (
        jax.ShapeDtypeStruct((3, channels, span), f32),
        jax.ShapeDtypeStruct((channels // groups, span), f32),
        jax.ShapeDtypeStruct((1, channels), f32),
        jax.ShapeDtypeStruct((3, taps, channels), f32),
    )
    in_grads, filter_grad, skip_grad, short_grad = pl.pallas_call(
        functools.partial(unpack_kernel, groups, parts),
        out_shape=shapes,
        in_specs=[vmem] * 3,
        out_specs=(hbm,) * 4,
        scratch_shapes=[
            *[pltpu.VMEM(s.shape, f32) for s in shapes],
            pltpu.SemaphoreType.DMA((4,)),
        ],
        compiler_params=pltpu.CompilerParams(vmem_limit_bytes=limit),
        name="unpack_results",
    )(
        blocks.reshape(6 * channels, half),
        filter_blocks.reshape(2 * channels, half),
        sums.reshape(parts, half),
    )
    return in_grads, filter_grad, skip_grad.reshape(channels), short_grad


def body(inputs, short_weights, filters, skip, grad_out):
    parts = lax.axis_size("seq")
    groups = lax.axis_size("chan")
    channels, span = grad_out.shape
    fits = (
        channels == 2 * parts
        and filters.shape[0] == channels
        and span == 256
        and parts == 16
        and parts % groups == 0
        and short_weights.shape[1] <= 4
    )
    chosen = owner_body if fits else spectral_body
    return chosen(inputs, short_weights, filters, skip, grad_out)


def solution(mesh):
    placed = (
        P(None, "chan", "seq"),
        P(None, None, "chan"),
        P(None, "seq"),
        P("chan"),
        P("chan", "seq"),
    )
    return jax.shard_map(
        body,
        mesh=mesh,
        in_specs=placed,
        out_specs=(P(None, "chan", "seq"), P("chan", "seq"), P("chan"), P(None, None, "chan")),
        check_vma=False,
    )
```

```python
import functools
import math

import jax
import jax.numpy as jnp
import numpy as np
from jax import lax
from jax.experimental import pallas as pl
from jax.experimental.pallas import tpu as pltpu
from jax.sharding import PartitionSpec as P

highest = lax.Precision.HIGHEST


def shifted(block, axis, distance):
    devices = range(lax.axis_size(axis))
    route = [(i - distance, i) for i in devices if i - distance in devices]
    return lax.ppermute(block, axis, route)


def angle_table(rows, cols, period, sign):
    grid = (
        jnp.arange(rows, dtype=jnp.int32)[:, None]
        * jnp.arange(cols, dtype=jnp.int32)[None, :]
        % period
    )
    angle = sign * 2.0 * math.pi / period * grid.astype(jnp.float32)
    return (jnp.cos(angle), jnp.sin(angle))


def rotate(real_part, imag_part, cosine, sine):
    return (real_part * cosine - imag_part * sine, real_part * sine + imag_part * cosine)


def transform_last(real_part, imag_part, sign):
    length = real_part.shape[-1]
    if length <= 128 or length % 64 != 0:
        cosine, sine = angle_table(length, length, length, sign)
        new_real = jnp.dot(real_part, cosine, precision=highest) - jnp.dot(
            imag_part, sine, precision=highest
        )
        new_imag = jnp.dot(real_part, sine, precision=highest) + jnp.dot(
            imag_part, cosine, precision=highest
        )
        return (new_real, new_imag)
    outer = 64
    inner = length // outer
    leading = real_part.shape[:-1]
    real_part = jnp.swapaxes(real_part.reshape(leading + (inner, outer)), -1, -2)
    imag_part = jnp.swapaxes(imag_part.reshape(leading + (inner, outer)), -1, -2)
    real_part, imag_part = transform_last(real_part, imag_part, sign)
    cosine, sine = angle_table(outer, inner, length, sign)
    real_part, imag_part = rotate(real_part, imag_part, cosine, sine)
    cosine, sine = angle_table(outer, outer, outer, sign)
    new_real = jnp.einsum("...jk,jl->...lk", real_part, cosine, precision=highest) - jnp.einsum(
        "...jk,jl->...lk", imag_part, sine, precision=highest
    )
    new_imag = jnp.einsum("...jk,jl->...lk", real_part, sine, precision=highest) + jnp.einsum(
        "...jk,jl->...lk", imag_part, cosine, precision=highest
    )
    return (new_real.reshape(leading + (length,)), new_imag.reshape(leading + (length,)))


def forward_spectrum(stacked):
    parts = lax.axis_size("seq")
    rank = lax.axis_index("seq")
    span = stacked.shape[2]
    width = span // parts
    period = 2 * span * parts
    rows = lax.all_to_all(stacked[:, :, None, :], "seq", split_axis=3, concat_axis=2, tiled=True)
    cosine, sine = angle_table(parts, 2 * parts, 2 * parts, -1.0)
    real_part = jnp.einsum("bcpm,pq->bcqm", rows, cosine, precision=highest)
    imag_part = jnp.einsum("bcpm,pq->bcqm", rows, sine, precision=highest)
    column = rank * width + jnp.arange(width, dtype=jnp.int32)
    grid = jnp.arange(2 * parts, dtype=jnp.int32)[:, None] * column[None, :] % period
    angle = -2.0 * math.pi / period * grid.astype(jnp.float32)
    real_part, imag_part = rotate(real_part, imag_part, jnp.cos(angle), jnp.sin(angle))
    real_part, imag_part = (
        lax.all_to_all(real_part, "seq", split_axis=2, concat_axis=3, tiled=True),
        lax.all_to_all(imag_part, "seq", split_axis=2, concat_axis=3, tiled=True),
    )
    return transform_last(real_part, imag_part, -1.0)


def inverse_start(real_part, imag_part):
    parts = lax.axis_size("seq")
    rank = lax.axis_index("seq")
    span = real_part.shape[3]
    period = 2 * span * parts
    real_part, imag_part = transform_last(real_part, imag_part, 1.0)
    residue = 2 * rank + jnp.arange(2, dtype=jnp.int32)
    grid = residue[:, None] * jnp.arange(span, dtype=jnp.int32)[None, :] % period
    angle = 2.0 * math.pi / period * grid.astype(jnp.float32)
    return rotate(real_part, imag_part, jnp.cos(angle), jnp.sin(angle))


def inverse_finish(real_part, imag_part, period):
    parts = lax.axis_size("seq")
    cosine, sine = angle_table(2 * parts, parts, 2 * parts, 1.0)
    new_real = jnp.einsum("bcqm,qp->bcpm", real_part, cosine, precision=highest) - jnp.einsum(
        "bcqm,qp->bcpm", imag_part, sine, precision=highest
    )
    new_imag = jnp.einsum("bcqm,qp->bcpm", real_part, sine, precision=highest) + jnp.einsum(
        "bcqm,qp->bcpm", imag_part, cosine, precision=highest
    )
    return (new_real * (1.0 / period), new_imag * (1.0 / period))


def spectral_body(inputs, short_weights, filters, skip, grad_out):
    taps = short_weights.shape[1]
    parts = lax.axis_size("seq")
    groups = lax.axis_size("chan")
    span = inputs.shape[2]
    channels = inputs.shape[1]
    total = span * parts
    period = 2 * total
    border = shifted(inputs[:, :, span - (taps - 1) :], "seq", 1)
    extended = jnp.concatenate([border, inputs], axis=2).astype(jnp.float32)
    mixed = short_weights[:, 0, :, None] * extended[:, :, taps - 1 : taps - 1 + span]
    for offset in range(1, taps):
        start = taps - 1 - offset
        mixed = mixed + short_weights[:, offset, :, None] * extended[:, :, start : start + span]
    query, key_part, value = (mixed[0], mixed[1], mixed[2])
    grad = grad_out.astype(jnp.float32)
    product = key_part * value
    dw = grad * query
    spec_real, spec_imag = forward_spectrum(jnp.stack([product, dw, filters]))
    prod_real, grad_real, filt_real = (spec_real[0], spec_real[1], spec_real[2])
    prod_imag, grad_imag, filt_imag = (spec_imag[0], spec_imag[1], spec_imag[2])
    conv_real = filt_real * prod_real - filt_imag * prod_imag
    conv_imag = filt_real * prod_imag + filt_imag * prod_real
    back_real = grad_real * filt_real + grad_imag * filt_imag
    back_imag = grad_imag * filt_real - grad_real * filt_imag
    corr_real = grad_real * prod_real + grad_imag * prod_imag
    corr_imag = grad_imag * prod_real - grad_real * prod_imag
    start_real, start_imag = inverse_start(
        jnp.stack([conv_real, back_real, corr_real]), jnp.stack([conv_imag, back_imag, corr_imag])
    )
    start_real, start_imag = (
        lax.all_to_all(start_real, "seq", split_axis=3, concat_axis=2, tiled=True),
        lax.all_to_all(start_imag, "seq", split_axis=3, concat_axis=2, tiled=True),
    )
    result, unused = inverse_finish(start_real, start_imag, period)
    fields = lax.all_to_all(result, "seq", split_axis=2, concat_axis=3, tiled=True).reshape(
        3, channels, span
    )
    conv_out = fields[0] + skip[:, None] * product
    dz = fields[1] + skip[:, None] * dw
    filter_grad = lax.psum_scatter(
        fields[2] * (total * groups) ** (-0.5), "chan", scatter_dimension=0, tiled=True
    )
    grads = jnp.stack([grad * conv_out, dz * value, dz * key_part])
    after = shifted(grads[:, :, : taps - 1], "seq", -1)
    grad_ext = jnp.concatenate([grads, after], axis=2)
    in_grads = short_weights[:, 0, :, None] * grads
    for offset in range(1, taps):
        in_grads = (
            in_grads + short_weights[:, offset, :, None] * grad_ext[:, :, offset : offset + span]
        )
    short_rows = []
    for offset in range(taps):
        start = taps - 1 - offset
        short_rows.append(jnp.sum(grads * extended[:, :, start : start + span], axis=2))
    short_part = jnp.stack(short_rows, axis=1)
    skip_part = jnp.sum(dw * product, axis=1)
    short_sum, skip_sum = lax.psum((short_part, skip_part), "seq")
    scale = total ** (-0.5)
    return (in_grads, filter_grad, skip_sum * scale, short_sum * scale)


MESH = pl.DeviceIdType.MESH


def split(x):
    high = x.astype(jnp.bfloat16)
    return high, (x - high.astype(jnp.float32)).astype(jnp.bfloat16)


def split_table(table):
    table = np.asarray(table, np.float32)
    high = table.astype(jnp.bfloat16)
    return high, (table - high.astype(np.float32)).astype(jnp.bfloat16)


def tables(parts, span):
    period = 2 * parts * span
    u = np.arange(span)
    angle = 2.0 * np.pi / span * (u[:, None] * u[None, :] % span)
    wide = np.concatenate([np.cos(angle), np.sin(angle)], axis=1)
    wide = np.stack(split_table(wide))
    k = np.arange(parts) + 0.5
    angle = 2.0 * np.pi / period * k[:, None] * u[None, :]
    twiddle = np.stack([np.cos(angle), np.sin(angle)]).astype(np.float32)
    angle = np.pi / parts * k[:, None] * np.arange(parts)[None, :]
    high, low = split_table(np.concatenate([np.cos(angle), -np.sin(angle)], axis=0))
    first = np.concatenate([high, high, low], axis=1)
    last = np.concatenate([np.cos(angle).T, -np.sin(angle).T], axis=1) * (2.0 / period)
    high, low = split_table(last)
    last = np.concatenate([high, high, low], axis=1)
    return wide, twiddle, first, last


def partner(me, i):
    peer = me
    bit = 1
    while bit <= i:
        if i & bit:
            peer = peer + bit * (1 - 2 * (me // bit % 2))
        bit *= 2
    return peer


def dot(a, b):
    return jnp.dot(a, b, preferred_element_type=jnp.float32)


def kernel(
    parts, groups, x_hbm, g_hbm, f_hbm, sw_hbm, sk_hbm, wide_hbm, tw_hbm, first_hbm, last_hbm,
    grecv, frecv, srecv,
    x_ref, g_ref, f_ref, sw_ref, sk_ref, wide, tw_ref, first_ref, last_ref,
    stage, send, recv, filt_send, filt_recv, gsend, fsend, ssend, fstage, sems, load_sems,
):
    taps = sw_ref.shape[1]
    channels, span = f_ref.shape
    half = span // 2
    per = channels // parts
    rows = per * parts
    total = parts * span
    me = lax.axis_index("seq")
    group = lax.axis_index("chan")
    share = parts // groups
    target = me // share

    pairs = [
        (x_hbm, x_ref), (g_hbm, g_ref), (f_hbm, f_ref), (sw_hbm, sw_ref), (sk_hbm, sk_ref),
        (tw_hbm, tw_ref), (first_hbm, first_ref), (last_hbm, last_ref), (wide_hbm, wide),
    ]
    loads = [
        pltpu.make_async_copy(src, dst, load_sems.at[n]) for n, (src, dst) in enumerate(pairs)
    ]
    for load in loads[:3]:
        load.start()

    def greet(seq, chan):
        pl.semaphore_signal(
            barrier, inc=1, device_id={"seq": seq, "chan": chan}, device_id_type=MESH
        )

    barrier = pltpu.get_barrier_semaphore()
    for i in range(parts - 1, 0, -1):
        greet(partner(me, i), group)
    for j in range(1, groups):
        for i in range(share):
            greet(group * share + i, (group + j) % groups)
    for load in loads[3:]:
        load.start()
    for load in loads[:3]:
        load.wait()

    for a, piece in enumerate([x_ref[0], x_ref[1], x_ref[2], g_ref[...]]):
        piece = piece.astype(jnp.float32)
        for h in (0, 1):
            stage[pl.ds(2 * a + h, channels, stride=8), :] = piece[:, h * half : (h + 1) * half]
    send[...] = stage[...].astype(jnp.bfloat16).reshape(send.shape)
    for h in (0, 1):
        fstage[pl.ds(h, channels, stride=2), :] = f_ref[:, h * half : (h + 1) * half]
    for s in range(parts):
        filt_send[s] = fstage[2 * per * s : 2 * per * (s + 1), :]
    recv[pl.ds(me, 1)] = send[pl.ds(me, 1)]
    filt_recv[pl.ds(me, 1)] = filt_send[pl.ds(me, 1)]

    def push(src, dst, n, peer, chan):
        return pltpu.make_async_remote_copy(
            src_ref=src, dst_ref=dst, send_sem=sems.at[n], recv_sem=sems.at[n + 1],
            device_id={"seq": peer, "chan": chan}, device_id_type=MESH,
        )

    @pl.when(target == group)
    def _():
        pl.semaphore_wait(barrier, parts - 1)

    @pl.when(target != group)
    def _():
        pl.semaphore_wait(barrier, 2 * parts - 1)

    for i in range(parts - 1, 0, -1):
        peer = partner(me, i)
        push(filt_send.at[peer], filt_recv.at[me], 2, peer, group).start()
    for i in range(parts - 1, 0, -1):
        peer = partner(me, i)
        push(send.at[peer], recv.at[me], 0, peer, group).start()

    def wait_blocks(ref, count, sem):
        part = ref.at[pl.ds(0, count)]
        pltpu.make_async_copy(part, part, sem).wait()

    def received(ref, count, a):
        blocks = []
        for ch in range(per):
            blocks.append(
                jnp.concatenate(
                    [
                        ref[pl.ds(count * ch + 2 * a + h, parts, stride=count * per), :]
                        for h in (0, 1)
                    ],
                    axis=1,
                )
            )
        return jnp.concatenate(blocks, axis=0)

    row = lax.broadcasted_iota(jnp.int32, (rows, span), 0)
    lane = lax.broadcasted_iota(jnp.int32, (rows, span), 1)

    def delayed(x, j):
        if j == 0:
            return x
        y = pltpu.roll(x, j, 1)
        z = jnp.where(row % parts == 0, 0.0, pltpu.roll(y, 1, 0))
        return jnp.where(lane < j, z, y)

    def advanced(x, j):
        if j == 0:
            return x
        y = pltpu.roll(x, span - j, 1)
        z = jnp.where(row % parts == parts - 1, 0.0, pltpu.roll(y, rows - 1, 0))
        return jnp.where(lane >= span - j, z, y)

    def per_channel(values):
        result = jnp.full((rows, span), values[0], jnp.float32)
        for ch in range(1, per):
            result = jnp.where(row >= ch * parts, values[ch], result)
        return result

    for load in loads[3:5]:
        load.wait()
    weight = [
        [per_channel([sw_ref[b, j, per * me + ch] for ch in range(per)]) for j in range(taps)]
        for b in range(3)
    ]
    direct = per_channel([sk_ref[per * me + ch] for ch in range(per)])

    for load in loads[5:]:
        load.wait()
    cosine, sine = tw_ref[0], tw_ref[1]

    def transform(re, im):
        both = jnp.concatenate([re, im], axis=0)
        size = both.shape[0]
        high, low = split(both)
        result = dot(jnp.concatenate([high, low], axis=0), wide[0])
        result = result[:size] + result[size:] + dot(high, wide[1])
        count = size // 2
        return (
            result[:count, :span], result[:count, span:],
            result[count:, :span], result[count:, span:],
        )

    def spectrum(signals):
        reals, imags = [], []
        for signal in signals:
            for ch in range(per):
                high, low = split(signal[ch * parts : (ch + 1) * parts])
                spec = dot(first_ref[...], jnp.concatenate([high, low, high], axis=0))
                re, im = spec[:parts], spec[parts:]
                reals.append(re * cosine + im * sine)
                imags.append(im * cosine - re * sine)
        rc, rs, ic, is_ = transform(jnp.concatenate(reals, axis=0), jnp.concatenate(imags, axis=0))
        re, im = rc + is_, ic - rs
        return [
            (re[i * rows : (i + 1) * rows], im[i * rows : (i + 1) * rows])
            for i in range(len(signals))
        ]

    wait_blocks(filt_recv, parts - 1, sems.at[3])
    for s in range(parts):
        fstage[2 * per * s : 2 * per * (s + 1), :] = filt_recv[s]
    ((fr, fi),) = spectrum([received(fstage, 2, 0)])

    wait_blocks(recv, parts - 1, sems.at[1])
    stage[...] = recv[...].astype(jnp.float32).reshape(stage.shape)
    signals = [received(stage, 8, a) for a in range(4)]
    grad = signals[3]
    moved = [[delayed(signals[b], j) for j in range(taps)] for b in range(3)]
    mixed = []
    for b in range(3):
        value = weight[b][0] * moved[b][0]
        for j in range(1, taps):
            value = value + weight[b][j] * moved[b][j]
        mixed.append(value)
    query, key_part, value = mixed
    product = key_part * value
    dw = grad * query
    (pr, pi), (dr, di) = spectrum([product, dw])

    def inverse(spectra):
        rc, rs, ic, is_ = transform(
            jnp.concatenate([re for re, _ in spectra], axis=0),
            jnp.concatenate([im for _, im in spectra], axis=0),
        )
        re, im = rc - is_, ic + rs
        results = []
        for i in range(len(spectra)):
            blocks = []
            for ch in range(per):
                start = (i * per + ch) * parts
                cr, ci = re[start : start + parts], im[start : start + parts]
                both = jnp.concatenate([cr * cosine - ci * sine, ci * cosine + cr * sine], axis=0)
                high, low = split(both)
                blocks.append(dot(last_ref[...], jnp.concatenate([high, low, high], axis=0)))
            results.append(jnp.concatenate(blocks, axis=0))
        return results

    conv_out, dz = inverse(
        [(fr * pr - fi * pi, fr * pi + fi * pr), (dr * fr + di * fi, di * fr - dr * fi)]
    )
    conv_out = conv_out + direct * product
    dz = dz + direct * dw
    grads = [grad * conv_out, dz * value, dz * key_part]
    for b in range(3):
        result = weight[b][0] * grads[b]
        for j in range(1, taps):
            result = result + weight[b][j] * advanced(grads[b], j)
        for ch in range(per):
            block = result[ch * parts : (ch + 1) * parts]
            for h in (0, 1):
                start = b * parts * 2 * per + h * per + ch
                stage[pl.ds(start, parts, stride=2 * per), :] = block[:, h * half : (h + 1) * half]
        for s in range(parts):
            for h in (0, 1):
                start = (b * parts + s) * 2 * per + h * per
                gsend[s, b, h] = stage[start : start + per, :]
    near = 8 // per
    landing = grecv.at[:, me // near, :, me % near]
    pltpu.make_async_copy(gsend.at[me], landing, sems.at[7]).start()
    for i in range(parts - 1, 0, -1):
        peer = partner(me, i)
        push(gsend.at[peer], landing, 6, peer, group).start()

    (corr,) = inverse([(dr * pr + di * pi, di * pr - dr * pi)])
    corr = corr * (total * groups) ** (-0.5)
    for ch in range(per):
        block = corr[ch * parts : (ch + 1) * parts]
        fstage[pl.ds(2 * ch, parts, stride=2 * per), :] = block[:, :half]
        fstage[pl.ds(2 * ch + 1, parts, stride=2 * per), :] = block[:, half:]
    for s in range(parts):
        fsend[s] = fstage[2 * per * s : 2 * per * (s + 1), :]

    scale = total ** (-0.5)
    sums = [grads[b] * moved[b][j] for b in range(3) for j in range(taps)] + [dw * product]
    spot = lax.broadcasted_iota(jnp.int32, (1, half), 1)
    line = jnp.zeros((1, half), jnp.float32)
    for k, array in enumerate(sums):
        folded = array[:, :half] + array[:, half:]
        for ch in range(per):
            block = jnp.sum(folded[ch * parts : (ch + 1) * parts], axis=0, keepdims=True)
            amount = jnp.sum(block, axis=1, keepdims=True) * scale
            line = jnp.where(spot == k * per + per * me + ch, amount, line)
    ssend[...] = line

    slot = group * share + me % share
    for i in range(parts - 1, -1, -1):
        peer = partner(me, i)
        remote = push(fsend.at[peer], frecv.at[slot], 4, peer, target)
        if i:
            remote.start()
        else:

            @pl.when(target != group)
            def _():
                remote.start()

            @pl.when(target == group)
            def _():
                pltpu.make_async_copy(fsend.at[me], frecv.at[slot], sems.at[5]).start()

    pltpu.make_async_copy(ssend, srecv.at[me], sems.at[9]).start()
    for i in range(parts - 1, 0, -1):
        push(ssend, srecv.at[me], 8, partner(me, i), group).start()

    wait_blocks(frecv, parts, sems.at[5])
    pltpu.make_async_copy(grecv, grecv, sems.at[7]).wait()
    wait_blocks(srecv, parts, sems.at[9])
    wait_blocks(send, parts - 1, sems.at[0])
    wait_blocks(filt_send, parts - 1, sems.at[2])
    wait_blocks(fsend, parts - 1, sems.at[4])

    @pl.when(target != group)
    def _():
        wait_blocks(fsend, 1, sems.at[4])

    wait_blocks(gsend, parts - 1, sems.at[6])
    wait_blocks(srecv, parts - 1, sems.at[8])


def unpack_kernel(
    groups, parts, grecv, frecv_hbm, srecv_hbm, ig_hbm, fg_hbm, skg_hbm, sg_hbm,
    frecv, srecv, fg_ref, skg_ref, sg_ref, sems,
):
    taps, channels = sg_ref.shape[1:]
    half = grecv.shape[-1]
    per = channels // parts
    share = channels // groups
    copies = []

    def copy(src, dst):
        made = pltpu.make_async_copy(src, dst, sems.at[len(copies)])
        made.start()
        copies.append(made)
        return made

    loads = [copy(frecv_hbm, frecv), copy(srecv_hbm, srecv)]
    for b in range(3):
        for h in (0, 1):
            copy(grecv.at[b, :, h], ig_hbm.at[b, :, :, pl.ds(h * half, half)])
    loads[0].wait()
    for h in (0, 1):
        both = frecv[pl.ds(h, share, stride=2), :]
        for j in range(1, groups):
            both = both + frecv[pl.ds(2 * share * j + h, share, stride=2), :]
        fg_ref[:, h * half : (h + 1) * half] = both
    copy(fg_ref, fg_hbm)
    loads[1].wait()
    sums = srecv[...]
    row = lax.broadcasted_iota(jnp.int32, sums.shape, 0)
    lane = lax.broadcasted_iota(jnp.int32, sums.shape, 1)
    for k in range(3 * taps + 1):
        first = (row + k) * per
        mine = (lane >= first) & (lane < first + per)
        line = jnp.sum(jnp.where(mine, sums, 0.0), axis=0, keepdims=True)
        piece = line[:, k * per : k * per + channels]
        if k < 3 * taps:
            sg_ref[k // taps, pl.ds(k % taps, 1), :] = piece
        else:
            skg_ref[...] = piece
    copy(skg_ref, skg_hbm)
    copy(sg_ref, sg_hbm)
    for made in copies[2:]:
        made.wait()


def owner_body(inputs, short_weights, filters, skip, grad_out):
    parts = lax.axis_size("seq")
    groups = lax.axis_size("chan")
    taps = short_weights.shape[1]
    channels, span = grad_out.shape
    per = channels // parts
    half = span // 2
    wide, twiddle, first, last = (jnp.asarray(t) for t in tables(parts, span))
    vmem = pl.BlockSpec(memory_space=pltpu.VMEM)
    hbm = pl.BlockSpec(memory_space=pltpu.HBM)
    f32 = jnp.float32
    operands = (
        inputs, grad_out, filters, short_weights, skip, wide, twiddle, first, last
    )
    limit = 60 * 1024 * 1024
    landing = (
        jax.ShapeDtypeStruct((3, channels // 8, 2, 8 // per, per, half), f32),
        jax.ShapeDtypeStruct((parts, 2 * per, half), f32),
        jax.ShapeDtypeStruct((parts, 1, half), f32),
    )
    blocks, filter_blocks, sums = pl.pallas_call(
        functools.partial(kernel, parts, groups),
        out_shape=landing,
        in_specs=[hbm] * 9,
        out_specs=(hbm,) * 3,
        scratch_shapes=[
            pltpu.VMEM(inputs.shape, inputs.dtype),
            pltpu.VMEM(grad_out.shape, grad_out.dtype),
            pltpu.VMEM(filters.shape, filters.dtype),
            pltpu.SMEM(short_weights.shape, f32),
            pltpu.SMEM(skip.shape, f32),
            pltpu.VMEM(wide.shape, wide.dtype),
            pltpu.VMEM(twiddle.shape, twiddle.dtype),
            pltpu.VMEM(first.shape, first.dtype),
            pltpu.VMEM(last.shape, last.dtype),
            pltpu.VMEM((8 * channels, half), f32),
            pltpu.VMEM((parts, 8 * per, half), jnp.bfloat16),
            pltpu.VMEM((parts, 8 * per, half), jnp.bfloat16),
            pltpu.VMEM((parts, 2 * per, half), f32),
            pltpu.VMEM((parts, 2 * per, half), f32),
            pltpu.VMEM((parts, 3, 2, per, half), f32),
            pltpu.VMEM((parts, 2 * per, half), f32),
            pltpu.VMEM((1, half), f32),
            pltpu.VMEM((2 * channels, half), f32),
            pltpu.SemaphoreType.DMA((10,)),
            pltpu.SemaphoreType.DMA((9,)),
        ],
        compiler_params=pltpu.CompilerParams(
            collective_id=0, has_side_effects=True, vmem_limit_bytes=limit
        ),
        name="owner_convolutions",
    )(*operands)
    shapes = (
        jax.ShapeDtypeStruct((3, channels // 8, 8, span), f32),
        jax.ShapeDtypeStruct((channels // groups, span), f32),
        jax.ShapeDtypeStruct((1, channels), f32),
        jax.ShapeDtypeStruct((3, taps, channels), f32),
    )
    in_grads, filter_grad, skip_grad, short_grad = pl.pallas_call(
        functools.partial(unpack_kernel, groups, parts),
        out_shape=shapes,
        in_specs=[hbm] * 3,
        out_specs=(hbm,) * 4,
        scratch_shapes=[
            pltpu.VMEM((2 * channels, half), f32),
            pltpu.VMEM((parts, half), f32),
            *[pltpu.VMEM(s.shape, f32) for s in shapes[1:]],
            pltpu.SemaphoreType.DMA((11,)),
        ],
        compiler_params=pltpu.CompilerParams(vmem_limit_bytes=limit),
        name="unpack_results",
    )(
        blocks.reshape(3, channels // 8, 2, 8, half),
        filter_blocks.reshape(2 * channels, half),
        sums.reshape(parts, half),
    )
    in_grads = in_grads.reshape(3, channels, span)
    return in_grads, filter_grad, skip_grad.reshape(channels), short_grad


def body(inputs, short_weights, filters, skip, grad_out):
    parts = lax.axis_size("seq")
    groups = lax.axis_size("chan")
    channels, span = grad_out.shape
    fits = (
        channels == 2 * parts
        and filters.shape[0] == channels
        and span == 256
        and parts == 16
        and parts % groups == 0
        and short_weights.shape[1] <= 4
    )
    chosen = owner_body if fits else spectral_body
    return chosen(inputs, short_weights, filters, skip, grad_out)


def solution(mesh):
    placed = (
        P(None, "chan", "seq"),
        P(None, None, "chan"),
        P(None, "seq"),
        P("chan"),
        P("chan", "seq"),
    )
    return jax.shard_map(
        body,
        mesh=mesh,
        in_specs=placed,
        out_specs=(P(None, "chan", "seq"), P("chan", "seq"), P("chan"), P(None, None, "chan")),
        check_vma=False,
    )
```

```python
import functools
import math

import jax
import jax.numpy as jnp
import numpy as np
from jax import lax
from jax.experimental import pallas as pl
from jax.experimental.pallas import tpu as pltpu
from jax.sharding import PartitionSpec as P

highest = lax.Precision.HIGHEST


def shifted(block, axis, distance):
    devices = range(lax.axis_size(axis))
    route = [(i - distance, i) for i in devices if i - distance in devices]
    return lax.ppermute(block, axis, route)


def angle_table(rows, cols, period, sign):
    grid = (
        jnp.arange(rows, dtype=jnp.int32)[:, None]
        * jnp.arange(cols, dtype=jnp.int32)[None, :]
        % period
    )
    angle = sign * 2.0 * math.pi / period * grid.astype(jnp.float32)
    return (jnp.cos(angle), jnp.sin(angle))


def rotate(real_part, imag_part, cosine, sine):
    return (real_part * cosine - imag_part * sine, real_part * sine + imag_part * cosine)


def transform_last(real_part, imag_part, sign):
    length = real_part.shape[-1]
    if length <= 128 or length % 64 != 0:
        cosine, sine = angle_table(length, length, length, sign)
        new_real = jnp.dot(real_part, cosine, precision=highest) - jnp.dot(
            imag_part, sine, precision=highest
        )
        new_imag = jnp.dot(real_part, sine, precision=highest) + jnp.dot(
            imag_part, cosine, precision=highest
        )
        return (new_real, new_imag)
    outer = 64
    inner = length // outer
    leading = real_part.shape[:-1]
    real_part = jnp.swapaxes(real_part.reshape(leading + (inner, outer)), -1, -2)
    imag_part = jnp.swapaxes(imag_part.reshape(leading + (inner, outer)), -1, -2)
    real_part, imag_part = transform_last(real_part, imag_part, sign)
    cosine, sine = angle_table(outer, inner, length, sign)
    real_part, imag_part = rotate(real_part, imag_part, cosine, sine)
    cosine, sine = angle_table(outer, outer, outer, sign)
    new_real = jnp.einsum("...jk,jl->...lk", real_part, cosine, precision=highest) - jnp.einsum(
        "...jk,jl->...lk", imag_part, sine, precision=highest
    )
    new_imag = jnp.einsum("...jk,jl->...lk", real_part, sine, precision=highest) + jnp.einsum(
        "...jk,jl->...lk", imag_part, cosine, precision=highest
    )
    return (new_real.reshape(leading + (length,)), new_imag.reshape(leading + (length,)))


def forward_spectrum(stacked):
    parts = lax.axis_size("seq")
    rank = lax.axis_index("seq")
    span = stacked.shape[2]
    width = span // parts
    period = 2 * span * parts
    rows = lax.all_to_all(stacked[:, :, None, :], "seq", split_axis=3, concat_axis=2, tiled=True)
    cosine, sine = angle_table(parts, 2 * parts, 2 * parts, -1.0)
    real_part = jnp.einsum("bcpm,pq->bcqm", rows, cosine, precision=highest)
    imag_part = jnp.einsum("bcpm,pq->bcqm", rows, sine, precision=highest)
    column = rank * width + jnp.arange(width, dtype=jnp.int32)
    grid = jnp.arange(2 * parts, dtype=jnp.int32)[:, None] * column[None, :] % period
    angle = -2.0 * math.pi / period * grid.astype(jnp.float32)
    real_part, imag_part = rotate(real_part, imag_part, jnp.cos(angle), jnp.sin(angle))
    real_part, imag_part = (
        lax.all_to_all(real_part, "seq", split_axis=2, concat_axis=3, tiled=True),
        lax.all_to_all(imag_part, "seq", split_axis=2, concat_axis=3, tiled=True),
    )
    return transform_last(real_part, imag_part, -1.0)


def inverse_start(real_part, imag_part):
    parts = lax.axis_size("seq")
    rank = lax.axis_index("seq")
    span = real_part.shape[3]
    period = 2 * span * parts
    real_part, imag_part = transform_last(real_part, imag_part, 1.0)
    residue = 2 * rank + jnp.arange(2, dtype=jnp.int32)
    grid = residue[:, None] * jnp.arange(span, dtype=jnp.int32)[None, :] % period
    angle = 2.0 * math.pi / period * grid.astype(jnp.float32)
    return rotate(real_part, imag_part, jnp.cos(angle), jnp.sin(angle))


def inverse_finish(real_part, imag_part, period):
    parts = lax.axis_size("seq")
    cosine, sine = angle_table(2 * parts, parts, 2 * parts, 1.0)
    new_real = jnp.einsum("bcqm,qp->bcpm", real_part, cosine, precision=highest) - jnp.einsum(
        "bcqm,qp->bcpm", imag_part, sine, precision=highest
    )
    new_imag = jnp.einsum("bcqm,qp->bcpm", real_part, sine, precision=highest) + jnp.einsum(
        "bcqm,qp->bcpm", imag_part, cosine, precision=highest
    )
    return (new_real * (1.0 / period), new_imag * (1.0 / period))


def spectral_body(inputs, short_weights, filters, skip, grad_out):
    taps = short_weights.shape[1]
    parts = lax.axis_size("seq")
    groups = lax.axis_size("chan")
    span = inputs.shape[2]
    channels = inputs.shape[1]
    total = span * parts
    period = 2 * total
    border = shifted(inputs[:, :, span - (taps - 1) :], "seq", 1)
    extended = jnp.concatenate([border, inputs], axis=2).astype(jnp.float32)
    mixed = short_weights[:, 0, :, None] * extended[:, :, taps - 1 : taps - 1 + span]
    for offset in range(1, taps):
        start = taps - 1 - offset
        mixed = mixed + short_weights[:, offset, :, None] * extended[:, :, start : start + span]
    query, key_part, value = (mixed[0], mixed[1], mixed[2])
    grad = grad_out.astype(jnp.float32)
    product = key_part * value
    dw = grad * query
    spec_real, spec_imag = forward_spectrum(jnp.stack([product, dw, filters]))
    prod_real, grad_real, filt_real = (spec_real[0], spec_real[1], spec_real[2])
    prod_imag, grad_imag, filt_imag = (spec_imag[0], spec_imag[1], spec_imag[2])
    conv_real = filt_real * prod_real - filt_imag * prod_imag
    conv_imag = filt_real * prod_imag + filt_imag * prod_real
    back_real = grad_real * filt_real + grad_imag * filt_imag
    back_imag = grad_imag * filt_real - grad_real * filt_imag
    corr_real = grad_real * prod_real + grad_imag * prod_imag
    corr_imag = grad_imag * prod_real - grad_real * prod_imag
    start_real, start_imag = inverse_start(
        jnp.stack([conv_real, back_real, corr_real]), jnp.stack([conv_imag, back_imag, corr_imag])
    )
    start_real, start_imag = (
        lax.all_to_all(start_real, "seq", split_axis=3, concat_axis=2, tiled=True),
        lax.all_to_all(start_imag, "seq", split_axis=3, concat_axis=2, tiled=True),
    )
    result, unused = inverse_finish(start_real, start_imag, period)
    fields = lax.all_to_all(result, "seq", split_axis=2, concat_axis=3, tiled=True).reshape(
        3, channels, span
    )
    conv_out = fields[0] + skip[:, None] * product
    dz = fields[1] + skip[:, None] * dw
    filter_grad = lax.psum_scatter(
        fields[2] * (total * groups) ** (-0.5), "chan", scatter_dimension=0, tiled=True
    )
    grads = jnp.stack([grad * conv_out, dz * value, dz * key_part])
    after = shifted(grads[:, :, : taps - 1], "seq", -1)
    grad_ext = jnp.concatenate([grads, after], axis=2)
    in_grads = short_weights[:, 0, :, None] * grads
    for offset in range(1, taps):
        in_grads = (
            in_grads + short_weights[:, offset, :, None] * grad_ext[:, :, offset : offset + span]
        )
    short_rows = []
    for offset in range(taps):
        start = taps - 1 - offset
        short_rows.append(jnp.sum(grads * extended[:, :, start : start + span], axis=2))
    short_part = jnp.stack(short_rows, axis=1)
    skip_part = jnp.sum(dw * product, axis=1)
    short_sum, skip_sum = lax.psum((short_part, skip_part), "seq")
    scale = total ** (-0.5)
    return (in_grads, filter_grad, skip_sum * scale, short_sum * scale)


MESH = pl.DeviceIdType.MESH


def split(x):
    high = x.astype(jnp.bfloat16)
    return high, (x - high.astype(jnp.float32)).astype(jnp.bfloat16)


def split_table(table):
    table = np.asarray(table, np.float32)
    high = table.astype(jnp.bfloat16)
    return high, (table - high.astype(np.float32)).astype(jnp.bfloat16)


def tables(parts, span):
    period = 2 * parts * span
    u = np.arange(span)
    angle = 2.0 * np.pi / span * (u[:, None] * u[None, :] % span)
    wide = np.concatenate([np.cos(angle), np.sin(angle)], axis=1)
    wide = np.stack(split_table(wide))
    k = np.arange(parts) + 0.5
    angle = 2.0 * np.pi / period * k[:, None] * u[None, :]
    twiddle = np.stack([np.cos(angle), np.sin(angle)]).astype(np.float32)
    angle = np.pi / parts * k[:, None] * np.arange(parts)[None, :]
    high, low = split_table(np.concatenate([np.cos(angle), -np.sin(angle)], axis=0))
    first = np.concatenate([high, high, low], axis=1)
    last = np.concatenate([np.cos(angle).T, -np.sin(angle).T], axis=1) * (2.0 / period)
    high, low = split_table(last)
    last = np.concatenate([high, high, low], axis=1)
    return wide, twiddle, first, last


def partner(me, i):
    peer = me
    bit = 1
    while bit <= i:
        if i & bit:
            peer = peer + bit * (1 - 2 * (me // bit % 2))
        bit *= 2
    return peer


def dot(a, b):
    return jnp.dot(a, b, preferred_element_type=jnp.float32)


def kernel(
    parts, groups, x_hbm, g_hbm, f_hbm, sw_hbm, sk_hbm, wide_hbm, tw_hbm, first_hbm, last_hbm,
    grecv, frecv, srecv,
    x_ref, g_ref, f_ref, sw_ref, sk_ref, wide, tw_ref, first_ref, last_ref,
    stage, send, recv, filt_send, filt_recv, gsend, fsend, ssend, fstage, sems, load_sems,
):
    taps = sw_ref.shape[1]
    channels, span = f_ref.shape
    half = span // 2
    per = channels // parts
    rows = per * parts
    total = parts * span
    me = lax.axis_index("seq")
    group = lax.axis_index("chan")
    share = parts // groups
    target = me // share

    pairs = [
        (x_hbm, x_ref), (g_hbm, g_ref), (f_hbm, f_ref), (sw_hbm, sw_ref), (sk_hbm, sk_ref),
        (tw_hbm, tw_ref), (first_hbm, first_ref), (last_hbm, last_ref), (wide_hbm, wide),
    ]
    loads = [
        pltpu.make_async_copy(src, dst, load_sems.at[n]) for n, (src, dst) in enumerate(pairs)
    ]
    for load in loads[:3]:
        load.start()

    def greet(seq, chan):
        pl.semaphore_signal(
            barrier, inc=1, device_id={"seq": seq, "chan": chan}, device_id_type=MESH
        )

    barrier = pltpu.get_barrier_semaphore()
    for i in range(parts - 1, 0, -1):
        greet(partner(me, i), group)
    for j in range(1, groups):
        for i in range(share):
            greet(group * share + i, (group + j) % groups)
    for load in loads[3:]:
        load.start()
    for load in loads[:3]:
        load.wait()

    for a, piece in enumerate([x_ref[0], x_ref[1], x_ref[2], g_ref[...]]):
        piece = piece.astype(jnp.float32)
        for h in (0, 1):
            stage[pl.ds(2 * a + h, channels, stride=8), :] = piece[:, h * half : (h + 1) * half]
    send[...] = stage[...].astype(jnp.bfloat16).reshape(send.shape)
    for h in (0, 1):
        fstage[pl.ds(h, channels, stride=2), :] = f_ref[:, h * half : (h + 1) * half]
    for s in range(parts):
        filt_send[s] = fstage[2 * per * s : 2 * per * (s + 1), :]
    recv[pl.ds(me, 1)] = send[pl.ds(me, 1)]
    filt_recv[pl.ds(me, 1)] = filt_send[pl.ds(me, 1)]

    def push(src, dst, n, peer, chan):
        return pltpu.make_async_remote_copy(
            src_ref=src, dst_ref=dst, send_sem=sems.at[n], recv_sem=sems.at[n + 1],
            device_id={"seq": peer, "chan": chan}, device_id_type=MESH,
        )

    @pl.when(target == group)
    def _():
        pl.semaphore_wait(barrier, parts - 1)

    @pl.when(target != group)
    def _():
        pl.semaphore_wait(barrier, 2 * parts - 1)

    for i in range(parts - 1, 0, -1):
        peer = partner(me, i)
        push(filt_send.at[peer], filt_recv.at[me], 2, peer, group).start()
    for i in range(parts - 1, 0, -1):
        peer = partner(me, i)
        push(send.at[peer], recv.at[me], 0, peer, group).start()

    def wait_blocks(ref, count, sem):
        part = ref.at[pl.ds(0, count)]
        pltpu.make_async_copy(part, part, sem).wait()

    def received(ref, count, a):
        blocks = []
        for ch in range(per):
            blocks.append(
                jnp.concatenate(
                    [
                        ref[pl.ds(count * ch + 2 * a + h, parts, stride=count * per), :]
                        for h in (0, 1)
                    ],
                    axis=1,
                )
            )
        return jnp.concatenate(blocks, axis=0)

    row = lax.broadcasted_iota(jnp.int32, (rows, span), 0)
    lane = lax.broadcasted_iota(jnp.int32, (rows, span), 1)

    def delayed(x, j):
        if j == 0:
            return x
        y = pltpu.roll(x, j, 1)
        z = jnp.where(row % parts == 0, 0.0, pltpu.roll(y, 1, 0))
        return jnp.where(lane < j, z, y)

    def advanced(x, j):
        if j == 0:
            return x
        y = pltpu.roll(x, span - j, 1)
        z = jnp.where(row % parts == parts - 1, 0.0, pltpu.roll(y, rows - 1, 0))
        return jnp.where(lane >= span - j, z, y)

    def per_channel(values):
        result = jnp.full((rows, span), values[0], jnp.float32)
        for ch in range(1, per):
            result = jnp.where(row >= ch * parts, values[ch], result)
        return result

    for load in loads[3:5]:
        load.wait()
    weight = [
        [per_channel([sw_ref[b, j, per * me + ch] for ch in range(per)]) for j in range(taps)]
        for b in range(3)
    ]
    direct = per_channel([sk_ref[per * me + ch] for ch in range(per)])

    for load in loads[5:]:
        load.wait()
    cosine, sine = tw_ref[0], tw_ref[1]

    def transform(re, im):
        both = jnp.concatenate([re, im], axis=0)
        size = both.shape[0]
        high, low = split(both)
        result = dot(jnp.concatenate([high, low], axis=0), wide[0])
        result = result[:size] + result[size:] + dot(high, wide[1])
        count = size // 2
        return (
            result[:count, :span], result[:count, span:],
            result[count:, :span], result[count:, span:],
        )

    def spectrum(signals):
        reals, imags = [], []
        for signal in signals:
            for ch in range(per):
                high, low = split(signal[ch * parts : (ch + 1) * parts])
                spec = dot(first_ref[...], jnp.concatenate([high, low, high], axis=0))
                re, im = spec[:parts], spec[parts:]
                reals.append(re * cosine + im * sine)
                imags.append(im * cosine - re * sine)
        rc, rs, ic, is_ = transform(jnp.concatenate(reals, axis=0), jnp.concatenate(imags, axis=0))
        re, im = rc + is_, ic - rs
        return [
            (re[i * rows : (i + 1) * rows], im[i * rows : (i + 1) * rows])
            for i in range(len(signals))
        ]

    wait_blocks(filt_recv, parts - 1, sems.at[3])
    for s in range(parts):
        fstage[2 * per * s : 2 * per * (s + 1), :] = filt_recv[s]
    ((fr, fi),) = spectrum([received(fstage, 2, 0)])

    wait_blocks(recv, parts - 1, sems.at[1])
    stage[...] = recv[...].astype(jnp.float32).reshape(stage.shape)
    signals = [received(stage, 8, a) for a in range(4)]
    grad = signals[3]
    moved = [[delayed(signals[b], j) for j in range(taps)] for b in range(3)]
    mixed = []
    for b in range(3):
        value = weight[b][0] * moved[b][0]
        for j in range(1, taps):
            value = value + weight[b][j] * moved[b][j]
        mixed.append(value)
    query, key_part, value = mixed
    product = key_part * value
    dw = grad * query
    (pr, pi), (dr, di) = spectrum([product, dw])

    def inverse(spectra):
        rc, rs, ic, is_ = transform(
            jnp.concatenate([re for re, _ in spectra], axis=0),
            jnp.concatenate([im for _, im in spectra], axis=0),
        )
        re, im = rc - is_, ic + rs
        results = []
        for i in range(len(spectra)):
            blocks = []
            for ch in range(per):
                start = (i * per + ch) * parts
                cr, ci = re[start : start + parts], im[start : start + parts]
                both = jnp.concatenate([cr * cosine - ci * sine, ci * cosine + cr * sine], axis=0)
                high, low = split(both)
                blocks.append(dot(last_ref[...], jnp.concatenate([high, low, high], axis=0)))
            results.append(jnp.concatenate(blocks, axis=0))
        return results

    conv_out, dz = inverse(
        [(fr * pr - fi * pi, fr * pi + fi * pr), (dr * fr + di * fi, di * fr - dr * fi)]
    )
    conv_out = conv_out + direct * product
    dz = dz + direct * dw
    grads = [grad * conv_out, dz * value, dz * key_part]
    for b in range(3):
        result = weight[b][0] * grads[b]
        for j in range(1, taps):
            result = result + weight[b][j] * advanced(grads[b], j)
        for ch in range(per):
            block = result[ch * parts : (ch + 1) * parts]
            for h in (0, 1):
                start = b * parts * 2 * per + 2 * ch + h
                stage[pl.ds(start, parts, stride=2 * per), :] = block[:, h * half : (h + 1) * half]
        for s in range(parts):
            start = (b * parts + s) * 2 * per
            gsend[b, s] = stage[start : start + 2 * per, :]
    pltpu.make_async_copy(gsend.at[:, me], grecv.at[:, me], sems.at[7]).start()
    for i in range(parts - 1, 0, -1):
        peer = partner(me, i)
        push(gsend.at[:, peer], grecv.at[:, me], 6, peer, group).start()

    (corr,) = inverse([(dr * pr + di * pi, di * pr - dr * pi)])
    corr = corr * (total * groups) ** (-0.5)
    for ch in range(per):
        block = corr[ch * parts : (ch + 1) * parts]
        fstage[pl.ds(2 * ch, parts, stride=2 * per), :] = block[:, :half]
        fstage[pl.ds(2 * ch + 1, parts, stride=2 * per), :] = block[:, half:]
    for s in range(parts):
        fsend[s] = fstage[2 * per * s : 2 * per * (s + 1), :]

    scale = total ** (-0.5)
    sums = [grads[b] * moved[b][j] for b in range(3) for j in range(taps)] + [dw * product]
    spot = lax.broadcasted_iota(jnp.int32, (1, half), 1)
    line = jnp.zeros((1, half), jnp.float32)
    for k, array in enumerate(sums):
        folded = array[:, :half] + array[:, half:]
        for ch in range(per):
            block = jnp.sum(folded[ch * parts : (ch + 1) * parts], axis=0, keepdims=True)
            amount = jnp.sum(block, axis=1, keepdims=True) * scale
            line = jnp.where(spot == k * per + per * me + ch, amount, line)
    ssend[...] = line

    slot = group * share + me % share
    for i in range(parts - 1, -1, -1):
        peer = partner(me, i)
        remote = push(fsend.at[peer], frecv.at[slot], 4, peer, target)
        if i:
            remote.start()
        else:

            @pl.when(target != group)
            def _():
                remote.start()

            @pl.when(target == group)
            def _():
                pltpu.make_async_copy(fsend.at[me], frecv.at[slot], sems.at[5]).start()

    pltpu.make_async_copy(ssend, srecv.at[me], sems.at[9]).start()
    for i in range(parts - 1, 0, -1):
        push(ssend, srecv.at[me], 8, partner(me, i), group).start()

    wait_blocks(frecv, parts, sems.at[5])
    pltpu.make_async_copy(grecv, grecv, sems.at[7]).wait()
    wait_blocks(srecv, parts, sems.at[9])
    wait_blocks(send, parts - 1, sems.at[0])
    wait_blocks(filt_send, parts - 1, sems.at[2])
    wait_blocks(fsend, parts - 1, sems.at[4])

    @pl.when(target != group)
    def _():
        wait_blocks(fsend, 1, sems.at[4])

    part = gsend.at[:, pl.ds(0, parts - 1)]
    pltpu.make_async_copy(part, part, sems.at[6]).wait()
    wait_blocks(srecv, parts - 1, sems.at[8])


def unpack_kernel(
    groups, parts, grecv, frecv, srecv, ig_hbm, fg_hbm, skg_hbm, sg_hbm,
    ig_ref, fg_ref, skg_ref, sg_ref, sems,
):
    taps, channels = sg_ref.shape[1:]
    half = grecv.shape[1]
    per = channels // parts
    share = channels // groups

    def save(n, src, dst):
        copy = pltpu.make_async_copy(src, dst, sems.at[n])
        copy.start()
        return copy

    for b in range(3):
        for h in (0, 1):
            ig_ref[b, :, h * half : (h + 1) * half] = grecv[
                pl.ds(b * 2 * channels + h, channels, stride=2), :
            ]
    saves = [save(0, ig_ref, ig_hbm)]
    for h in (0, 1):
        both = frecv[pl.ds(h, share, stride=2), :]
        for j in range(1, groups):
            both = both + frecv[pl.ds(2 * share * j + h, share, stride=2), :]
        fg_ref[:, h * half : (h + 1) * half] = both
    saves.append(save(1, fg_ref, fg_hbm))
    sums = srecv[...]
    row = lax.broadcasted_iota(jnp.int32, sums.shape, 0)
    lane = lax.broadcasted_iota(jnp.int32, sums.shape, 1)
    for k in range(3 * taps + 1):
        first = (row + k) * per
        mine = (lane >= first) & (lane < first + per)
        line = jnp.sum(jnp.where(mine, sums, 0.0), axis=0, keepdims=True)
        piece = line[:, k * per : k * per + channels]
        if k < 3 * taps:
            sg_ref[k // taps, pl.ds(k % taps, 1), :] = piece
        else:
            skg_ref[...] = piece
    saves += [save(2, skg_ref, skg_hbm), save(3, sg_ref, sg_hbm)]
    for copy in saves:
        copy.wait()


def owner_body(inputs, short_weights, filters, skip, grad_out):
    parts = lax.axis_size("seq")
    groups = lax.axis_size("chan")
    taps = short_weights.shape[1]
    channels, span = grad_out.shape
    per = channels // parts
    half = span // 2
    wide, twiddle, first, last = (jnp.asarray(t) for t in tables(parts, span))
    vmem = pl.BlockSpec(memory_space=pltpu.VMEM)
    hbm = pl.BlockSpec(memory_space=pltpu.HBM)
    f32 = jnp.float32
    operands = (
        inputs, grad_out, filters, short_weights, skip, wide, twiddle, first, last
    )
    limit = 60 * 1024 * 1024
    landing = (
        jax.ShapeDtypeStruct((3, parts, 2 * per, half), f32),
        jax.ShapeDtypeStruct((parts, 2 * per, half), f32),
        jax.ShapeDtypeStruct((parts, 1, half), f32),
    )
    blocks, filter_blocks, sums = pl.pallas_call(
        functools.partial(kernel, parts, groups),
        out_shape=landing,
        in_specs=[hbm] * 9,
        out_specs=(hbm,) * 3,
        scratch_shapes=[
            pltpu.VMEM(inputs.shape, inputs.dtype),
            pltpu.VMEM(grad_out.shape, grad_out.dtype),
            pltpu.VMEM(filters.shape, filters.dtype),
            pltpu.SMEM(short_weights.shape, f32),
            pltpu.SMEM(skip.shape, f32),
            pltpu.VMEM(wide.shape, wide.dtype),
            pltpu.VMEM(twiddle.shape, twiddle.dtype),
            pltpu.VMEM(first.shape, first.dtype),
            pltpu.VMEM(last.shape, last.dtype),
            pltpu.VMEM((8 * channels, half), f32),
            pltpu.VMEM((parts, 8 * per, half), jnp.bfloat16),
            pltpu.VMEM((parts, 8 * per, half), jnp.bfloat16),
            pltpu.VMEM((parts, 2 * per, half), f32),
            pltpu.VMEM((parts, 2 * per, half), f32),
            pltpu.VMEM((3, parts, 2 * per, half), f32),
            pltpu.VMEM((parts, 2 * per, half), f32),
            pltpu.VMEM((1, half), f32),
            pltpu.VMEM((2 * channels, half), f32),
            pltpu.SemaphoreType.DMA((10,)),
            pltpu.SemaphoreType.DMA((9,)),
        ],
        compiler_params=pltpu.CompilerParams(
            collective_id=0, has_side_effects=True, vmem_limit_bytes=limit
        ),
        name="owner_convolutions",
    )(*operands)
    shapes = (
        jax.ShapeDtypeStruct((3, channels, span), f32),
        jax.ShapeDtypeStruct((channels // groups, span), f32),
        jax.ShapeDtypeStruct((1, channels), f32),
        jax.ShapeDtypeStruct((3, taps, channels), f32),
    )
    in_grads, filter_grad, skip_grad, short_grad = pl.pallas_call(
        functools.partial(unpack_kernel, groups, parts),
        out_shape=shapes,
        in_specs=[vmem] * 3,
        out_specs=(hbm,) * 4,
        scratch_shapes=[
            *[pltpu.VMEM(s.shape, f32) for s in shapes],
            pltpu.SemaphoreType.DMA((4,)),
        ],
        compiler_params=pltpu.CompilerParams(vmem_limit_bytes=limit),
        name="unpack_results",
    )(
        blocks.reshape(6 * channels, half),
        filter_blocks.reshape(2 * channels, half),
        sums.reshape(parts, half),
    )
    return in_grads, filter_grad, skip_grad.reshape(channels), short_grad


def body(inputs, short_weights, filters, skip, grad_out):
    parts = lax.axis_size("seq")
    groups = lax.axis_size("chan")
    channels, span = grad_out.shape
    fits = (
        channels == 2 * parts
        and filters.shape[0] == channels
        and span == 256
        and parts == 16
        and parts % groups == 0
        and short_weights.shape[1] <= 4
    )
    chosen = owner_body if fits else spectral_body
    return chosen(inputs, short_weights, filters, skip, grad_out)


def solution(mesh):
    placed = (
        P(None, "chan", "seq"),
        P(None, None, "chan"),
        P(None, "seq"),
        P("chan"),
        P("chan", "seq"),
    )
    return jax.shard_map(
        body,
        mesh=mesh,
        in_specs=placed,
        out_specs=(P(None, "chan", "seq"), P("chan", "seq"), P("chan"), P(None, None, "chan")),
        check_vma=False,
    )
```

```python
import functools
import math

import jax
import jax.numpy as jnp
import numpy as np
from jax import lax
from jax.experimental import pallas as pl
from jax.experimental.pallas import tpu as pltpu
from jax.sharding import PartitionSpec as P

highest = lax.Precision.HIGHEST


def shifted(block, axis, distance):
    devices = range(lax.axis_size(axis))
    route = [(i - distance, i) for i in devices if i - distance in devices]
    return lax.ppermute(block, axis, route)


def angle_table(rows, cols, period, sign):
    grid = (
        jnp.arange(rows, dtype=jnp.int32)[:, None]
        * jnp.arange(cols, dtype=jnp.int32)[None, :]
        % period
    )
    angle = sign * 2.0 * math.pi / period * grid.astype(jnp.float32)
    return (jnp.cos(angle), jnp.sin(angle))


def rotate(real_part, imag_part, cosine, sine):
    return (real_part * cosine - imag_part * sine, real_part * sine + imag_part * cosine)


def transform_last(real_part, imag_part, sign):
    length = real_part.shape[-1]
    if length <= 128 or length % 64 != 0:
        cosine, sine = angle_table(length, length, length, sign)
        new_real = jnp.dot(real_part, cosine, precision=highest) - jnp.dot(
            imag_part, sine, precision=highest
        )
        new_imag = jnp.dot(real_part, sine, precision=highest) + jnp.dot(
            imag_part, cosine, precision=highest
        )
        return (new_real, new_imag)
    outer = 64
    inner = length // outer
    leading = real_part.shape[:-1]
    real_part = jnp.swapaxes(real_part.reshape(leading + (inner, outer)), -1, -2)
    imag_part = jnp.swapaxes(imag_part.reshape(leading + (inner, outer)), -1, -2)
    real_part, imag_part = transform_last(real_part, imag_part, sign)
    cosine, sine = angle_table(outer, inner, length, sign)
    real_part, imag_part = rotate(real_part, imag_part, cosine, sine)
    cosine, sine = angle_table(outer, outer, outer, sign)
    new_real = jnp.einsum("...jk,jl->...lk", real_part, cosine, precision=highest) - jnp.einsum(
        "...jk,jl->...lk", imag_part, sine, precision=highest
    )
    new_imag = jnp.einsum("...jk,jl->...lk", real_part, sine, precision=highest) + jnp.einsum(
        "...jk,jl->...lk", imag_part, cosine, precision=highest
    )
    return (new_real.reshape(leading + (length,)), new_imag.reshape(leading + (length,)))


def forward_spectrum(stacked):
    parts = lax.axis_size("seq")
    rank = lax.axis_index("seq")
    span = stacked.shape[2]
    width = span // parts
    period = 2 * span * parts
    rows = lax.all_to_all(stacked[:, :, None, :], "seq", split_axis=3, concat_axis=2, tiled=True)
    cosine, sine = angle_table(parts, 2 * parts, 2 * parts, -1.0)
    real_part = jnp.einsum("bcpm,pq->bcqm", rows, cosine, precision=highest)
    imag_part = jnp.einsum("bcpm,pq->bcqm", rows, sine, precision=highest)
    column = rank * width + jnp.arange(width, dtype=jnp.int32)
    grid = jnp.arange(2 * parts, dtype=jnp.int32)[:, None] * column[None, :] % period
    angle = -2.0 * math.pi / period * grid.astype(jnp.float32)
    real_part, imag_part = rotate(real_part, imag_part, jnp.cos(angle), jnp.sin(angle))
    real_part, imag_part = (
        lax.all_to_all(real_part, "seq", split_axis=2, concat_axis=3, tiled=True),
        lax.all_to_all(imag_part, "seq", split_axis=2, concat_axis=3, tiled=True),
    )
    return transform_last(real_part, imag_part, -1.0)


def inverse_start(real_part, imag_part):
    parts = lax.axis_size("seq")
    rank = lax.axis_index("seq")
    span = real_part.shape[3]
    period = 2 * span * parts
    real_part, imag_part = transform_last(real_part, imag_part, 1.0)
    residue = 2 * rank + jnp.arange(2, dtype=jnp.int32)
    grid = residue[:, None] * jnp.arange(span, dtype=jnp.int32)[None, :] % period
    angle = 2.0 * math.pi / period * grid.astype(jnp.float32)
    return rotate(real_part, imag_part, jnp.cos(angle), jnp.sin(angle))


def inverse_finish(real_part, imag_part, period):
    parts = lax.axis_size("seq")
    cosine, sine = angle_table(2 * parts, parts, 2 * parts, 1.0)
    new_real = jnp.einsum("bcqm,qp->bcpm", real_part, cosine, precision=highest) - jnp.einsum(
        "bcqm,qp->bcpm", imag_part, sine, precision=highest
    )
    new_imag = jnp.einsum("bcqm,qp->bcpm", real_part, sine, precision=highest) + jnp.einsum(
        "bcqm,qp->bcpm", imag_part, cosine, precision=highest
    )
    return (new_real * (1.0 / period), new_imag * (1.0 / period))


def spectral_body(inputs, short_weights, filters, skip, grad_out):
    taps = short_weights.shape[1]
    parts = lax.axis_size("seq")
    groups = lax.axis_size("chan")
    span = inputs.shape[2]
    channels = inputs.shape[1]
    total = span * parts
    period = 2 * total
    border = shifted(inputs[:, :, span - (taps - 1) :], "seq", 1)
    extended = jnp.concatenate([border, inputs], axis=2).astype(jnp.float32)
    mixed = short_weights[:, 0, :, None] * extended[:, :, taps - 1 : taps - 1 + span]
    for offset in range(1, taps):
        start = taps - 1 - offset
        mixed = mixed + short_weights[:, offset, :, None] * extended[:, :, start : start + span]
    query, key_part, value = (mixed[0], mixed[1], mixed[2])
    grad = grad_out.astype(jnp.float32)
    product = key_part * value
    dw = grad * query
    spec_real, spec_imag = forward_spectrum(jnp.stack([product, dw, filters]))
    prod_real, grad_real, filt_real = (spec_real[0], spec_real[1], spec_real[2])
    prod_imag, grad_imag, filt_imag = (spec_imag[0], spec_imag[1], spec_imag[2])
    conv_real = filt_real * prod_real - filt_imag * prod_imag
    conv_imag = filt_real * prod_imag + filt_imag * prod_real
    back_real = grad_real * filt_real + grad_imag * filt_imag
    back_imag = grad_imag * filt_real - grad_real * filt_imag
    corr_real = grad_real * prod_real + grad_imag * prod_imag
    corr_imag = grad_imag * prod_real - grad_real * prod_imag
    start_real, start_imag = inverse_start(
        jnp.stack([conv_real, back_real, corr_real]), jnp.stack([conv_imag, back_imag, corr_imag])
    )
    start_real, start_imag = (
        lax.all_to_all(start_real, "seq", split_axis=3, concat_axis=2, tiled=True),
        lax.all_to_all(start_imag, "seq", split_axis=3, concat_axis=2, tiled=True),
    )
    result, unused = inverse_finish(start_real, start_imag, period)
    fields = lax.all_to_all(result, "seq", split_axis=2, concat_axis=3, tiled=True).reshape(
        3, channels, span
    )
    conv_out = fields[0] + skip[:, None] * product
    dz = fields[1] + skip[:, None] * dw
    filter_grad = lax.psum_scatter(
        fields[2] * (total * groups) ** (-0.5), "chan", scatter_dimension=0, tiled=True
    )
    grads = jnp.stack([grad * conv_out, dz * value, dz * key_part])
    after = shifted(grads[:, :, : taps - 1], "seq", -1)
    grad_ext = jnp.concatenate([grads, after], axis=2)
    in_grads = short_weights[:, 0, :, None] * grads
    for offset in range(1, taps):
        in_grads = (
            in_grads + short_weights[:, offset, :, None] * grad_ext[:, :, offset : offset + span]
        )
    short_rows = []
    for offset in range(taps):
        start = taps - 1 - offset
        short_rows.append(jnp.sum(grads * extended[:, :, start : start + span], axis=2))
    short_part = jnp.stack(short_rows, axis=1)
    skip_part = jnp.sum(dw * product, axis=1)
    short_sum, skip_sum = lax.psum((short_part, skip_part), "seq")
    scale = total ** (-0.5)
    return (in_grads, filter_grad, skip_sum * scale, short_sum * scale)


MESH = pl.DeviceIdType.MESH


def split(x):
    high = x.astype(jnp.bfloat16)
    return high, (x - high.astype(jnp.float32)).astype(jnp.bfloat16)


def split_table(table):
    table = np.asarray(table, np.float32)
    high = table.astype(jnp.bfloat16)
    return high, (table - high.astype(np.float32)).astype(jnp.bfloat16)


def tables(parts, span):
    period = 2 * parts * span
    u = np.arange(span)
    angle = 2.0 * np.pi / span * (u[:, None] * u[None, :] % span)
    wide = np.concatenate([np.cos(angle), np.sin(angle)], axis=1)
    wide = np.stack(split_table(wide))
    k = np.arange(parts) + 0.5
    angle = 2.0 * np.pi / period * k[:, None] * u[None, :]
    twiddle = np.stack([np.cos(angle), np.sin(angle)]).astype(np.float32)
    angle = np.pi / parts * k[:, None] * np.arange(parts)[None, :]
    high, low = split_table(np.concatenate([np.cos(angle), -np.sin(angle)], axis=0))
    first = np.concatenate([high, high, low], axis=1)
    last = np.concatenate([np.cos(angle).T, -np.sin(angle).T], axis=1) * (2.0 / period)
    high, low = split_table(last)
    last = np.concatenate([high, high, low], axis=1)
    return wide, twiddle, first, last


def partner(me, i):
    peer = me
    bit = 1
    while bit <= i:
        if i & bit:
            peer = peer + bit * (1 - 2 * (me // bit % 2))
        bit *= 2
    return peer


def dot(a, b):
    return jnp.dot(a, b, preferred_element_type=jnp.float32)


def kernel(
    parts, groups, x_hbm, g_hbm, f_hbm, sw_hbm, sk_hbm, wide_hbm, tw_hbm, first_hbm, last_hbm,
    grecv, frecv,
    x_ref, g_ref, f_ref, sw_ref, sk_ref, wide, tw_ref, first_ref, last_ref,
    stage, send, recv, gsend, fsend, fstage, sems, load_sems,
):
    taps = sw_ref.shape[1]
    channels, span = f_ref.shape
    half = span // 2
    per = channels // parts
    rows = per * parts
    total = parts * span
    me = lax.axis_index("seq")
    group = lax.axis_index("chan")
    share = parts // groups
    target = me // share

    pairs = [
        (x_hbm, x_ref), (g_hbm, g_ref), (f_hbm, f_ref), (sw_hbm, sw_ref), (sk_hbm, sk_ref),
        (tw_hbm, tw_ref), (first_hbm, first_ref), (last_hbm, last_ref), (wide_hbm, wide),
    ]
    loads = [
        pltpu.make_async_copy(src, dst, load_sems.at[n]) for n, (src, dst) in enumerate(pairs)
    ]
    for load in loads[:3]:
        load.start()

    def greet(seq, chan):
        pl.semaphore_signal(
            barrier, inc=1, device_id={"seq": seq, "chan": chan}, device_id_type=MESH
        )

    barrier = pltpu.get_barrier_semaphore()
    for i in range(parts - 1, 0, -1):
        greet(partner(me, i), group)
    for j in range(1, groups):
        for i in range(share):
            greet(group * share + i, (group + j) % groups)
    for load in loads[3:]:
        load.start()
    for load in loads[:3]:
        load.wait()

    for a, piece in enumerate([x_ref[0], x_ref[1], x_ref[2], g_ref[...]]):
        piece = piece.astype(jnp.float32)
        for h in (0, 1):
            stage[pl.ds(2 * a + h, channels, stride=8), :] = piece[:, h * half : (h + 1) * half]
    for n, piece in enumerate(split(f_ref[...])):
        piece = piece.astype(jnp.float32)
        for h in (0, 1):
            start = 2 * n + h
            fstage[pl.ds(start, channels, stride=4), :] = piece[:, h * half : (h + 1) * half]
    send[:, :per] = stage[...].reshape(parts, per, 8, half).astype(jnp.bfloat16)
    send[:, per:] = fstage[...].reshape(parts, per // 2, 8, half).astype(jnp.bfloat16)
    recv[pl.ds(me, 1)] = send[pl.ds(me, 1)]

    def push(src, dst, n, peer, chan):
        return pltpu.make_async_remote_copy(
            src_ref=src, dst_ref=dst, send_sem=sems.at[n], recv_sem=sems.at[n + 1],
            device_id={"seq": peer, "chan": chan}, device_id_type=MESH,
        )

    @pl.when(target == group)
    def _():
        pl.semaphore_wait(barrier, parts - 1)

    @pl.when(target != group)
    def _():
        pl.semaphore_wait(barrier, 2 * parts - 1)

    for i in range(parts - 1, 0, -1):
        peer = partner(me, i)
        push(send.at[peer], recv.at[me], 0, peer, group).start()

    def wait_blocks(ref, count, sem):
        part = ref.at[pl.ds(0, count)]
        pltpu.make_async_copy(part, part, sem).wait()

    def received(ref, count, a):
        blocks = []
        for ch in range(per):
            blocks.append(
                jnp.concatenate(
                    [
                        ref[pl.ds(count * ch + 2 * a + h, parts, stride=count * per), :]
                        for h in (0, 1)
                    ],
                    axis=1,
                )
            )
        return jnp.concatenate(blocks, axis=0)

    row = lax.broadcasted_iota(jnp.int32, (rows, span), 0)
    lane = lax.broadcasted_iota(jnp.int32, (rows, span), 1)

    def delayed(x, j):
        if j == 0:
            return x
        y = pltpu.roll(x, j, 1)
        z = jnp.where(row % parts == 0, 0.0, pltpu.roll(y, 1, 0))
        return jnp.where(lane < j, z, y)

    def advanced(x, j):
        if j == 0:
            return x
        y = pltpu.roll(x, span - j, 1)
        z = jnp.where(row % parts == parts - 1, 0.0, pltpu.roll(y, rows - 1, 0))
        return jnp.where(lane >= span - j, z, y)

    def per_channel(values):
        result = jnp.full((rows, span), values[0], jnp.float32)
        for ch in range(1, per):
            result = jnp.where(row >= ch * parts, values[ch], result)
        return result

    for load in loads[3:5]:
        load.wait()
    weight = [
        [per_channel([sw_ref[b, j, per * me + ch] for ch in range(per)]) for j in range(taps)]
        for b in range(3)
    ]
    direct = per_channel([sk_ref[per * me + ch] for ch in range(per)])

    for load in loads[5:]:
        load.wait()
    wait_blocks(recv, parts - 1, sems.at[1])
    stage[...] = recv[:, :per].astype(jnp.float32).reshape(stage.shape)
    fstage[...] = recv[:, per:].astype(jnp.float32).reshape(fstage.shape)
    signals = [received(stage, 8, a) for a in range(4)]
    filt = received(fstage, 4, 0) + received(fstage, 4, 1)
    grad = signals[3]
    moved = [[delayed(signals[b], j) for j in range(taps)] for b in range(3)]
    mixed = []
    for b in range(3):
        value = weight[b][0] * moved[b][0]
        for j in range(1, taps):
            value = value + weight[b][j] * moved[b][j]
        mixed.append(value)
    query, key_part, value = mixed
    product = key_part * value
    dw = grad * query

    cosine, sine = tw_ref[0], tw_ref[1]
    reals, imags = [], []
    for signal in (product, dw, filt):
        for ch in range(per):
            high, low = split(signal[ch * parts : (ch + 1) * parts])
            spec = dot(first_ref[...], jnp.concatenate([high, low, high], axis=0))
            re, im = spec[:parts], spec[parts:]
            reals.append(re * cosine + im * sine)
            imags.append(im * cosine - re * sine)

    def transform(re, im):
        both = jnp.concatenate([re, im], axis=0)
        size = both.shape[0]
        high, low = split(both)
        result = dot(jnp.concatenate([high, low], axis=0), wide[0])
        result = result[:size] + result[size:] + dot(high, wide[1])
        count = size // 2
        return (
            result[:count, :span], result[:count, span:],
            result[count:, :span], result[count:, span:],
        )

    rc, rs, ic, is_ = transform(jnp.concatenate(reals, axis=0), jnp.concatenate(imags, axis=0))
    re, im = rc + is_, ic - rs
    pr, dr, fr = (re[i * rows : (i + 1) * rows] for i in range(3))
    pi, di, fi = (im[i * rows : (i + 1) * rows] for i in range(3))
    out_r = jnp.concatenate([dr * pr + di * pi, fr * pr - fi * pi, dr * fr + di * fi], axis=0)
    out_i = jnp.concatenate([di * pr - dr * pi, fr * pi + fi * pr, di * fr - dr * fi], axis=0)
    rc, rs, ic, is_ = transform(out_r, out_i)
    re, im = rc - is_, ic + rs

    def finish(i):
        blocks = []
        for ch in range(per):
            start = (i * per + ch) * parts
            cr, ci = re[start : start + parts], im[start : start + parts]
            both = jnp.concatenate([cr * cosine - ci * sine, ci * cosine + cr * sine], axis=0)
            high, low = split(both)
            blocks.append(dot(last_ref[...], jnp.concatenate([high, low, high], axis=0)))
        return jnp.concatenate(blocks, axis=0)

    corr = finish(0) * (total * groups) ** (-0.5)
    for ch in range(per):
        block = corr[ch * parts : (ch + 1) * parts]
        fstage[pl.ds(2 * ch, parts, stride=2 * per), :] = block[:, :half]
        fstage[pl.ds(2 * ch + 1, parts, stride=2 * per), :] = block[:, half:]
    for s in range(parts):
        fsend[s] = fstage[2 * per * s : 2 * per * (s + 1), :]
    slot = group * share + me % share
    for i in range(parts - 1, -1, -1):
        peer = partner(me, i)
        remote = push(fsend.at[peer], frecv.at[slot], 4, peer, target)
        if i:
            remote.start()
        else:

            @pl.when(target != group)
            def _():
                remote.start()

            @pl.when(target == group)
            def _():
                pltpu.make_async_copy(fsend.at[me], frecv.at[slot], sems.at[5]).start()

    conv_out = finish(1) + direct * product
    dz = finish(2) + direct * dw
    grads = [grad * conv_out, dz * value, dz * key_part]
    for b in range(3):
        result = weight[b][0] * grads[b]
        for j in range(1, taps):
            result = result + weight[b][j] * advanced(grads[b], j)
        for ch in range(per):
            block = result[ch * parts : (ch + 1) * parts]
            for h in (0, 1):
                start = (2 * b + h) * channels + ch
                stage[pl.ds(start, parts, stride=per), :] = block[:, h * half : (h + 1) * half]
            if ch == per - 1:
                for n in (2 * b, 2 * b + 1):
                    for s in range(parts):
                        start = n * channels + s * per
                        gsend[s, n] = stage[start : start + per, :]

    scale = total ** (-0.5)
    sums = [grads[b] * moved[b][j] for b in range(3) for j in range(taps)] + [dw * product]
    spot = lax.broadcasted_iota(jnp.int32, (1, half), 1)
    line = jnp.zeros((1, half), jnp.float32)
    for k, array in enumerate(sums):
        folded = array[:, :half] + array[:, half:]
        for ch in range(per):
            block = jnp.sum(folded[ch * parts : (ch + 1) * parts], axis=0, keepdims=True)
            amount = jnp.sum(block, axis=1, keepdims=True) * scale
            line = jnp.where(spot == k * per + per * me + ch, amount, line)
    gsend[:, 6] = jnp.broadcast_to(line.reshape(1, 1, half), (parts, per, half))
    pltpu.make_async_copy(gsend.at[me], grecv.at[me], sems.at[7]).start()
    for i in range(parts - 1, 0, -1):
        peer = partner(me, i)
        push(gsend.at[peer], grecv.at[me], 6, peer, group).start()

    wait_blocks(frecv, parts, sems.at[5])
    pltpu.make_async_copy(grecv, grecv, sems.at[7]).wait()
    wait_blocks(send, parts - 1, sems.at[0])
    wait_blocks(fsend, parts - 1, sems.at[4])

    @pl.when(target != group)
    def _():
        wait_blocks(fsend, 1, sems.at[4])

    wait_blocks(gsend, parts - 1, sems.at[6])


def unpack_kernel(
    groups, parts, grecv, frecv, ig_hbm, fg_hbm, skg_hbm, sg_hbm,
    stage, ig_ref, fg_ref, skg_ref, sg_ref, sems,
):
    taps, channels = sg_ref.shape[1:]
    half = grecv.shape[1]
    per = channels // parts
    share = channels // groups

    def save(n, src, dst):
        copy = pltpu.make_async_copy(src, dst, sems.at[n])
        copy.start()
        return copy

    for b in range(3):
        for h in (0, 1):
            n = 2 * b + h
            for ch in range(per):
                stage[pl.ds(n * channels + ch, parts, stride=per), :] = grecv[
                    pl.ds(n * per + ch, parts, stride=7 * per), :
                ]
            ig_ref[b, :, h * half : (h + 1) * half] = stage[n * channels : (n + 1) * channels, :]
    saves = [save(0, ig_ref, ig_hbm)]
    for h in (0, 1):
        both = frecv[pl.ds(h, share, stride=2), :]
        for j in range(1, groups):
            both = both + frecv[pl.ds(2 * share * j + h, share, stride=2), :]
        fg_ref[:, h * half : (h + 1) * half] = both
    saves.append(save(1, fg_ref, fg_hbm))
    sums = grecv[pl.ds(6 * per, parts, stride=7 * per), :]
    row = lax.broadcasted_iota(jnp.int32, sums.shape, 0)
    lane = lax.broadcasted_iota(jnp.int32, sums.shape, 1)
    for k in range(3 * taps + 1):
        first = (row + k) * per
        mine = (lane >= first) & (lane < first + per)
        line = jnp.sum(jnp.where(mine, sums, 0.0), axis=0, keepdims=True)
        piece = line[:, k * per : k * per + channels]
        if k < 3 * taps:
            sg_ref[k // taps, pl.ds(k % taps, 1), :] = piece
        else:
            skg_ref[...] = piece
    saves += [save(2, skg_ref, skg_hbm), save(3, sg_ref, sg_hbm)]
    for copy in saves:
        copy.wait()


def owner_body(inputs, short_weights, filters, skip, grad_out):
    parts = lax.axis_size("seq")
    groups = lax.axis_size("chan")
    taps = short_weights.shape[1]
    channels, span = grad_out.shape
    per = channels // parts
    half = span // 2
    wide, twiddle, first, last = (jnp.asarray(t) for t in tables(parts, span))
    vmem = pl.BlockSpec(memory_space=pltpu.VMEM)
    hbm = pl.BlockSpec(memory_space=pltpu.HBM)
    f32 = jnp.float32
    operands = (
        inputs, grad_out, filters, short_weights, skip, wide, twiddle, first, last
    )
    limit = 60 * 1024 * 1024
    landing = (
        jax.ShapeDtypeStruct((parts, 7, per, half), f32),
        jax.ShapeDtypeStruct((parts, 2 * per, half), f32),
    )
    blocks, filter_blocks = pl.pallas_call(
        functools.partial(kernel, parts, groups),
        out_shape=landing,
        in_specs=[hbm] * 9,
        out_specs=(hbm,) * 2,
        scratch_shapes=[
            pltpu.VMEM(inputs.shape, inputs.dtype),
            pltpu.VMEM(grad_out.shape, grad_out.dtype),
            pltpu.VMEM(filters.shape, filters.dtype),
            pltpu.SMEM(short_weights.shape, f32),
            pltpu.SMEM(skip.shape, f32),
            pltpu.VMEM(wide.shape, wide.dtype),
            pltpu.VMEM(twiddle.shape, twiddle.dtype),
            pltpu.VMEM(first.shape, first.dtype),
            pltpu.VMEM(last.shape, last.dtype),
            pltpu.VMEM((8 * channels, half), f32),
            pltpu.VMEM((parts, per + per // 2, 8, half), jnp.bfloat16),
            pltpu.VMEM((parts, per + per // 2, 8, half), jnp.bfloat16),
            pltpu.VMEM((parts, 7, per, half), f32),
            pltpu.VMEM((parts, 2 * per, half), f32),
            pltpu.VMEM((4 * channels, half), f32),
            pltpu.SemaphoreType.DMA((10,)),
            pltpu.SemaphoreType.DMA((9,)),
        ],
        compiler_params=pltpu.CompilerParams(
            collective_id=0, has_side_effects=True, vmem_limit_bytes=limit
        ),
        name="owner_convolutions",
    )(*operands)
    shapes = (
        jax.ShapeDtypeStruct((3, channels, span), f32),
        jax.ShapeDtypeStruct((channels // groups, span), f32),
        jax.ShapeDtypeStruct((1, channels), f32),
        jax.ShapeDtypeStruct((3, taps, channels), f32),
    )
    in_grads, filter_grad, skip_grad, short_grad = pl.pallas_call(
        functools.partial(unpack_kernel, groups, parts),
        out_shape=shapes,
        in_specs=[vmem] * 2,
        out_specs=(hbm,) * 4,
        scratch_shapes=[
            pltpu.VMEM((6 * channels, half), f32),
            *[pltpu.VMEM(s.shape, f32) for s in shapes],
            pltpu.SemaphoreType.DMA((4,)),
        ],
        compiler_params=pltpu.CompilerParams(vmem_limit_bytes=limit),
        name="unpack_results",
    )(
        blocks.reshape(7 * channels, half), filter_blocks.reshape(2 * channels, half)
    )
    return in_grads, filter_grad, skip_grad.reshape(channels), short_grad


def body(inputs, short_weights, filters, skip, grad_out):
    parts = lax.axis_size("seq")
    groups = lax.axis_size("chan")
    channels, span = grad_out.shape
    fits = (
        channels == 2 * parts
        and filters.shape[0] == channels
        and span == 256
        and parts == 16
        and parts % groups == 0
        and short_weights.shape[1] <= 4
    )
    chosen = owner_body if fits else spectral_body
    return chosen(inputs, short_weights, filters, skip, grad_out)


def solution(mesh):
    placed = (
        P(None, "chan", "seq"),
        P(None, None, "chan"),
        P(None, "seq"),
        P("chan"),
        P("chan", "seq"),
    )
    return jax.shard_map(
        body,
        mesh=mesh,
        in_specs=placed,
        out_specs=(P(None, "chan", "seq"), P("chan", "seq"), P("chan"), P(None, None, "chan")),
        check_vma=False,
    )
```

```python
import functools
import math

import jax
import jax.numpy as jnp
import numpy as np
from jax import lax
from jax.experimental import pallas as pl
from jax.experimental.pallas import tpu as pltpu
from jax.sharding import PartitionSpec as P

highest = lax.Precision.HIGHEST


def shifted(block, axis, distance):
    devices = range(lax.axis_size(axis))
    route = [(i - distance, i) for i in devices if i - distance in devices]
    return lax.ppermute(block, axis, route)


def angle_table(rows, cols, period, sign):
    grid = (
        jnp.arange(rows, dtype=jnp.int32)[:, None]
        * jnp.arange(cols, dtype=jnp.int32)[None, :]
        % period
    )
    angle = sign * 2.0 * math.pi / period * grid.astype(jnp.float32)
    return (jnp.cos(angle), jnp.sin(angle))


def rotate(real_part, imag_part, cosine, sine):
    return (real_part * cosine - imag_part * sine, real_part * sine + imag_part * cosine)


def transform_last(real_part, imag_part, sign):
    length = real_part.shape[-1]
    if length <= 128 or length % 64 != 0:
        cosine, sine = angle_table(length, length, length, sign)
        new_real = jnp.dot(real_part, cosine, precision=highest) - jnp.dot(
            imag_part, sine, precision=highest
        )
        new_imag = jnp.dot(real_part, sine, precision=highest) + jnp.dot(
            imag_part, cosine, precision=highest
        )
        return (new_real, new_imag)
    outer = 64
    inner = length // outer
    leading = real_part.shape[:-1]
    real_part = jnp.swapaxes(real_part.reshape(leading + (inner, outer)), -1, -2)
    imag_part = jnp.swapaxes(imag_part.reshape(leading + (inner, outer)), -1, -2)
    real_part, imag_part = transform_last(real_part, imag_part, sign)
    cosine, sine = angle_table(outer, inner, length, sign)
    real_part, imag_part = rotate(real_part, imag_part, cosine, sine)
    cosine, sine = angle_table(outer, outer, outer, sign)
    new_real = jnp.einsum("...jk,jl->...lk", real_part, cosine, precision=highest) - jnp.einsum(
        "...jk,jl->...lk", imag_part, sine, precision=highest
    )
    new_imag = jnp.einsum("...jk,jl->...lk", real_part, sine, precision=highest) + jnp.einsum(
        "...jk,jl->...lk", imag_part, cosine, precision=highest
    )
    return (new_real.reshape(leading + (length,)), new_imag.reshape(leading + (length,)))


def forward_spectrum(stacked):
    parts = lax.axis_size("seq")
    rank = lax.axis_index("seq")
    span = stacked.shape[2]
    width = span // parts
    period = 2 * span * parts
    rows = lax.all_to_all(stacked[:, :, None, :], "seq", split_axis=3, concat_axis=2, tiled=True)
    cosine, sine = angle_table(parts, 2 * parts, 2 * parts, -1.0)
    real_part = jnp.einsum("bcpm,pq->bcqm", rows, cosine, precision=highest)
    imag_part = jnp.einsum("bcpm,pq->bcqm", rows, sine, precision=highest)
    column = rank * width + jnp.arange(width, dtype=jnp.int32)
    grid = jnp.arange(2 * parts, dtype=jnp.int32)[:, None] * column[None, :] % period
    angle = -2.0 * math.pi / period * grid.astype(jnp.float32)
    real_part, imag_part = rotate(real_part, imag_part, jnp.cos(angle), jnp.sin(angle))
    real_part, imag_part = (
        lax.all_to_all(real_part, "seq", split_axis=2, concat_axis=3, tiled=True),
        lax.all_to_all(imag_part, "seq", split_axis=2, concat_axis=3, tiled=True),
    )
    return transform_last(real_part, imag_part, -1.0)


def inverse_start(real_part, imag_part):
    parts = lax.axis_size("seq")
    rank = lax.axis_index("seq")
    span = real_part.shape[3]
    period = 2 * span * parts
    real_part, imag_part = transform_last(real_part, imag_part, 1.0)
    residue = 2 * rank + jnp.arange(2, dtype=jnp.int32)
    grid = residue[:, None] * jnp.arange(span, dtype=jnp.int32)[None, :] % period
    angle = 2.0 * math.pi / period * grid.astype(jnp.float32)
    return rotate(real_part, imag_part, jnp.cos(angle), jnp.sin(angle))


def inverse_finish(real_part, imag_part, period):
    parts = lax.axis_size("seq")
    cosine, sine = angle_table(2 * parts, parts, 2 * parts, 1.0)
    new_real = jnp.einsum("bcqm,qp->bcpm", real_part, cosine, precision=highest) - jnp.einsum(
        "bcqm,qp->bcpm", imag_part, sine, precision=highest
    )
    new_imag = jnp.einsum("bcqm,qp->bcpm", real_part, sine, precision=highest) + jnp.einsum(
        "bcqm,qp->bcpm", imag_part, cosine, precision=highest
    )
    return (new_real * (1.0 / period), new_imag * (1.0 / period))


def spectral_body(inputs, short_weights, filters, skip, grad_out):
    taps = short_weights.shape[1]
    parts = lax.axis_size("seq")
    groups = lax.axis_size("chan")
    span = inputs.shape[2]
    channels = inputs.shape[1]
    total = span * parts
    period = 2 * total
    border = shifted(inputs[:, :, span - (taps - 1) :], "seq", 1)
    extended = jnp.concatenate([border, inputs], axis=2).astype(jnp.float32)
    mixed = short_weights[:, 0, :, None] * extended[:, :, taps - 1 : taps - 1 + span]
    for offset in range(1, taps):
        start = taps - 1 - offset
        mixed = mixed + short_weights[:, offset, :, None] * extended[:, :, start : start + span]
    query, key_part, value = (mixed[0], mixed[1], mixed[2])
    grad = grad_out.astype(jnp.float32)
    product = key_part * value
    dw = grad * query
    spec_real, spec_imag = forward_spectrum(jnp.stack([product, dw, filters]))
    prod_real, grad_real, filt_real = (spec_real[0], spec_real[1], spec_real[2])
    prod_imag, grad_imag, filt_imag = (spec_imag[0], spec_imag[1], spec_imag[2])
    conv_real = filt_real * prod_real - filt_imag * prod_imag
    conv_imag = filt_real * prod_imag + filt_imag * prod_real
    back_real = grad_real * filt_real + grad_imag * filt_imag
    back_imag = grad_imag * filt_real - grad_real * filt_imag
    corr_real = grad_real * prod_real + grad_imag * prod_imag
    corr_imag = grad_imag * prod_real - grad_real * prod_imag
    start_real, start_imag = inverse_start(
        jnp.stack([conv_real, back_real, corr_real]), jnp.stack([conv_imag, back_imag, corr_imag])
    )
    start_real, start_imag = (
        lax.all_to_all(start_real, "seq", split_axis=3, concat_axis=2, tiled=True),
        lax.all_to_all(start_imag, "seq", split_axis=3, concat_axis=2, tiled=True),
    )
    result, unused = inverse_finish(start_real, start_imag, period)
    fields = lax.all_to_all(result, "seq", split_axis=2, concat_axis=3, tiled=True).reshape(
        3, channels, span
    )
    conv_out = fields[0] + skip[:, None] * product
    dz = fields[1] + skip[:, None] * dw
    filter_grad = lax.psum_scatter(
        fields[2] * (total * groups) ** (-0.5), "chan", scatter_dimension=0, tiled=True
    )
    grads = jnp.stack([grad * conv_out, dz * value, dz * key_part])
    after = shifted(grads[:, :, : taps - 1], "seq", -1)
    grad_ext = jnp.concatenate([grads, after], axis=2)
    in_grads = short_weights[:, 0, :, None] * grads
    for offset in range(1, taps):
        in_grads = (
            in_grads + short_weights[:, offset, :, None] * grad_ext[:, :, offset : offset + span]
        )
    short_rows = []
    for offset in range(taps):
        start = taps - 1 - offset
        short_rows.append(jnp.sum(grads * extended[:, :, start : start + span], axis=2))
    short_part = jnp.stack(short_rows, axis=1)
    skip_part = jnp.sum(dw * product, axis=1)
    short_sum, skip_sum = lax.psum((short_part, skip_part), "seq")
    scale = total ** (-0.5)
    return (in_grads, filter_grad, skip_sum * scale, short_sum * scale)


MESH = pl.DeviceIdType.MESH


def split(x):
    high = x.astype(jnp.bfloat16)
    return high, (x - high.astype(jnp.float32)).astype(jnp.bfloat16)


def split_table(table):
    table = np.asarray(table, np.float32)
    high = table.astype(jnp.bfloat16)
    return high, (table - high.astype(np.float32)).astype(jnp.bfloat16)


def tables(parts, span, count):
    period = 2 * parts * span
    u = np.arange(span)
    angle = 2.0 * np.pi / span * (u[:, None] * u[None, :] % span)
    high, low = split_table(np.concatenate([np.cos(angle), np.sin(angle)], axis=1))
    wide = np.concatenate([high, high, low], axis=0)
    k = np.arange(parts) + 0.5
    angle = 2.0 * np.pi / period * k[:, None] * u[None, :]
    twiddle = np.stack([np.tile(np.cos(angle), (count, 1)), np.tile(np.sin(angle), (count, 1))])
    angle = np.pi / parts * k[:, None] * np.arange(parts)[None, :]
    each = np.eye(count)
    cosine, sine = np.kron(each, np.cos(angle)), np.kron(each, np.sin(angle))
    high, low = split_table(np.concatenate([cosine, -sine], axis=0))
    first = np.concatenate([high, high, low], axis=1)
    high, low = split_table(np.concatenate([cosine.T, -sine.T], axis=1) * (2.0 / period))
    last = np.concatenate([high, high, low], axis=1)
    return wide, twiddle.astype(np.float32), first, last


def partner(me, i):
    peer = me
    bit = 1
    while bit <= i:
        if i & bit:
            peer = peer + bit * (1 - 2 * (me // bit % 2))
        bit *= 2
    return peer


def dot(a, b):
    return jnp.dot(a, b, preferred_element_type=jnp.float32)


def kernel(
    parts, groups, x_hbm, g_hbm, f_hbm, sw_hbm, sk_hbm, wide_hbm, tw_hbm, first_hbm, last_hbm,
    grecv, frecv,
    x_ref, g_ref, f_ref, sw_ref, sk_ref, wide, tw_ref, first_ref, last_ref,
    stage, send, recv, gsend, fsend, fstage, sems, load_sems,
):
    taps = sw_ref.shape[1]
    channels, span = f_ref.shape
    half = span // 2
    per = channels // parts
    rows = per * parts
    total = parts * span
    me = lax.axis_index("seq")
    group = lax.axis_index("chan")
    share = parts // groups
    target = me // share

    pairs = [
        (x_hbm, x_ref), (g_hbm, g_ref), (f_hbm, f_ref), (sw_hbm, sw_ref), (sk_hbm, sk_ref),
        (tw_hbm, tw_ref), (first_hbm, first_ref), (last_hbm, last_ref), (wide_hbm, wide),
    ]
    loads = [
        pltpu.make_async_copy(src, dst, load_sems.at[n]) for n, (src, dst) in enumerate(pairs)
    ]
    for load in loads[:3]:
        load.start()

    def greet(seq, chan):
        pl.semaphore_signal(
            barrier, inc=1, device_id={"seq": seq, "chan": chan}, device_id_type=MESH
        )

    barrier = pltpu.get_barrier_semaphore()
    for i in range(parts - 1, 0, -1):
        greet(partner(me, i), group)
    for j in range(1, groups):
        for i in range(share):
            greet(group * share + i, (group + j) % groups)
    for load in loads[3:]:
        load.start()
    for load in loads[:3]:
        load.wait()

    for a, piece in enumerate([x_ref[0], x_ref[1], x_ref[2], g_ref[...]]):
        piece = piece.astype(jnp.float32)
        for h in (0, 1):
            stage[pl.ds(2 * a + h, channels, stride=8), :] = piece[:, h * half : (h + 1) * half]
    for n, piece in enumerate(split(f_ref[...])):
        piece = piece.astype(jnp.float32)
        for h in (0, 1):
            start = 2 * n + h
            fstage[pl.ds(start, channels, stride=4), :] = piece[:, h * half : (h + 1) * half]
    send[:, :per] = stage[...].reshape(parts, per, 8, half).astype(jnp.bfloat16)
    send[:, per:] = fstage[...].reshape(parts, per // 2, 8, half).astype(jnp.bfloat16)
    recv[pl.ds(me, 1)] = send[pl.ds(me, 1)]

    def push(src, dst, n, peer, chan):
        return pltpu.make_async_remote_copy(
            src_ref=src, dst_ref=dst, send_sem=sems.at[n], recv_sem=sems.at[n + 1],
            device_id={"seq": peer, "chan": chan}, device_id_type=MESH,
        )

    @pl.when(target == group)
    def _():
        pl.semaphore_wait(barrier, parts - 1)

    @pl.when(target != group)
    def _():
        pl.semaphore_wait(barrier, 2 * parts - 1)

    for i in range(parts - 1, 0, -1):
        peer = partner(me, i)
        push(send.at[peer], recv.at[me], 0, peer, group).start()

    def wait_blocks(ref, count, sem):
        part = ref.at[pl.ds(0, count)]
        pltpu.make_async_copy(part, part, sem).wait()

    def received(ref, count, a):
        blocks = []
        for ch in range(per):
            blocks.append(
                jnp.concatenate(
                    [
                        ref[pl.ds(count * ch + 2 * a + h, parts, stride=count * per), :]
                        for h in (0, 1)
                    ],
                    axis=1,
                )
            )
        return jnp.concatenate(blocks, axis=0)

    row = lax.broadcasted_iota(jnp.int32, (rows, span), 0)
    lane = lax.broadcasted_iota(jnp.int32, (rows, span), 1)

    def delayed(x, j):
        if j == 0:
            return x
        y = pltpu.roll(x, j, 1)
        z = jnp.where(row % parts == 0, 0.0, pltpu.roll(y, 1, 0))
        return jnp.where(lane < j, z, y)

    def advanced(x, j):
        if j == 0:
            return x
        y = pltpu.roll(x, span - j, 1)
        z = jnp.where(row % parts == parts - 1, 0.0, pltpu.roll(y, rows - 1, 0))
        return jnp.where(lane >= span - j, z, y)

    def per_channel(values):
        result = jnp.full((rows, span), values[0], jnp.float32)
        for ch in range(1, per):
            result = jnp.where(row >= ch * parts, values[ch], result)
        return result

    for load in loads[3:5]:
        load.wait()
    weight = [
        [per_channel([sw_ref[b, j, per * me + ch] for ch in range(per)]) for j in range(taps)]
        for b in range(3)
    ]
    direct = per_channel([sk_ref[per * me + ch] for ch in range(per)])

    for load in loads[5:]:
        load.wait()
    wait_blocks(recv, parts - 1, sems.at[1])
    stage[...] = recv[:, :per].astype(jnp.float32).reshape(stage.shape)
    fstage[...] = recv[:, per:].astype(jnp.float32).reshape(fstage.shape)
    signals = [received(stage, 8, a) for a in range(4)]
    filt = received(fstage, 4, 0) + received(fstage, 4, 1)
    grad = signals[3]
    moved = [[delayed(signals[b], j) for j in range(taps)] for b in range(3)]
    mixed = []
    for b in range(3):
        value = weight[b][0] * moved[b][0]
        for j in range(1, taps):
            value = value + weight[b][j] * moved[b][j]
        mixed.append(value)
    query, key_part, value = mixed
    product = key_part * value
    dw = grad * query

    cosine, sine = tw_ref[0], tw_ref[1]
    def transform(re, im):
        high, low = split(jnp.concatenate([re, im], axis=0))
        result = dot(jnp.concatenate([high, low, high], axis=1), wide[...])
        count = result.shape[0] // 2
        return (
            result[:count, :span], result[:count, span:],
            result[count:, :span], result[count:, span:],
        )

    high, low = split(jnp.concatenate([product, dw, filt], axis=0))
    spec = dot(first_ref[...], jnp.concatenate([high, low, high], axis=0))
    count = spec.shape[0] // 2
    re, im = spec[:count], spec[count:]
    rc, rs, ic, is_ = transform(re * cosine + im * sine, im * cosine - re * sine)
    re, im = rc + is_, ic - rs
    pr, dr, fr = (re[i * rows : (i + 1) * rows] for i in range(3))
    pi, di, fi = (im[i * rows : (i + 1) * rows] for i in range(3))
    out_r = jnp.concatenate([dr * pr + di * pi, fr * pr - fi * pi, dr * fr + di * fi], axis=0)
    out_i = jnp.concatenate([di * pr - dr * pi, fr * pi + fi * pr, di * fr - dr * fi], axis=0)
    rc, rs, ic, is_ = transform(out_r, out_i)
    re, im = rc - is_, ic + rs
    both = jnp.concatenate([re * cosine - im * sine, im * cosine + re * sine], axis=0)
    high, low = split(both)
    fields = dot(last_ref[...], jnp.concatenate([high, low, high], axis=0))

    corr = fields[:rows] * (total * groups) ** (-0.5)
    for ch in range(per):
        block = corr[ch * parts : (ch + 1) * parts]
        fstage[pl.ds(2 * ch, parts, stride=2 * per), :] = block[:, :half]
        fstage[pl.ds(2 * ch + 1, parts, stride=2 * per), :] = block[:, half:]
    for s in range(parts):
        fsend[s] = fstage[2 * per * s : 2 * per * (s + 1), :]
    slot = group * share + me % share
    for i in range(parts - 1, -1, -1):
        peer = partner(me, i)
        remote = push(fsend.at[peer], frecv.at[slot], 4, peer, target)
        if i:
            remote.start()
        else:

            @pl.when(target != group)
            def _():
                remote.start()

            @pl.when(target == group)
            def _():
                pltpu.make_async_copy(fsend.at[me], frecv.at[slot], sems.at[5]).start()

    conv_out = fields[rows : 2 * rows] + direct * product
    dz = fields[2 * rows :] + direct * dw
    grads = [grad * conv_out, dz * value, dz * key_part]
    for b in range(3):
        result = weight[b][0] * grads[b]
        for j in range(1, taps):
            result = result + weight[b][j] * advanced(grads[b], j)
        for ch in range(per):
            block = result[ch * parts : (ch + 1) * parts]
            for h in (0, 1):
                start = (2 * b + h) * channels + ch
                stage[pl.ds(start, parts, stride=per), :] = block[:, h * half : (h + 1) * half]
            if ch == per - 1:
                for n in (2 * b, 2 * b + 1):
                    for s in range(parts):
                        start = n * channels + s * per
                        gsend[s, n] = stage[start : start + per, :]

    scale = total ** (-0.5)
    sums = [grads[b] * moved[b][j] for b in range(3) for j in range(taps)] + [dw * product]
    spot = lax.broadcasted_iota(jnp.int32, (per * 16, half), 0)
    table = jnp.zeros((per * 16, half), jnp.float32)
    for k, array in enumerate(sums):
        folded = array[:, :half] + array[:, half:]
        for ch in range(per):
            block = jnp.sum(folded[ch * parts : (ch + 1) * parts], axis=0, keepdims=True)
            table = jnp.where(spot == k * per + ch, block, table)
    table = jnp.sum(table, axis=1, keepdims=True) * scale
    column = lax.broadcasted_iota(jnp.int32, (per * 16, half), 1)
    line = jnp.sum(jnp.where(column == spot + per * me, table, 0.0), axis=0, keepdims=True)
    gsend[:, 6] = jnp.broadcast_to(line.reshape(1, 1, half), (parts, per, half))
    pltpu.make_async_copy(gsend.at[me], grecv.at[me], sems.at[7]).start()
    for i in range(parts - 1, 0, -1):
        peer = partner(me, i)
        push(gsend.at[peer], grecv.at[me], 6, peer, group).start()

    wait_blocks(frecv, parts, sems.at[5])
    pltpu.make_async_copy(grecv, grecv, sems.at[7]).wait()
    wait_blocks(send, parts - 1, sems.at[0])
    wait_blocks(fsend, parts - 1, sems.at[4])

    @pl.when(target != group)
    def _():
        wait_blocks(fsend, 1, sems.at[4])

    wait_blocks(gsend, parts - 1, sems.at[6])


def unpack_kernel(
    groups, parts, grecv, frecv, ig_hbm, fg_hbm, skg_hbm, sg_hbm,
    stage, ig_ref, fg_ref, skg_ref, sg_ref, sems,
):
    taps, channels = sg_ref.shape[1:]
    half = grecv.shape[1]
    per = channels // parts
    share = channels // groups

    def save(n, src, dst):
        copy = pltpu.make_async_copy(src, dst, sems.at[n])
        copy.start()
        return copy

    for b in range(3):
        for h in (0, 1):
            n = 2 * b + h
            for ch in range(per):
                stage[pl.ds(n * channels + ch, parts, stride=per), :] = grecv[
                    pl.ds(n * per + ch, parts, stride=7 * per), :
                ]
            ig_ref[b, :, h * half : (h + 1) * half] = stage[n * channels : (n + 1) * channels, :]
    saves = [save(0, ig_ref, ig_hbm)]
    for h in (0, 1):
        both = frecv[pl.ds(h, share, stride=2), :]
        for j in range(1, groups):
            both = both + frecv[pl.ds(2 * share * j + h, share, stride=2), :]
        fg_ref[:, h * half : (h + 1) * half] = both
    saves.append(save(1, fg_ref, fg_hbm))
    sums = grecv[pl.ds(6 * per, parts, stride=7 * per), :]
    row = lax.broadcasted_iota(jnp.int32, sums.shape, 0)
    lane = lax.broadcasted_iota(jnp.int32, sums.shape, 1)
    for k in range(3 * taps + 1):
        first = (row + k) * per
        mine = (lane >= first) & (lane < first + per)
        line = jnp.sum(jnp.where(mine, sums, 0.0), axis=0, keepdims=True)
        piece = line[:, k * per : k * per + channels]
        if k < 3 * taps:
            sg_ref[k // taps, pl.ds(k % taps, 1), :] = piece
        else:
            skg_ref[...] = piece
    saves += [save(2, skg_ref, skg_hbm), save(3, sg_ref, sg_hbm)]
    for copy in saves:
        copy.wait()


def owner_body(inputs, short_weights, filters, skip, grad_out):
    parts = lax.axis_size("seq")
    groups = lax.axis_size("chan")
    taps = short_weights.shape[1]
    channels, span = grad_out.shape
    per = channels // parts
    half = span // 2
    wide, twiddle, first, last = (jnp.asarray(t) for t in tables(parts, span, 3 * per))
    vmem = pl.BlockSpec(memory_space=pltpu.VMEM)
    hbm = pl.BlockSpec(memory_space=pltpu.HBM)
    f32 = jnp.float32
    operands = (
        inputs, grad_out, filters, short_weights, skip, wide, twiddle, first, last
    )
    limit = 60 * 1024 * 1024
    landing = (
        jax.ShapeDtypeStruct((parts, 7, per, half), f32),
        jax.ShapeDtypeStruct((parts, 2 * per, half), f32),
    )
    blocks, filter_blocks = pl.pallas_call(
        functools.partial(kernel, parts, groups),
        out_shape=landing,
        in_specs=[hbm] * 9,
        out_specs=(hbm,) * 2,
        scratch_shapes=[
            pltpu.VMEM(inputs.shape, inputs.dtype),
            pltpu.VMEM(grad_out.shape, grad_out.dtype),
            pltpu.VMEM(filters.shape, filters.dtype),
            pltpu.SMEM(short_weights.shape, f32),
            pltpu.SMEM(skip.shape, f32),
            pltpu.VMEM(wide.shape, wide.dtype),
            pltpu.VMEM(twiddle.shape, twiddle.dtype),
            pltpu.VMEM(first.shape, first.dtype),
            pltpu.VMEM(last.shape, last.dtype),
            pltpu.VMEM((8 * channels, half), f32),
            pltpu.VMEM((parts, per + per // 2, 8, half), jnp.bfloat16),
            pltpu.VMEM((parts, per + per // 2, 8, half), jnp.bfloat16),
            pltpu.VMEM((parts, 7, per, half), f32),
            pltpu.VMEM((parts, 2 * per, half), f32),
            pltpu.VMEM((4 * channels, half), f32),
            pltpu.SemaphoreType.DMA((10,)),
            pltpu.SemaphoreType.DMA((9,)),
        ],
        compiler_params=pltpu.CompilerParams(
            collective_id=0, has_side_effects=True, vmem_limit_bytes=limit
        ),
        name="owner_convolutions",
    )(*operands)
    shapes = (
        jax.ShapeDtypeStruct((3, channels, span), f32),
        jax.ShapeDtypeStruct((channels // groups, span), f32),
        jax.ShapeDtypeStruct((1, channels), f32),
        jax.ShapeDtypeStruct((3, taps, channels), f32),
    )
    in_grads, filter_grad, skip_grad, short_grad = pl.pallas_call(
        functools.partial(unpack_kernel, groups, parts),
        out_shape=shapes,
        in_specs=[vmem] * 2,
        out_specs=(hbm,) * 4,
        scratch_shapes=[
            pltpu.VMEM((6 * channels, half), f32),
            *[pltpu.VMEM(s.shape, f32) for s in shapes],
            pltpu.SemaphoreType.DMA((4,)),
        ],
        compiler_params=pltpu.CompilerParams(vmem_limit_bytes=limit),
        name="unpack_results",
    )(
        blocks.reshape(7 * channels, half), filter_blocks.reshape(2 * channels, half)
    )
    return in_grads, filter_grad, skip_grad.reshape(channels), short_grad


def body(inputs, short_weights, filters, skip, grad_out):
    parts = lax.axis_size("seq")
    groups = lax.axis_size("chan")
    channels, span = grad_out.shape
    fits = (
        channels == 2 * parts
        and filters.shape[0] == channels
        and span == 256
        and parts == 16
        and parts % groups == 0
        and short_weights.shape[1] <= 4
    )
    chosen = owner_body if fits else spectral_body
    return chosen(inputs, short_weights, filters, skip, grad_out)


def solution(mesh):
    placed = (
        P(None, "chan", "seq"),
        P(None, None, "chan"),
        P(None, "seq"),
        P("chan"),
        P("chan", "seq"),
    )
    return jax.shard_map(
        body,
        mesh=mesh,
        in_specs=placed,
        out_specs=(P(None, "chan", "seq"), P("chan", "seq"), P("chan"), P(None, None, "chan")),
        check_vma=False,
    )
```

```python
import functools
import math

import jax
import jax.numpy as jnp
import numpy as np
from jax import lax
from jax.experimental import pallas as pl
from jax.experimental.pallas import tpu as pltpu
from jax.sharding import PartitionSpec as P

highest = lax.Precision.HIGHEST


def shifted(block, axis, distance):
    devices = range(lax.axis_size(axis))
    route = [(i - distance, i) for i in devices if i - distance in devices]
    return lax.ppermute(block, axis, route)


def angle_table(rows, cols, period, sign):
    grid = (
        jnp.arange(rows, dtype=jnp.int32)[:, None]
        * jnp.arange(cols, dtype=jnp.int32)[None, :]
        % period
    )
    angle = sign * 2.0 * math.pi / period * grid.astype(jnp.float32)
    return (jnp.cos(angle), jnp.sin(angle))


def rotate(real_part, imag_part, cosine, sine):
    return (real_part * cosine - imag_part * sine, real_part * sine + imag_part * cosine)


def transform_last(real_part, imag_part, sign):
    length = real_part.shape[-1]
    if length <= 128 or length % 64 != 0:
        cosine, sine = angle_table(length, length, length, sign)
        new_real = jnp.dot(real_part, cosine, precision=highest) - jnp.dot(
            imag_part, sine, precision=highest
        )
        new_imag = jnp.dot(real_part, sine, precision=highest) + jnp.dot(
            imag_part, cosine, precision=highest
        )
        return (new_real, new_imag)
    outer = 64
    inner = length // outer
    leading = real_part.shape[:-1]
    real_part = jnp.swapaxes(real_part.reshape(leading + (inner, outer)), -1, -2)
    imag_part = jnp.swapaxes(imag_part.reshape(leading + (inner, outer)), -1, -2)
    real_part, imag_part = transform_last(real_part, imag_part, sign)
    cosine, sine = angle_table(outer, inner, length, sign)
    real_part, imag_part = rotate(real_part, imag_part, cosine, sine)
    cosine, sine = angle_table(outer, outer, outer, sign)
    new_real = jnp.einsum("...jk,jl->...lk", real_part, cosine, precision=highest) - jnp.einsum(
        "...jk,jl->...lk", imag_part, sine, precision=highest
    )
    new_imag = jnp.einsum("...jk,jl->...lk", real_part, sine, precision=highest) + jnp.einsum(
        "...jk,jl->...lk", imag_part, cosine, precision=highest
    )
    return (new_real.reshape(leading + (length,)), new_imag.reshape(leading + (length,)))


def forward_spectrum(stacked):
    parts = lax.axis_size("seq")
    rank = lax.axis_index("seq")
    span = stacked.shape[2]
    width = span // parts
    period = 2 * span * parts
    rows = lax.all_to_all(stacked[:, :, None, :], "seq", split_axis=3, concat_axis=2, tiled=True)
    cosine, sine = angle_table(parts, 2 * parts, 2 * parts, -1.0)
    real_part = jnp.einsum("bcpm,pq->bcqm", rows, cosine, precision=highest)
    imag_part = jnp.einsum("bcpm,pq->bcqm", rows, sine, precision=highest)
    column = rank * width + jnp.arange(width, dtype=jnp.int32)
    grid = jnp.arange(2 * parts, dtype=jnp.int32)[:, None] * column[None, :] % period
    angle = -2.0 * math.pi / period * grid.astype(jnp.float32)
    real_part, imag_part = rotate(real_part, imag_part, jnp.cos(angle), jnp.sin(angle))
    real_part, imag_part = (
        lax.all_to_all(real_part, "seq", split_axis=2, concat_axis=3, tiled=True),
        lax.all_to_all(imag_part, "seq", split_axis=2, concat_axis=3, tiled=True),
    )
    return transform_last(real_part, imag_part, -1.0)


def inverse_start(real_part, imag_part):
    parts = lax.axis_size("seq")
    rank = lax.axis_index("seq")
    span = real_part.shape[3]
    period = 2 * span * parts
    real_part, imag_part = transform_last(real_part, imag_part, 1.0)
    residue = 2 * rank + jnp.arange(2, dtype=jnp.int32)
    grid = residue[:, None] * jnp.arange(span, dtype=jnp.int32)[None, :] % period
    angle = 2.0 * math.pi / period * grid.astype(jnp.float32)
    return rotate(real_part, imag_part, jnp.cos(angle), jnp.sin(angle))


def inverse_finish(real_part, imag_part, period):
    parts = lax.axis_size("seq")
    cosine, sine = angle_table(2 * parts, parts, 2 * parts, 1.0)
    new_real = jnp.einsum("bcqm,qp->bcpm", real_part, cosine, precision=highest) - jnp.einsum(
        "bcqm,qp->bcpm", imag_part, sine, precision=highest
    )
    new_imag = jnp.einsum("bcqm,qp->bcpm", real_part, sine, precision=highest) + jnp.einsum(
        "bcqm,qp->bcpm", imag_part, cosine, precision=highest
    )
    return (new_real * (1.0 / period), new_imag * (1.0 / period))


def spectral_body(inputs, short_weights, filters, skip, grad_out):
    taps = short_weights.shape[1]
    parts = lax.axis_size("seq")
    groups = lax.axis_size("chan")
    span = inputs.shape[2]
    channels = inputs.shape[1]
    total = span * parts
    period = 2 * total
    border = shifted(inputs[:, :, span - (taps - 1) :], "seq", 1)
    extended = jnp.concatenate([border, inputs], axis=2).astype(jnp.float32)
    mixed = short_weights[:, 0, :, None] * extended[:, :, taps - 1 : taps - 1 + span]
    for offset in range(1, taps):
        start = taps - 1 - offset
        mixed = mixed + short_weights[:, offset, :, None] * extended[:, :, start : start + span]
    query, key_part, value = (mixed[0], mixed[1], mixed[2])
    grad = grad_out.astype(jnp.float32)
    product = key_part * value
    dw = grad * query
    spec_real, spec_imag = forward_spectrum(jnp.stack([product, dw, filters]))
    prod_real, grad_real, filt_real = (spec_real[0], spec_real[1], spec_real[2])
    prod_imag, grad_imag, filt_imag = (spec_imag[0], spec_imag[1], spec_imag[2])
    conv_real = filt_real * prod_real - filt_imag * prod_imag
    conv_imag = filt_real * prod_imag + filt_imag * prod_real
    back_real = grad_real * filt_real + grad_imag * filt_imag
    back_imag = grad_imag * filt_real - grad_real * filt_imag
    corr_real = grad_real * prod_real + grad_imag * prod_imag
    corr_imag = grad_imag * prod_real - grad_real * prod_imag
    start_real, start_imag = inverse_start(
        jnp.stack([conv_real, back_real, corr_real]), jnp.stack([conv_imag, back_imag, corr_imag])
    )
    start_real, start_imag = (
        lax.all_to_all(start_real, "seq", split_axis=3, concat_axis=2, tiled=True),
        lax.all_to_all(start_imag, "seq", split_axis=3, concat_axis=2, tiled=True),
    )
    result, unused = inverse_finish(start_real, start_imag, period)
    fields = lax.all_to_all(result, "seq", split_axis=2, concat_axis=3, tiled=True).reshape(
        3, channels, span
    )
    conv_out = fields[0] + skip[:, None] * product
    dz = fields[1] + skip[:, None] * dw
    filter_grad = lax.psum_scatter(
        fields[2] * (total * groups) ** (-0.5), "chan", scatter_dimension=0, tiled=True
    )
    grads = jnp.stack([grad * conv_out, dz * value, dz * key_part])
    after = shifted(grads[:, :, : taps - 1], "seq", -1)
    grad_ext = jnp.concatenate([grads, after], axis=2)
    in_grads = short_weights[:, 0, :, None] * grads
    for offset in range(1, taps):
        in_grads = (
            in_grads + short_weights[:, offset, :, None] * grad_ext[:, :, offset : offset + span]
        )
    short_rows = []
    for offset in range(taps):
        start = taps - 1 - offset
        short_rows.append(jnp.sum(grads * extended[:, :, start : start + span], axis=2))
    short_part = jnp.stack(short_rows, axis=1)
    skip_part = jnp.sum(dw * product, axis=1)
    short_sum, skip_sum = lax.psum((short_part, skip_part), "seq")
    scale = total ** (-0.5)
    return (in_grads, filter_grad, skip_sum * scale, short_sum * scale)


MESH = pl.DeviceIdType.MESH


def split(x):
    high = x.astype(jnp.bfloat16)
    return high, (x - high.astype(jnp.float32)).astype(jnp.bfloat16)


def split_table(table):
    table = np.asarray(table, np.float32)
    high = table.astype(jnp.bfloat16)
    return high, (table - high.astype(np.float32)).astype(jnp.bfloat16)


def tables(parts, span):
    period = 2 * parts * span
    u = np.arange(span)
    angle = 2.0 * np.pi / span * (u[:, None] * u[None, :] % span)
    wide = np.concatenate([np.cos(angle), np.sin(angle)], axis=1)
    wide = np.stack(split_table(wide))
    k = np.arange(parts) + 0.5
    angle = 2.0 * np.pi / period * k[:, None] * u[None, :]
    twiddle = np.stack([np.cos(angle), np.sin(angle)]).astype(np.float32)
    angle = np.pi / parts * k[:, None] * np.arange(parts)[None, :]
    high, low = split_table(np.concatenate([np.cos(angle), -np.sin(angle)], axis=0))
    first = np.concatenate([high, high, low], axis=1)
    last = np.concatenate([np.cos(angle).T, -np.sin(angle).T], axis=1) * (2.0 / period)
    high, low = split_table(last)
    last = np.concatenate([high, high, low], axis=1)
    return wide, twiddle, first, last


def partner(me, i, parts):
    peer = me
    bit = 1
    while bit < parts:
        step = bit * (1 - 2 * lax.rem(lax.div(me, bit), 2))
        peer = peer + step * lax.rem(lax.div(i, bit), 2)
        bit *= 2
    return peer


def each_partner(me, parts, act):
    def step(n, carry):
        act(partner(me, parts - 1 - n, parts))
        return carry

    lax.fori_loop(0, parts - 1, step, 0)


def dot(a, b):
    return jnp.dot(a, b, preferred_element_type=jnp.float32)


def kernel(
    parts, groups, x_hbm, g_hbm, f_hbm, sw_hbm, sk_hbm, wide_hbm, tw_hbm, first_hbm, last_hbm,
    grecv, frecv,
    x_ref, g_ref, f_ref, sw_ref, sk_ref, wide, tw_ref, first_ref, last_ref,
    stage, send, recv, gsend, fsend, fstage, sems, load_sems,
):
    taps = sw_ref.shape[1]
    channels, span = f_ref.shape
    half = span // 2
    per = channels // parts
    rows = per * parts
    total = parts * span
    me = lax.axis_index("seq")
    group = lax.axis_index("chan")
    share = parts // groups
    target = me // share

    pairs = [
        (x_hbm, x_ref), (g_hbm, g_ref), (f_hbm, f_ref), (sw_hbm, sw_ref), (sk_hbm, sk_ref),
        (tw_hbm, tw_ref), (first_hbm, first_ref), (last_hbm, last_ref), (wide_hbm, wide),
    ]
    loads = [
        pltpu.make_async_copy(src, dst, load_sems.at[n]) for n, (src, dst) in enumerate(pairs)
    ]
    for load in loads[:3]:
        load.start()

    def greet(seq, chan):
        pl.semaphore_signal(
            barrier, inc=1, device_id={"seq": seq, "chan": chan}, device_id_type=MESH
        )

    barrier = pltpu.get_barrier_semaphore()
    each_partner(me, parts, lambda peer: greet(peer, group))
    for j in range(1, groups):

        def greet_other(i, carry, j=j):
            greet(group * share + i, lax.rem(group + j, groups))
            return carry

        lax.fori_loop(0, share, greet_other, 0)
    for load in loads[3:]:
        load.start()
    for load in loads[:3]:
        load.wait()

    for a, piece in enumerate([x_ref[0], x_ref[1], x_ref[2], g_ref[...]]):
        piece = piece.astype(jnp.float32)
        for h in (0, 1):
            stage[pl.ds(2 * a + h, channels, stride=8), :] = piece[:, h * half : (h + 1) * half]
    for n, piece in enumerate(split(f_ref[...])):
        piece = piece.astype(jnp.float32)
        for h in (0, 1):
            start = 2 * n + h
            fstage[pl.ds(start, channels, stride=4), :] = piece[:, h * half : (h + 1) * half]
    send[:, :per] = stage[...].reshape(parts, per, 8, half).astype(jnp.bfloat16)
    send[:, per:] = fstage[...].reshape(parts, per // 2, 8, half).astype(jnp.bfloat16)
    recv[pl.ds(me, 1)] = send[pl.ds(me, 1)]

    def push(src, dst, n, peer, chan):
        return pltpu.make_async_remote_copy(
            src_ref=src, dst_ref=dst, send_sem=sems.at[n], recv_sem=sems.at[n + 1],
            device_id={"seq": peer, "chan": chan}, device_id_type=MESH,
        )

    @pl.when(target == group)
    def _():
        pl.semaphore_wait(barrier, parts - 1)

    @pl.when(target != group)
    def _():
        pl.semaphore_wait(barrier, 2 * parts - 1)

    each_partner(
        me, parts, lambda peer: push(send.at[peer], recv.at[me], 0, peer, group).start()
    )

    def wait_blocks(ref, count, sem):
        part = ref.at[pl.ds(0, count)]
        pltpu.make_async_copy(part, part, sem).wait()

    def received(ref, count, a):
        blocks = []
        for ch in range(per):
            blocks.append(
                jnp.concatenate(
                    [
                        ref[pl.ds(count * ch + 2 * a + h, parts, stride=count * per), :]
                        for h in (0, 1)
                    ],
                    axis=1,
                )
            )
        return jnp.concatenate(blocks, axis=0)

    row = lax.broadcasted_iota(jnp.int32, (rows, span), 0)
    lane = lax.broadcasted_iota(jnp.int32, (rows, span), 1)

    def delayed(x, j):
        if j == 0:
            return x
        y = pltpu.roll(x, j, 1)
        z = jnp.where(row % parts == 0, 0.0, pltpu.roll(y, 1, 0))
        return jnp.where(lane < j, z, y)

    def advanced(x, j):
        if j == 0:
            return x
        y = pltpu.roll(x, span - j, 1)
        z = jnp.where(row % parts == parts - 1, 0.0, pltpu.roll(y, rows - 1, 0))
        return jnp.where(lane >= span - j, z, y)

    def per_channel(values):
        result = jnp.full((rows, span), values[0], jnp.float32)
        for ch in range(1, per):
            result = jnp.where(row >= ch * parts, values[ch], result)
        return result

    for load in loads[3:5]:
        load.wait()
    weight = [
        [per_channel([sw_ref[b, j, per * me + ch] for ch in range(per)]) for j in range(taps)]
        for b in range(3)
    ]
    direct = per_channel([sk_ref[per * me + ch] for ch in range(per)])

    for load in loads[5:]:
        load.wait()
    wait_blocks(recv, parts - 1, sems.at[1])
    stage[...] = recv[:, :per].astype(jnp.float32).reshape(stage.shape)
    fstage[...] = recv[:, per:].astype(jnp.float32).reshape(fstage.shape)
    signals = [received(stage, 8, a) for a in range(4)]
    filt = received(fstage, 4, 0) + received(fstage, 4, 1)
    grad = signals[3]
    moved = [[delayed(signals[b], j) for j in range(taps)] for b in range(3)]
    mixed = []
    for b in range(3):
        value = weight[b][0] * moved[b][0]
        for j in range(1, taps):
            value = value + weight[b][j] * moved[b][j]
        mixed.append(value)
    query, key_part, value = mixed
    product = key_part * value
    dw = grad * query

    cosine, sine = tw_ref[0], tw_ref[1]
    reals, imags = [], []
    for signal in (product, dw, filt):
        for ch in range(per):
            high, low = split(signal[ch * parts : (ch + 1) * parts])
            spec = dot(first_ref[...], jnp.concatenate([high, low, high], axis=0))
            re, im = spec[:parts], spec[parts:]
            reals.append(re * cosine + im * sine)
            imags.append(im * cosine - re * sine)

    def transform(re, im):
        both = jnp.concatenate([re, im], axis=0)
        size = both.shape[0]
        high, low = split(both)
        result = dot(jnp.concatenate([high, low], axis=0), wide[0])
        result = result[:size] + result[size:] + dot(high, wide[1])
        count = size // 2
        return (
            result[:count, :span], result[:count, span:],
            result[count:, :span], result[count:, span:],
        )

    rc, rs, ic, is_ = transform(jnp.concatenate(reals, axis=0), jnp.concatenate(imags, axis=0))
    re, im = rc + is_, ic - rs
    pr, dr, fr = (re[i * rows : (i + 1) * rows] for i in range(3))
    pi, di, fi = (im[i * rows : (i + 1) * rows] for i in range(3))
    out_r = jnp.concatenate([dr * pr + di * pi, fr * pr - fi * pi, dr * fr + di * fi], axis=0)
    out_i = jnp.concatenate([di * pr - dr * pi, fr * pi + fi * pr, di * fr - dr * fi], axis=0)
    rc, rs, ic, is_ = transform(out_r, out_i)
    re, im = rc - is_, ic + rs

    def finish(i):
        blocks = []
        for ch in range(per):
            start = (i * per + ch) * parts
            cr, ci = re[start : start + parts], im[start : start + parts]
            both = jnp.concatenate([cr * cosine - ci * sine, ci * cosine + cr * sine], axis=0)
            high, low = split(both)
            blocks.append(dot(last_ref[...], jnp.concatenate([high, low, high], axis=0)))
        return jnp.concatenate(blocks, axis=0)

    corr = finish(0) * (total * groups) ** (-0.5)
    for ch in range(per):
        block = corr[ch * parts : (ch + 1) * parts]
        fstage[pl.ds(2 * ch, parts, stride=2 * per), :] = block[:, :half]
        fstage[pl.ds(2 * ch + 1, parts, stride=2 * per), :] = block[:, half:]
    for s in range(parts):
        fsend[s] = fstage[2 * per * s : 2 * per * (s + 1), :]
    slot = group * share + me % share

    def push_filter(peer):
        return push(fsend.at[peer], frecv.at[slot], 4, peer, target)

    each_partner(me, parts, lambda peer: push_filter(peer).start())

    @pl.when(target != group)
    def _():
        push_filter(me).start()

    @pl.when(target == group)
    def _():
        pltpu.make_async_copy(fsend.at[me], frecv.at[slot], sems.at[5]).start()

    conv_out = finish(1) + direct * product
    dz = finish(2) + direct * dw
    grads = [grad * conv_out, dz * value, dz * key_part]
    for b in range(3):
        result = weight[b][0] * grads[b]
        for j in range(1, taps):
            result = result + weight[b][j] * advanced(grads[b], j)
        for ch in range(per):
            block = result[ch * parts : (ch + 1) * parts]
            for h in (0, 1):
                start = (2 * b + h) * channels + ch
                stage[pl.ds(start, parts, stride=per), :] = block[:, h * half : (h + 1) * half]
            if ch == per - 1:
                for n in (2 * b, 2 * b + 1):
                    for s in range(parts):
                        start = n * channels + s * per
                        gsend[s, n] = stage[start : start + per, :]

    scale = total ** (-0.5)
    sums = [grads[b] * moved[b][j] for b in range(3) for j in range(taps)] + [dw * product]
    spot = lax.broadcasted_iota(jnp.int32, (1, half), 1)
    line = jnp.zeros((1, half), jnp.float32)
    for k, array in enumerate(sums):
        folded = array[:, :half] + array[:, half:]
        for ch in range(per):
            block = jnp.sum(folded[ch * parts : (ch + 1) * parts], axis=0, keepdims=True)
            amount = jnp.sum(block, axis=1, keepdims=True) * scale
            line = jnp.where(spot == k * per + per * me + ch, amount, line)
    gsend[:, 6] = jnp.broadcast_to(line.reshape(1, 1, half), (parts, per, half))
    pltpu.make_async_copy(gsend.at[me], grecv.at[me], sems.at[7]).start()
    each_partner(
        me, parts, lambda peer: push(gsend.at[peer], grecv.at[me], 6, peer, group).start()
    )

    wait_blocks(frecv, parts, sems.at[5])
    pltpu.make_async_copy(grecv, grecv, sems.at[7]).wait()
    wait_blocks(send, parts - 1, sems.at[0])
    wait_blocks(fsend, parts - 1, sems.at[4])

    @pl.when(target != group)
    def _():
        wait_blocks(fsend, 1, sems.at[4])

    wait_blocks(gsend, parts - 1, sems.at[6])


def unpack_kernel(
    groups, parts, grecv, frecv, ig_hbm, fg_hbm, skg_hbm, sg_hbm,
    stage, ig_ref, fg_ref, skg_ref, sg_ref, sems,
):
    taps, channels = sg_ref.shape[1:]
    half = grecv.shape[1]
    per = channels // parts
    share = channels // groups

    def save(n, src, dst):
        copy = pltpu.make_async_copy(src, dst, sems.at[n])
        copy.start()
        return copy

    for b in range(3):
        for h in (0, 1):
            n = 2 * b + h
            for ch in range(per):
                stage[pl.ds(n * channels + ch, parts, stride=per), :] = grecv[
                    pl.ds(n * per + ch, parts, stride=7 * per), :
                ]
            ig_ref[b, :, h * half : (h + 1) * half] = stage[n * channels : (n + 1) * channels, :]
    saves = [save(0, ig_ref, ig_hbm)]
    for h in (0, 1):
        both = frecv[pl.ds(h, share, stride=2), :]
        for j in range(1, groups):
            both = both + frecv[pl.ds(2 * share * j + h, share, stride=2), :]
        fg_ref[:, h * half : (h + 1) * half] = both
    saves.append(save(1, fg_ref, fg_hbm))
    sums = grecv[pl.ds(6 * per, parts, stride=7 * per), :]
    row = lax.broadcasted_iota(jnp.int32, sums.shape, 0)
    lane = lax.broadcasted_iota(jnp.int32, sums.shape, 1)
    for k in range(3 * taps + 1):
        first = (row + k) * per
        mine = (lane >= first) & (lane < first + per)
        line = jnp.sum(jnp.where(mine, sums, 0.0), axis=0, keepdims=True)
        piece = line[:, k * per : k * per + channels]
        if k < 3 * taps:
            sg_ref[k // taps, pl.ds(k % taps, 1), :] = piece
        else:
            skg_ref[...] = piece
    saves += [save(2, skg_ref, skg_hbm), save(3, sg_ref, sg_hbm)]
    for copy in saves:
        copy.wait()


def owner_body(inputs, short_weights, filters, skip, grad_out):
    parts = lax.axis_size("seq")
    groups = lax.axis_size("chan")
    taps = short_weights.shape[1]
    channels, span = grad_out.shape
    per = channels // parts
    half = span // 2
    wide, twiddle, first, last = (jnp.asarray(t) for t in tables(parts, span))
    vmem = pl.BlockSpec(memory_space=pltpu.VMEM)
    hbm = pl.BlockSpec(memory_space=pltpu.HBM)
    f32 = jnp.float32
    operands = (
        inputs, grad_out, filters, short_weights, skip, wide, twiddle, first, last
    )
    limit = 60 * 1024 * 1024
    landing = (
        jax.ShapeDtypeStruct((parts, 7, per, half), f32),
        jax.ShapeDtypeStruct((parts, 2 * per, half), f32),
    )
    blocks, filter_blocks = pl.pallas_call(
        functools.partial(kernel, parts, groups),
        out_shape=landing,
        in_specs=[hbm] * 9,
        out_specs=(hbm,) * 2,
        scratch_shapes=[
            pltpu.VMEM(inputs.shape, inputs.dtype),
            pltpu.VMEM(grad_out.shape, grad_out.dtype),
            pltpu.VMEM(filters.shape, filters.dtype),
            pltpu.SMEM(short_weights.shape, f32),
            pltpu.SMEM(skip.shape, f32),
            pltpu.VMEM(wide.shape, wide.dtype),
            pltpu.VMEM(twiddle.shape, twiddle.dtype),
            pltpu.VMEM(first.shape, first.dtype),
            pltpu.VMEM(last.shape, last.dtype),
            pltpu.VMEM((8 * channels, half), f32),
            pltpu.VMEM((parts, per + per // 2, 8, half), jnp.bfloat16),
            pltpu.VMEM((parts, per + per // 2, 8, half), jnp.bfloat16),
            pltpu.VMEM((parts, 7, per, half), f32),
            pltpu.VMEM((parts, 2 * per, half), f32),
            pltpu.VMEM((4 * channels, half), f32),
            pltpu.SemaphoreType.DMA((10,)),
            pltpu.SemaphoreType.DMA((9,)),
        ],
        compiler_params=pltpu.CompilerParams(
            collective_id=0, has_side_effects=True, vmem_limit_bytes=limit
        ),
        name="owner_convolutions",
    )(*operands)
    shapes = (
        jax.ShapeDtypeStruct((3, channels, span), f32),
        jax.ShapeDtypeStruct((channels // groups, span), f32),
        jax.ShapeDtypeStruct((1, channels), f32),
        jax.ShapeDtypeStruct((3, taps, channels), f32),
    )
    in_grads, filter_grad, skip_grad, short_grad = pl.pallas_call(
        functools.partial(unpack_kernel, groups, parts),
        out_shape=shapes,
        in_specs=[vmem] * 2,
        out_specs=(hbm,) * 4,
        scratch_shapes=[
            pltpu.VMEM((6 * channels, half), f32),
            *[pltpu.VMEM(s.shape, f32) for s in shapes],
            pltpu.SemaphoreType.DMA((4,)),
        ],
        compiler_params=pltpu.CompilerParams(vmem_limit_bytes=limit),
        name="unpack_results",
    )(
        blocks.reshape(7 * channels, half), filter_blocks.reshape(2 * channels, half)
    )
    return in_grads, filter_grad, skip_grad.reshape(channels), short_grad


def body(inputs, short_weights, filters, skip, grad_out):
    parts = lax.axis_size("seq")
    groups = lax.axis_size("chan")
    channels, span = grad_out.shape
    fits = (
        channels == 2 * parts
        and filters.shape[0] == channels
        and span == 256
        and parts == 16
        and parts % groups == 0
        and short_weights.shape[1] <= 4
    )
    chosen = owner_body if fits else spectral_body
    return chosen(inputs, short_weights, filters, skip, grad_out)


def solution(mesh):
    placed = (
        P(None, "chan", "seq"),
        P(None, None, "chan"),
        P(None, "seq"),
        P("chan"),
        P("chan", "seq"),
    )
    return jax.shard_map(
        body,
        mesh=mesh,
        in_specs=placed,
        out_specs=(P(None, "chan", "seq"), P("chan", "seq"), P("chan"), P(None, None, "chan")),
        check_vma=False,
    )
```
